32 devices in a mesh: dp: 32 (over z, y, x, core).
Axes of the slice: x: 2, y: 2, z: 4, core: 2. Of those that a mesh axis runs over, the one named last changes fastest.
Arguments:
- picture_patch_inputs: bfloat16 [19200, 768], P('dp'), may hold values from -6 to 6
- caption_packed_inputs: bfloat16 [7392, 512], P('dp'), may hold values from -6 to 6
- picture_attend_entry_weight: bfloat16 [1, 768, 2304], P(None, 'dp'), may hold values from -0.21875 to 0.21875
- picture_attend_exit_weight: bfloat16 [1, 768, 768], P(None, 'dp'), may hold values from -0.625 to 0.625
- picture_widening_weight: bfloat16 [1, 768, 3072], P(None, 'dp'), may hold values from -0.21875 to 0.21875
- picture_narrowing_weight: bfloat16 [1, 3072, 768], P(None, 'dp'), may hold values from -0.109375 to 0.109375
- picture_affine_entries: bfloat16 [1, 8, 768], P(None, None, 'dp'), as said below
- picture_widening_offset: bfloat16 [1, 3072], P(None, 'dp'), may hold values from -2.5 to 2.5
- caption_attend_entry_weight: bfloat16 [1, 512, 1536], P(None, 'dp'), may hold values from -0.25 to 0.25
- caption_attend_exit_weight: bfloat16 [1, 512, 512], P(None, 'dp'), may hold values from -0.5 to 0.5
- caption_widening_weight: bfloat16 [1, 512, 2048], P(None, 'dp'), may hold values from -0.25 to 0.25
- caption_narrowing_weight: bfloat16 [1, 2048, 512], P(None, 'dp'), may hold values from -0.125 to 0.125
- caption_affine_entries: bfloat16 [1, 8, 512], P(None, None, 'dp'), as said below
- caption_widening_offset: bfloat16 [1, 2048], P(None, 'dp'), may hold values from -2.5 to 2.5
- picture_feature_mapping: bfloat16 [768, 512], P('dp'), may hold values from -0.21875 to 0.21875
- sharpness_exponent: float32 [], replicated, may hold values from 3.4 to 3.9
- caption_token_counts: int32 [96, 4], P('dp'), may hold values from 1 to 32, 77 in all within a row
- matching_picture_index: int32 [384], P('dp'), may hold values from 0 to 383, each once
Outputs:
- loss: float32 [], replicated
- d_logit_scale: float32 [], replicated
- d_x_img: float32 [19200, 768], P('dp')
- d_x_txt: float32 [7392, 512], P('dp')
- d_img_qkv: float32 [1, 768, 2304], P(None, 'dp')
- d_img_out: float32 [1, 768, 768], P(None, 'dp')
- d_img_fc: float32 [1, 768, 3072], P(None, 'dp')
- d_img_proj: float32 [1, 3072, 768], P(None, 'dp')
- d_img_vec: float32 [1, 8, 768], P(None, None, 'dp')
- d_img_fcb: float32 [1, 3072], P(None, 'dp')
- d_txt_qkv: float32 [1, 512, 1536], P(None, 'dp')
- d_txt_out: float32 [1, 512, 512], P(None, 'dp')
- d_txt_fc: float32 [1, 512, 2048], P(None, 'dp')
- d_txt_proj: float32 [1, 2048, 512], P(None, 'dp')
- d_txt_vec: float32 [1, 8, 512], P(None, None, 'dp')
- d_txt_fcb: float32 [1, 2048], P(None, 'dp')
- d_w_img: float32 [768, 512], P('dp')
The draws below stay inside these ranges and needn't reach their ends.
Inputs may be any that keep to these rules, and one draw needn't show every extreme that they name: `caption_token_counts`: each row's 4 lengths add up to 77, and the longest is 32. `matching_picture_index`: every image is paired with exactly one caption. `picture_affine_entries`: rows 0 and 5 of each layer are gains between 0.7 and 1.3; the other rows are biases. `caption_affine_entries`: as picture_affine_entries.
All inputs are finite; a program needn't handle non-finite values.
Results may differ from the reference program's by a relative error of at most 0.015.
Values may be sent and summed in bfloat16 or wider, within the bound.
A program may use at most 256 MiB of HBM per device.

```python
import math
from functools import partial
import jax
import jax.numpy as jnp
import numpy as np
from jax import lax

D_I = 768
FF_I = 3072
D_T = 512
FF_T = 2048
HD = 64
TOK_I = 50
TOK_T = 77
CAP_ROW = 4
MAX_CAP = 32
LAYERS = 1
IMG_DEV = 12
ROWS_DEV = 3
IMAGES = 384
CAPTIONS = 384
ROWS = 96


def vector_rows(key, feature_width):
    spread = jax.random.uniform(key, (LAYERS, 8, feature_width), jnp.float32, -1.0, 1.0)
    noise = jax.random.normal(jax.random.fold_in(key, 7), (LAYERS, 8, feature_width), jnp.float32)
    row_index = lax.broadcasted_iota(jnp.int32, (LAYERS, 8, feature_width), 1)
    is_gain = (row_index == 0) | (row_index == 5)
    return jnp.where(is_gain, 1.0 + 0.3 * spread, 0.3 * jnp.clip(noise, -4.0, 4.0))


def draw_picture_affine_entries(key, part):
    key = jax.random.fold_in(key, 11)
    return vector_rows(key, D_I).astype(jnp.bfloat16)


def draw_caption_affine_entries(key, part):
    key = jax.random.fold_in(key, 12)
    return vector_rows(key, D_T).astype(jnp.bfloat16)


def block_scale(key, dims, cuts, smallest, high):
    level, own = 1.0, jax.random.fold_in(key, 6)
    for dim, blocks in cuts:
        draws = jnp.exp(jax.random.uniform(jax.random.fold_in(own, dim), (blocks,), jnp.float32, smallest / len(cuts), high / len(cuts)))
        level = level * jnp.repeat(draws, dims[dim] // blocks).reshape([-1 if axis == dim else 1 for axis in range(len(dims))])
    return level


def split_up(number_of, total, bound, lean):
    loads = [(1 << 20) // math.isqrt(grade ** lean) + 1 for grade in range(2, number_of + 1)]
    surplus, counts = total - bound - (number_of - 1), [1] * (number_of - 1)
    while surplus > 0:
        movable = [i for i in range(number_of - 1) if counts[i] < bound]
        whole, remaining = sum([loads[i] for i in movable]), surplus
        for i in movable:
            more = min(bound - counts[i], max(1, remaining * loads[i] // whole), surplus)
            counts[i] = counts[i] + more
            surplus = surplus - more
    return np.array([bound] + counts)


def ragged_sizes(key, number_of, total, reach, lean):
    if number_of == 2:
        one = jax.random.randint(key, (), max(1, total - reach), min(reach, total - 1) + 1)
        return jnp.stack([one, total - one])
    lengths = jnp.asarray(split_up(number_of, total, reach, lean), jnp.int32)
    couples = (number_of - 1) // 2
    source_of, sink = lengths[1:1 + 2 * couples:2], lengths[2:2 + 2 * couples:2]
    room = jnp.minimum(source_of - 1, reach - sink)
    passed = jax.random.randint(jax.random.fold_in(key, 1), (couples,), 0, 1 << 20) % (room + 1)
    lengths = lengths.at[1:1 + 2 * couples:2].set(source_of - passed).at[2:2 + 2 * couples:2].set(sink + passed)
    return lengths[jax.random.permutation(jax.random.fold_in(key, 2), number_of)]


def normal_values(stream_key, extent, scale, limit, split=(), kind=jnp.bfloat16):
    gain = block_scale(stream_key, extent, split, -0.22, 0.18) if split else 1.0
    entries = jax.random.normal(stream_key, extent, jnp.float32) * scale * gain
    return jnp.minimum(jnp.maximum(entries, -limit), limit).astype(kind)


def setup_inputs(seed: int = 0) -> dict:
    splits = jax.random.split(jax.random.key(seed), 19)
    picture_patch_inputs = normal_values(splits[0], (IMAGES * TOK_I, D_I), 1.0, 6.0, ((0, 32),))
    caption_packed_inputs = normal_values(splits[1], (ROWS * TOK_T, D_T), 1.0, 6.0, ((0, 32),))
    picture_attend_entry_weight = normal_values(splits[2], (LAYERS, D_I, 3 * D_I), D_I ** -0.5, 0.21875, ((1, 32),))
    picture_attend_exit_weight = normal_values(splits[3], (LAYERS, D_I, D_I), (D_I // 8) ** -0.5, 0.625, ((1, 32),))
    picture_widening_weight = normal_values(splits[4], (LAYERS, D_I, FF_I), D_I ** -0.5, 0.21875, ((1, 32),))
    picture_narrowing_weight = normal_values(splits[5], (LAYERS, FF_I, D_I), FF_I ** -0.5, 0.109375, ((1, 32),))
    picture_affine_entries = draw_picture_affine_entries(jax.random.fold_in(splits[18], 71), 0)
    picture_widening_offset = normal_values(splits[7], (LAYERS, FF_I), 0.3, 2.5, ((1, 32),))
    caption_attend_entry_weight = normal_values(splits[8], (LAYERS, D_T, 3 * D_T), D_T ** -0.5, 0.25, ((1, 32),))
    caption_attend_exit_weight = normal_values(splits[9], (LAYERS, D_T, D_T), (D_T // 4) ** -0.5, 0.5, ((1, 32),))
    caption_widening_weight = normal_values(splits[10], (LAYERS, D_T, FF_T), D_T ** -0.5, 0.25, ((1, 32),))
    caption_narrowing_weight = normal_values(splits[11], (LAYERS, FF_T, D_T), FF_T ** -0.5, 0.125, ((1, 32),))
    caption_affine_entries = draw_caption_affine_entries(jax.random.fold_in(splits[18], 71), 0)
    caption_widening_offset = normal_values(splits[13], (LAYERS, FF_T), 0.3, 2.5, ((1, 32),))
    picture_feature_mapping = normal_values(splits[14], (D_I, D_T), D_I ** -0.5, 0.21875, ((0, 32),))
    sharpness_exponent = jnp.clip(jax.random.uniform(splits[15], (), jnp.float32, 3.4, 3.9), 3.4, 3.9)
    caption_token_counts = jax.vmap(lambda own: ragged_sizes(own, CAP_ROW, TOK_T, MAX_CAP, 2))(jax.random.split(splits[16], ROWS)).reshape((ROWS, CAP_ROW)).astype(jnp.int32)
    matching_picture_index = jax.random.permutation(splits[17], CAPTIONS).astype(jnp.int32)
    return {"picture_patch_inputs": picture_patch_inputs, "caption_packed_inputs": caption_packed_inputs, "picture_attend_entry_weight": picture_attend_entry_weight, "picture_attend_exit_weight": picture_attend_exit_weight, "picture_widening_weight": picture_widening_weight, "picture_narrowing_weight": picture_narrowing_weight, "picture_affine_entries": picture_affine_entries, "picture_widening_offset": picture_widening_offset, "caption_attend_entry_weight": caption_attend_entry_weight, "caption_attend_exit_weight": caption_attend_exit_weight, "caption_widening_weight": caption_widening_weight, "caption_narrowing_weight": caption_narrowing_weight, "caption_affine_entries": caption_affine_entries, "caption_widening_offset": caption_widening_offset, "picture_feature_mapping": picture_feature_mapping, "sharpness_exponent": sharpness_exponent, "caption_token_counts": caption_token_counts, "matching_picture_index": matching_picture_index}


@jax.custom_vjp
def low(v):
    return lax.optimization_barrier(v.astype(jnp.bfloat16)).astype(jnp.float32)

@jax.custom_vjp
def low_back(v):
    return v

def low_keep(v):
    return (low(v), None)

def low_pass(kept, grad):
    return (grad,)

def back_keep(v):
    return (v, None)

def back_low(kept, grad):
    return (low(grad),)
low.defvjp(low_keep, low_pass)
low_back.defvjp(back_keep, back_low)

def matmul_high(left, right):
    return jnp.matmul(left, right, precision=lax.Precision.HIGHEST)

def layer_norm(hidden, norm_gain, norm_shift):
    row_mean = lax.optimization_barrier(jnp.mean(hidden, -1, keepdims=True))
    centred = hidden - row_mean
    inverse = lax.rsqrt(lax.optimization_barrier(jnp.mean(centred * centred, -1, keepdims=True)) + 1e-05)
    return centred * inverse * norm_gain + norm_shift

def log_total(values, axis_index):
    largest = lax.optimization_barrier(jnp.max(values, axis_index, keepdims=True))
    summed = jnp.log(lax.optimization_barrier(jnp.sum(jnp.exp(values - largest), axis_index, keepdims=True))) + largest
    return jnp.squeeze(summed, axis_index)

def block(hidden, weights, allowed):
    w_qkv, w_out, w_fc, w_proj, vectors, fc_bias = weights
    feature_width = hidden.shape[-1]
    head_shape = (hidden.shape[0], hidden.shape[1], feature_width // HD, HD)
    first = low(layer_norm(hidden, vectors[0], vectors[1]))
    projected = matmul_high(first, w_qkv)
    queries = low_back(low(projected[..., :feature_width] + vectors[2]))
    key_heads = low_back(low(projected[..., feature_width:2 * feature_width]))
    values = low_back(low(projected[..., 2 * feature_width:] + vectors[3]))
    scores = jnp.einsum('sqhd,skhd->shqk', queries.reshape(head_shape), key_heads.reshape(head_shape), precision=lax.Precision.HIGHEST) * 0.125
    scores = low_back(jnp.where(allowed[:, None], scores, -1000000000.0))
    attn_probs = low(jax.nn.softmax(scores, axis=-1))
    context = jnp.einsum('shqk,skhd->sqhd', attn_probs, values.reshape(head_shape), precision=lax.Precision.HIGHEST).reshape(hidden.shape)
    context = low_back(low(context))
    middle = hidden + low_back(matmul_high(context, w_out) + vectors[4])
    second = low(layer_norm(middle, vectors[5], vectors[6]))
    upward = low_back(matmul_high(second, w_fc) + fc_bias)
    activated = low(upward * jax.nn.sigmoid(1.702 * upward))
    return middle + low_back(matmul_high(activated, w_proj) + vectors[7])

def image_group(params, group):
    allowed = jnp.ones((group.shape[0], TOK_I, TOK_I), dtype=jnp.bool_)
    hidden = group
    for layer_index in range(LAYERS):
        hidden = block(hidden, tuple((stacked[layer_index] for stacked in params)), allowed)
    return hidden[:, 0, :]

def text_group(params, pair):
    group, group_lengths = pair
    seg_ends = jnp.cumsum(group_lengths, axis=1).astype(jnp.int32)
    position = jnp.arange(TOK_T, dtype=jnp.int32)
    segment = lax.optimization_barrier(jnp.sum((position[None, :, None] >= seg_ends[:, None, :]).astype(jnp.int32), -1))
    allowed = (segment[:, :, None] == segment[:, None, :]) & (position[None, None, :] <= position[None, :, None])
    pooling = (position[None, None, :] == seg_ends[:, :, None] - 1).astype(group.dtype)
    hidden = group
    for layer_index in range(LAYERS):
        hidden = block(hidden, tuple((stacked[layer_index] for stacked in params)), allowed)
    pooled = jnp.einsum('sct,std->scd', pooling, hidden, precision=lax.Precision.HIGHEST)
    return pooled.reshape(-1, hidden.shape[-1])

def unit_rows(raw):
    return raw * lax.rsqrt(lax.optimization_barrier(jnp.sum(raw * raw, -1, keepdims=True)) + 1e-06)

def full_loss(img_params, txt_params, img_inputs, txt_inputs, projection, sharpness_factor, caption_token_counts, matching_picture_index):
    img_groups = img_inputs.reshape(-1, IMG_DEV * 8, TOK_I, D_I)
    pooled_img = lax.map(jax.checkpoint(partial(image_group, img_params)), img_groups).reshape(-1, D_I)
    raw_img = low_back(matmul_high(low(pooled_img), projection))
    image_embedding_rows = low(unit_rows(raw_img))
    txt_groups = txt_inputs.reshape(-1, ROWS_DEV * 8, TOK_T, D_T)
    length_groups = caption_token_counts.reshape(-1, ROWS_DEV * 8, CAP_ROW)
    raw_txt = lax.map(jax.checkpoint(partial(text_group, txt_params)), (txt_groups, length_groups)).reshape(-1, D_T)
    text_embedding_rows = low(unit_rows(raw_txt))
    logits = jnp.exp(sharpness_factor) * matmul_high(text_embedding_rows, image_embedding_rows.T)
    row_totals = log_total(logits, 1)
    col_totals = log_total(logits, 0)
    target = (matching_picture_index[:, None] == jnp.arange(CAPTIONS, dtype=jnp.int32)[None, :]).astype(logits.dtype)
    return (jnp.sum(row_totals) + jnp.sum(col_totals)) / (2 * CAPTIONS) - jnp.sum(target * logits) / CAPTIONS

def reference(picture_patch_inputs, caption_packed_inputs, picture_attend_entry_weight, picture_attend_exit_weight, picture_widening_weight, picture_narrowing_weight, picture_affine_entries, picture_widening_offset, caption_attend_entry_weight, caption_attend_exit_weight, caption_widening_weight, caption_narrowing_weight, caption_affine_entries, caption_widening_offset, picture_feature_mapping, sharpness_exponent, caption_token_counts, matching_picture_index):
    img_params = tuple((stacked.astype(jnp.float32) for stacked in (picture_attend_entry_weight, picture_attend_exit_weight, picture_widening_weight, picture_narrowing_weight, picture_affine_entries, picture_widening_offset)))
    txt_params = tuple((stacked.astype(jnp.float32) for stacked in (caption_attend_entry_weight, caption_attend_exit_weight, caption_widening_weight, caption_narrowing_weight, caption_affine_entries, caption_widening_offset)))
    img_inputs = picture_patch_inputs.astype(jnp.float32).reshape(IMAGES, TOK_I, D_I)
    txt_inputs = caption_packed_inputs.astype(jnp.float32).reshape(ROWS, TOK_T, D_T)
    projection = picture_feature_mapping.astype(jnp.float32)
    sharpness_factor = sharpness_exponent.astype(jnp.float32)
    loss_fn = partial(full_loss, caption_token_counts=caption_token_counts, matching_picture_index=matching_picture_index)
    loss, pullback = jax.vjp(loss_fn, img_params, txt_params, img_inputs, txt_inputs, projection, sharpness_factor)
    d_img, d_txt, d_img_in, d_txt_in, d_projection, d_scale = pullback(jnp.ones_like(loss))
    return (loss, d_scale, d_img_in.reshape(IMAGES * TOK_I, D_I), d_txt_in.reshape(ROWS * TOK_T, D_T), d_img[0], d_img[1], d_img[2], d_img[3], d_img[4], d_img[5], d_txt[0], d_txt[1], d_txt[2], d_txt[3], d_txt[4], d_txt[5], d_projection)
```

```python
import jax
import jax.numpy as jnp
from jax import lax
from jax.experimental import pallas as pl
from jax.experimental.pallas import tpu as pltpu
from jax.sharding import PartitionSpec as P

HD = 64
TOK_I = 50
TOK_T = 77
CAP_ROW = 4


def norm_forward(hidden, norm_gain, norm_shift):
    row_mean = jnp.mean(hidden, -1, keepdims=True)
    centred = hidden - row_mean
    inverse = lax.rsqrt(jnp.mean(centred * centred, -1, keepdims=True) + 1e-05)
    normed = centred * inverse
    return (normed, inverse, normed * norm_gain + norm_shift)


def norm_backward(upstream, normed, inverse, norm_gain):
    scaled = upstream * norm_gain
    inner_sum = (
        scaled
        - jnp.mean(scaled, -1, keepdims=True)
        - normed * jnp.mean(scaled * normed, -1, keepdims=True)
    )
    return (inverse * inner_sum, jnp.sum(upstream * normed, (0, 1)), jnp.sum(upstream, (0, 1)))


def split_heads(values):
    return values.reshape(values.shape[0], values.shape[1], values.shape[2] // HD, HD)


def attention_scores(queries, key_heads, allowed):
    scores = (
        jnp.einsum("sqhd,skhd->shqk", queries, key_heads, preferred_element_type=jnp.float32)
        * 0.125
    )
    return jnp.where(allowed[:, None], scores, -1000000000.0)


def block_forward(hidden, weights, allowed):
    w_qkv, w_out, w_fc, w_proj, vectors, fc_bias = weights
    vectors = vectors.astype(jnp.float32)
    fc_bias = fc_bias.astype(jnp.float32)
    feature_width = hidden.shape[-1]
    normed_first, inverse_first, first = norm_forward(hidden, vectors[0], vectors[1])
    first_low = first.astype(jnp.bfloat16)
    projected = jnp.einsum("std,de->ste", first_low, w_qkv, preferred_element_type=jnp.float32)
    queries = (projected[..., :feature_width] + vectors[2]).astype(jnp.bfloat16)
    key_heads = projected[..., feature_width : 2 * feature_width].astype(jnp.bfloat16)
    values = (projected[..., 2 * feature_width :] + vectors[3]).astype(jnp.bfloat16)
    scores = attention_scores(split_heads(queries), split_heads(key_heads), allowed)
    totals = jax.nn.logsumexp(scores, -1, keepdims=True)
    attn_probs = jnp.exp(scores - totals).astype(jnp.bfloat16)
    context = jnp.einsum(
        "shqk,skhd->sqhd", attn_probs, split_heads(values), preferred_element_type=jnp.float32
    )
    context = context.reshape(hidden.shape).astype(jnp.bfloat16)
    middle = hidden + (
        jnp.einsum("std,de->ste", context, w_out, preferred_element_type=jnp.float32) + vectors[4]
    )
    normed_second, inverse_second, second = norm_forward(middle, vectors[5], vectors[6])
    second_low = second.astype(jnp.bfloat16)
    upward = (
        jnp.einsum("std,df->stf", second_low, w_fc, preferred_element_type=jnp.float32) + fc_bias
    )
    activated = (upward * jax.nn.sigmoid(1.702 * upward)).astype(jnp.bfloat16)
    output = middle + (
        jnp.einsum("stf,fd->std", activated, w_proj, preferred_element_type=jnp.float32)
        + vectors[7]
    )
    stored = (
        normed_first,
        inverse_first,
        first_low,
        queries,
        key_heads,
        values,
        totals,
        context,
        normed_second,
        inverse_second,
        second_low,
        upward,
        activated,
    )
    return (output, stored)


def block_backward(upstream, weights, stored, allowed):
    w_qkv, w_out, w_fc, w_proj, vectors, fc_bias = weights
    vectors = vectors.astype(jnp.float32)
    (
        normed_first,
        inverse_first,
        first_low,
        queries,
        key_heads,
        values,
        totals,
        context,
        normed_second,
        inverse_second,
        second_low,
        upward,
        activated,
    ) = stored
    feature_width = queries.shape[-1]
    branch = upstream.astype(jnp.bfloat16)
    d_proj_bias = jnp.sum(branch.astype(jnp.float32), (0, 1))
    d_w_proj = jnp.einsum("stf,std->fd", activated, branch, preferred_element_type=jnp.float32)
    d_activated = jnp.einsum("std,fd->stf", branch, w_proj, preferred_element_type=jnp.float32)
    sigmoid_up = jax.nn.sigmoid(1.702 * upward)
    d_upward = (
        d_activated * (sigmoid_up + 1.702 * upward * sigmoid_up * (1.0 - sigmoid_up))
    ).astype(jnp.bfloat16)
    d_fc_bias = jnp.sum(d_upward.astype(jnp.float32), (0, 1))
    d_w_fc = jnp.einsum("std,stf->df", second_low, d_upward, preferred_element_type=jnp.float32)
    d_second = jnp.einsum("stf,df->std", d_upward, w_fc, preferred_element_type=jnp.float32)
    d_middle_norm, d_gain_second, d_shift_second = norm_backward(
        d_second, normed_second, inverse_second, vectors[5]
    )
    d_middle = upstream + d_middle_norm
    attn_branch = d_middle.astype(jnp.bfloat16)
    d_out_bias = jnp.sum(attn_branch.astype(jnp.float32), (0, 1))
    d_w_out = jnp.einsum("std,ste->de", context, attn_branch, preferred_element_type=jnp.float32)
    d_context = jnp.einsum("ste,de->std", attn_branch, w_out, preferred_element_type=jnp.float32)
    d_context = split_heads(d_context.astype(jnp.bfloat16))
    query_heads = split_heads(queries)
    key_split = split_heads(key_heads)
    scores = attention_scores(query_heads, key_split, allowed)
    attn_probs = jnp.exp(scores - totals)
    d_probs = jnp.einsum(
        "sqhd,skhd->shqk", d_context, split_heads(values), preferred_element_type=jnp.float32
    )
    d_scores = (attn_probs * (d_probs - jnp.sum(attn_probs * d_probs, -1, keepdims=True))).astype(
        jnp.bfloat16
    )
    d_queries = (
        jnp.einsum("shqk,skhd->sqhd", d_scores, key_split, preferred_element_type=jnp.float32)
        * 0.125
    ).astype(jnp.bfloat16)
    d_keys = (
        jnp.einsum("shqk,sqhd->skhd", d_scores, query_heads, preferred_element_type=jnp.float32)
        * 0.125
    ).astype(jnp.bfloat16)
    d_values = jnp.einsum(
        "shqk,sqhd->skhd",
        attn_probs.astype(jnp.bfloat16),
        d_context,
        preferred_element_type=jnp.float32,
    ).astype(jnp.bfloat16)
    flat_shape = (queries.shape[0], queries.shape[1], feature_width)
    d_queries = d_queries.reshape(flat_shape)
    d_keys = d_keys.reshape(flat_shape)
    d_values = d_values.reshape(flat_shape)
    d_mixed = jnp.concatenate([d_queries, d_keys, d_values], -1)
    d_w_qkv = jnp.einsum("std,ste->de", first_low, d_mixed, preferred_element_type=jnp.float32)
    d_first = jnp.einsum("ste,de->std", d_mixed, w_qkv, preferred_element_type=jnp.float32)
    d_input_norm, d_gain_first, d_shift_first = norm_backward(
        d_first, normed_first, inverse_first, vectors[0]
    )
    d_hidden = d_middle + d_input_norm
    d_vectors = jnp.stack(
        [
            d_gain_first,
            d_shift_first,
            jnp.sum(d_queries.astype(jnp.float32), (0, 1)),
            jnp.sum(d_values.astype(jnp.float32), (0, 1)),
            d_out_bias,
            d_gain_second,
            d_shift_second,
            d_proj_bias,
        ]
    )
    return (d_hidden, (d_w_qkv, d_w_out, d_w_fc, d_w_proj, d_vectors, d_fc_bias))


def gather_first(img_stack, txt_stack, picture_feature_mapping):
    return (
        lax.all_gather(img_stack[0], "dp", axis=1, tiled=True),
        lax.all_gather(img_stack[1], "dp", axis=1, tiled=True),
        lax.all_gather(img_stack[2], "dp", axis=1, tiled=True),
        lax.all_gather(img_stack[3], "dp", axis=1, tiled=True),
        lax.all_gather(img_stack[4], "dp", axis=2, tiled=True),
        lax.all_gather(img_stack[5], "dp", axis=1, tiled=True),
        lax.all_gather(txt_stack[0], "dp", axis=1, tiled=True),
        lax.all_gather(txt_stack[1], "dp", axis=1, tiled=True),
        lax.all_gather(txt_stack[2], "dp", axis=1, tiled=True),
        lax.all_gather(txt_stack[3], "dp", axis=1, tiled=True),
        lax.all_gather(txt_stack[4], "dp", axis=2, tiled=True),
        lax.all_gather(txt_stack[5], "dp", axis=1, tiled=True),
        lax.all_gather(picture_feature_mapping, "dp", axis=0, tiled=True),
    )


def layer_of(stacks, layer_index):
    return tuple((stacked[layer_index] for stacked in stacks))


def local_plain(
    picture_patch_inputs,
    caption_packed_inputs,
    picture_attend_entry_weight,
    picture_attend_exit_weight,
    picture_widening_weight,
    picture_narrowing_weight,
    picture_affine_entries,
    picture_widening_offset,
    caption_attend_entry_weight,
    caption_attend_exit_weight,
    caption_widening_weight,
    caption_narrowing_weight,
    caption_affine_entries,
    caption_widening_offset,
    picture_feature_mapping,
    sharpness_exponent,
    caption_token_counts,
    matching_picture_index,
):
    img_stack = (
        picture_attend_entry_weight,
        picture_attend_exit_weight,
        picture_widening_weight,
        picture_narrowing_weight,
        picture_affine_entries,
        picture_widening_offset,
    )
    txt_stack = (
        caption_attend_entry_weight,
        caption_attend_exit_weight,
        caption_widening_weight,
        caption_narrowing_weight,
        caption_affine_entries,
        caption_widening_offset,
    )
    images = picture_patch_inputs.shape[0] // TOK_I
    row_count = caption_packed_inputs.shape[0] // TOK_T
    img_hidden = picture_patch_inputs.astype(jnp.float32).reshape(images, TOK_I, -1)
    txt_hidden = caption_packed_inputs.astype(jnp.float32).reshape(row_count, TOK_T, -1)
    img_allowed = jnp.ones((images, TOK_I, TOK_I), dtype=jnp.bool_)
    seg_ends = jnp.cumsum(caption_token_counts, axis=1)
    position = jnp.arange(TOK_T, dtype=jnp.int32)
    segment = jnp.sum((position[None, :, None] >= seg_ends[:, None, :]).astype(jnp.int32), -1)
    txt_allowed = (segment[:, :, None] == segment[:, None, :]) & (
        position[None, None, :] <= position[None, :, None]
    )
    pooling = (position[None, None, :] == seg_ends[:, :, None] - 1).astype(jnp.float32)
    gathered = gather_first(img_stack, txt_stack, picture_feature_mapping)
    img_full = gathered[0:6]
    txt_full = gathered[6:12]
    projection = gathered[12]
    img_stored, txt_stored = ([], [])
    layer_index = 0
    img_hidden, stored = block_forward(img_hidden, layer_of(img_full, layer_index), img_allowed)
    img_stored.append(stored)
    layer_index = 0
    txt_hidden, stored = block_forward(txt_hidden, layer_of(txt_full, layer_index), txt_allowed)
    txt_stored.append(stored)
    pooled_img = img_hidden[:, 0, :].astype(jnp.bfloat16)
    raw_img = jnp.dot(pooled_img, projection, preferred_element_type=jnp.float32)
    scale_img = lax.rsqrt(jnp.sum(raw_img * raw_img, -1, keepdims=True) + 1e-06)
    unit_img = raw_img * scale_img
    raw_txt = jnp.einsum("sct,std->scd", pooling, txt_hidden, precision=lax.Precision.HIGHEST)
    raw_txt = raw_txt.reshape(-1, raw_txt.shape[-1])
    scale_txt = lax.rsqrt(jnp.sum(raw_txt * raw_txt, -1, keepdims=True) + 1e-06)
    unit_txt = raw_txt * scale_txt
    image_embedding_rows = unit_img.astype(jnp.bfloat16)
    text_embedding_rows = unit_txt.astype(jnp.bfloat16)
    all_img, all_txt = (
        lax.all_gather(image_embedding_rows, "dp", axis=0, tiled=True),
        lax.all_gather(text_embedding_rows, "dp", axis=0, tiled=True),
    )
    batch_total = all_img.shape[0]
    affinity_sharpness = jnp.exp(sharpness_exponent)
    picture_wise_affinity_table = affinity_sharpness * jnp.einsum(
        "ce,ie->ci", text_embedding_rows, all_img, preferred_element_type=jnp.float32
    )
    caption_wise_affinity_table = affinity_sharpness * jnp.einsum(
        "ce,ie->ci", all_txt, image_embedding_rows, preferred_element_type=jnp.float32
    )
    lse_rows = jax.nn.logsumexp(picture_wise_affinity_table, 1)
    lse_cols = jax.nn.logsumexp(caption_wise_affinity_table, 0)
    columns = jnp.arange(batch_total, dtype=jnp.int32)
    target_rows = (matching_picture_index[:, None] == columns[None, :]).astype(jnp.float32)
    loss_part = (jnp.sum(lse_rows) + jnp.sum(lse_cols)) / (2 * batch_total) - jnp.sum(
        target_rows * picture_wise_affinity_table
    ) / batch_total
    probs_rows = jnp.exp(picture_wise_affinity_table - lse_rows[:, None])
    probs_cols = jnp.exp(caption_wise_affinity_table - lse_cols[None, :])
    gathered_image_matrix = all_img.astype(jnp.float32)
    gathered_text_matrix = all_txt.astype(jnp.float32)
    highest_precision = lax.Precision.HIGHEST
    row_gradient = probs_rows / (2 * batch_total) - target_rows / batch_total
    column_gradient = probs_cols / (2 * batch_total)
    caption_normalized_adjoint = affinity_sharpness * jnp.dot(
        row_gradient, gathered_image_matrix, precision=highest_precision
    )
    picture_normalized_adjoint = affinity_sharpness * jnp.dot(
        column_gradient.T, gathered_text_matrix, precision=highest_precision
    )
    picture_distributed_adjoint = affinity_sharpness * jnp.dot(
        row_gradient.T, text_embedding_rows.astype(jnp.float32), precision=highest_precision
    )
    caption_distributed_adjoint = affinity_sharpness * jnp.dot(
        column_gradient, image_embedding_rows.astype(jnp.float32), precision=highest_precision
    )
    back_img, back_txt = (
        lax.psum_scatter(picture_distributed_adjoint, "dp", scatter_dimension=0, tiled=True),
        lax.psum_scatter(caption_distributed_adjoint, "dp", scatter_dimension=0, tiled=True),
    )
    picture_normalized_adjoint = picture_normalized_adjoint + back_img
    caption_normalized_adjoint = caption_normalized_adjoint + back_txt
    scale_part = jnp.sum(row_gradient * picture_wise_affinity_table) + jnp.sum(
        column_gradient * caption_wise_affinity_table
    )
    loss, d_scale = lax.psum((loss_part, scale_part), "dp")
    img_back = gathered[0:6]
    txt_back = gathered[6:12]
    back_projection = gathered[12]
    d_raw_img = scale_img * (
        picture_normalized_adjoint
        - unit_img * jnp.sum(picture_normalized_adjoint * unit_img, -1, keepdims=True)
    )
    d_raw_low = d_raw_img.astype(jnp.bfloat16)
    d_projection = jnp.dot(pooled_img.T, d_raw_low, preferred_element_type=jnp.float32)
    d_pooled = jnp.dot(d_raw_low, back_projection.T, preferred_element_type=jnp.float32)
    d_img_hidden = jnp.concatenate(
        [d_pooled[:, None, :], jnp.zeros((images, TOK_I - 1, d_pooled.shape[-1]), jnp.float32)], 1
    )
    d_raw_txt = scale_txt * (
        caption_normalized_adjoint
        - unit_txt * jnp.sum(caption_normalized_adjoint * unit_txt, -1, keepdims=True)
    )
    d_txt_hidden = jnp.einsum(
        "sct,scd->std",
        pooling,
        d_raw_txt.reshape(row_count, CAP_ROW, -1),
        precision=highest_precision,
    )
    img_layer_grads, txt_layer_grads = ([], [])
    layer_index = 0
    d_img_hidden, layer_grads = block_backward(
        d_img_hidden, layer_of(img_back, layer_index), img_stored[layer_index], img_allowed
    )
    img_layer_grads.append(layer_grads)
    img_layer_grads = img_layer_grads[::-1]
    img_local = tuple(
        (jnp.stack([grads[member] for grads in img_layer_grads]) for member in range(6))
    )
    layer_index = 0
    d_txt_hidden, layer_grads = block_backward(
        d_txt_hidden, layer_of(txt_back, layer_index), txt_stored[layer_index], txt_allowed
    )
    txt_layer_grads.append(layer_grads)
    txt_layer_grads = txt_layer_grads[::-1]
    txt_local = tuple(
        (jnp.stack([grads[member] for grads in txt_layer_grads]) for member in range(6))
    )
    summed = (
        lax.psum_scatter(img_local[0], "dp", scatter_dimension=1, tiled=True),
        lax.psum_scatter(img_local[1], "dp", scatter_dimension=1, tiled=True),
        lax.psum_scatter(img_local[2], "dp", scatter_dimension=1, tiled=True),
        lax.psum_scatter(img_local[3], "dp", scatter_dimension=1, tiled=True),
        lax.psum_scatter(img_local[4], "dp", scatter_dimension=2, tiled=True),
        lax.psum_scatter(img_local[5], "dp", scatter_dimension=1, tiled=True),
        lax.psum_scatter(txt_local[0], "dp", scatter_dimension=1, tiled=True),
        lax.psum_scatter(txt_local[1], "dp", scatter_dimension=1, tiled=True),
        lax.psum_scatter(txt_local[2], "dp", scatter_dimension=1, tiled=True),
        lax.psum_scatter(txt_local[3], "dp", scatter_dimension=1, tiled=True),
        lax.psum_scatter(txt_local[4], "dp", scatter_dimension=2, tiled=True),
        lax.psum_scatter(txt_local[5], "dp", scatter_dimension=1, tiled=True),
        lax.psum_scatter(d_projection, "dp", scatter_dimension=0, tiled=True),
    )
    return (
        loss,
        d_scale,
        d_img_hidden.reshape(images * TOK_I, -1),
        d_txt_hidden.reshape(row_count * TOK_T, -1),
        summed[0],
        summed[1],
        summed[2],
        summed[3],
        summed[4],
        summed[5],
        summed[6],
        summed[7],
        summed[8],
        summed[9],
        summed[10],
        summed[11],
        summed[12],
    )


F32 = jnp.float32
BF16 = jnp.bfloat16
Z_PEERS = (8, 16, 24)
PLANE_PEERS = (2, 4, 6)
LINE_PEERS = (1, 8, 9, 16, 17, 24, 25)
ALL_PEERS = (1, 2, 4, 6, 8, 9, 16, 17, 24, 25)
PAD = 16
N_SEMS = 300


def fits(mesh):
    return mesh.size == 32


def dot(left, right):
    return lax.dot_general(left, right, (((1,), (0,)), ((), ())), preferred_element_type=F32)


def dot_nt(left, right):
    return lax.dot_general(left, right, (((1,), (1,)), ((), ())), preferred_element_type=F32)


def dot_tn(left, right):
    return lax.dot_general(left, right, (((0,), (0,)), ((), ())), preferred_element_type=F32)


def split_two(values):
    high = values.astype(BF16)
    return high, (values - high.astype(F32)).astype(BF16)


def iota(shape, dim):
    return lax.broadcasted_iota(jnp.int32, shape, dim)


def expand_heads(rows):
    lanes = iota(rows.shape, 1) // HD
    heads = rows.shape[1] // HD
    zero = jnp.zeros_like(rows)
    return jnp.concatenate([jnp.where(lanes == head, rows, zero) for head in range(heads)], 0)


def join_heads(stacked):
    heads = stacked.shape[1] // HD
    lanes = iota((PAD, stacked.shape[1]), 1) // HD
    total = jnp.zeros((PAD, stacked.shape[1]), F32)
    for head in range(heads):
        total = jnp.where(lanes == head, stacked[PAD * head : PAD * (head + 1)], total)
    return total


def small_norm(hidden, gain, shift):
    centred = hidden - jnp.mean(hidden, -1, keepdims=True)
    inverse = lax.rsqrt(jnp.mean(centred * centred, -1, keepdims=True) + 1e-05)
    normed = centred * inverse
    return normed, inverse, normed * gain + shift


def col_sum(values):
    return jnp.sum(values, 0, keepdims=True)


class Tower:
    def __init__(self, width, tokens, rows, block, real_tokens, extra):
        self.width = width
        self.tokens = tokens
        self.real_tokens = real_tokens
        self.rows = rows
        self.chip_rows = 2 * rows
        self.block = block
        self.group = 4 * block
        self.heads = width // HD
        self.queries = PAD * self.heads
        self.extra = extra
        self.packed = 2 * width + extra + 4 * self.group
        self.row_pad = -(-rows // 16) * 16

    def scratch(self):
        d, n, r, g, b, cr = self.width, self.tokens, self.queries, self.group, self.block, self.chip_rows
        v = pltpu.VMEM
        out = dict(
            pk=v((2, self.row_pad, self.packed), BF16),
            pr=v((self.row_pad, self.packed), BF16),
            w1=v((2, 16 * cr, d), BF16),
            w2=v((2, 16 * cr, d), BF16),
            mf=v((4, cr, g), BF16),
            fa=v((4, 4, cr, g), BF16),
            wp=v((4, b, d), BF16),
            vecs=v((8, d), F32),
            bias=v((8, g), F32),
            xh=v((n, d), F32),
            inv=v((n, 128), F32),
            a=v((n, d), BF16),
            p32=v((r, n), F32),
            lh=v((2 * r + 2 * PAD, n), BF16),
            rh=v((2 * r + 2 * PAD, d), BF16),
            q=v((PAD, d), BF16),
            ci=v((2, 4, PAD, d), BF16),
            hpf=v((2, 4, PAD, d), F32),
            hps=v((2, 4, PAD, d), BF16),
            hr=v((7, PAD, d), BF16),
            dcs=v((2, 4, PAD, d), BF16),
            dcr=v((7, PAD, d), BF16),
            u=v((8 * PAD, g), F32),
            m=v((8 * PAD, g), BF16),
            gpf=v((4, b, d), F32),
            gpb=v((4, b, d), BF16),
            gpr=v((3, b, d), BF16),
            gff=v((4, 4, cr, g), F32),
            gfb=v((4, 4, cr, g), BF16),
            gfr=v((3, 4, cr, g), BF16),
            gf2=v((4, cr, g), BF16),
            gf3=v((4, cr, g), F32),
            gf3r=v((4, cr, g), BF16),
            gf4=v((4, self.rows, g), F32),
            in1t=v((d, 256), BF16),
            in1r=v((4, 4 * cr, 256), BF16),
            in2t=v((d, r), BF16),
            in2r=v((4, 4 * cr, r), BF16),
            qg=v((4, PAD, d), BF16),
            wg=v((4, PAD, d), BF16),
            dog=v((4, PAD, d), BF16),
            dqg=v((4, PAD, d), BF16),
            r1f=v((4, cr, 2 * d + 2 * self.extra), F32),
            r1b=v((4, cr, 2 * d + 2 * self.extra), BF16),
            r1r=v((3, cr, 2 * d + 2 * self.extra), BF16),
            r1s=v((cr, 2 * d + 2 * self.extra), F32),
            r1p=v((self.rows, 2 * d + 2 * self.extra), F32),
            r2f=v((4, cr, 2 * d), F32),
            r2b=v((4, cr, 2 * d), BF16),
            r2r=v((3, cr, 2 * d), BF16),
            r2s=v((cr, 2 * d), F32),
            r2p=v((self.rows, 2 * d), F32),
            da=v((n, d), F32),
            gp=v((n, d), F32),
            g2=v((2, 4, PAD, d), F32),
            dbs=v((8, g), F32),
            dbr=v((3, 8, g), F32),
        )
        return out


SHARED = dict(
    vb=((2, 16, PAD, 128), BF16),
    w3=((2, 768, 256), BF16),
    eb=((2, 2, 16, PAD, 512), BF16),
    sc=((2, 4, 2, PAD, 128), F32),
    gtxt=((512, 512), F32),
    gimg=((512, 512), F32),
    drb=((2, 4, PAD, 512), BF16),
    vz=((8, 1280), F32),
    vzr=((3, 8, 1280), F32),
    vp=((8, 1280), F32),
    vpr=((3, 8, 1280), F32),
    vc=((8, 1280), F32),
    vcr=((8, 1280), F32),
)
INPUTS = (
    "ix", "tx", "iqkv", "iout", "ifc", "iproj", "ivec", "ifcb", "tqkv", "tout", "tfc", "tproj", "tvec", "tfcb",
    "map", "sharp", "counts", "match",
)
OUTPUTS = (
    "loss", "dls", "dxi", "dxt", "diqkv", "diout", "difc", "diproj", "divec", "difcb", "dtqkv", "dtout", "dtfc",
    "dtproj", "dtvec", "dtfcb", "dmap",
)


class Step:
    def __init__(self, ti, tt, images, names, refs):
        self.ref = dict(zip(names, refs, strict=True))
        self.ti, self.tt, self.images = ti, tt, images
        me = lax.axis_index("dp")
        self.bits = [lax.rem(me // (1 << bit), 2) for bit in range(5)]
        self.me = me
        self.core = lax.rem(me, 2)
        self.chip = me // 2
        self.plane = lax.rem(me // 2, 4)
        self.zed = me // 8
        self.used = 0
        self.copies = []

    def at_peer(self, mask):
        total = 0
        for bit in range(5):
            value = 1 - self.bits[bit] if mask >> bit & 1 else self.bits[bit]
            total = total + value * (1 << bit)
        return total

    def send(self, src, dst, mask):
        index = self.used
        self.used += 1
        copy = pltpu.make_async_remote_copy(
            src_ref=src,
            dst_ref=dst,
            send_sem=self.ref["ssem"].at[index],
            recv_sem=self.ref["rsem"].at[index],
            device_id=(self.at_peer(mask),),
            device_id_type=pl.DeviceIdType.MESH,
        )
        copy.start()
        self.copies.append(copy)
        return copy

    def barrier(self):
        semaphore = pltpu.get_barrier_semaphore()
        for mask in ALL_PEERS:
            pl.semaphore_signal(
                semaphore, inc=1, device_id=(self.at_peer(mask),), device_id_type=pl.DeviceIdType.MESH
            )
        pl.semaphore_wait(semaphore, len(ALL_PEERS))

    def gather_begin(self, slot, whole):
        here = slot(self.chip)
        to_z = [self.send(here, here, mask) for mask in Z_PEERS]
        arriving = [self.send(here, here, mask) for mask in PLANE_PEERS]
        return dict(slot=slot, whole=whole, to_z=to_z, arriving=arriving)

    def gather_middle(self, state):
        for copy, mask in zip(state["to_z"], Z_PEERS, strict=True):
            copy.wait_recv()
            there = state["slot"](self.at_peer(mask) // 2)
            state["arriving"] += [self.send(there, there, peer) for peer in PLANE_PEERS]

    def gather_end(self, state):
        for copy in state["arriving"]:
            copy.wait_recv()
        state["last"] = self.send(state["whole"], state["whole"], 1)

    def gather_done(self, state):
        state["last"].wait_recv()

    def line_gather(self, buffer):
        here = buffer.at[self.core, self.zed]
        return [self.send(here, here, mask) for mask in LINE_PEERS]

    def line_scatter(self, parts, landing):
        copies = []
        for slot, mask in enumerate(LINE_PEERS):
            peer = self.at_peer(mask)
            copies.append(self.send(parts.at[lax.rem(peer, 2), peer // 8], landing.at[slot], mask))
        return copies

    def wait(self, copies):
        for copy in copies:
            copy.wait_recv()

    def run(self):
        ti, tt = self.ti, self.tt
        self.pack(ti, "i", map_ref=self.ref["map"])
        self.pack(tt, "t")
        self.pack_vectors()
        self.barrier()
        self.pair = {
            t: self.send(self.ref[t + "pk"].at[1 - self.core], self.ref[t + "pr"], 1) for t in ("i", "t")
        }
        vb = self.ref["vb"]
        vectors = self.gather_begin(lambda chip: vb.at[self.core, chip], vb.at[self.core])
        self.standardize(tt, "t", 0, tt.tokens)
        chunk = {}
        self.merge(ti, "i")
        self.merge(tt, "t")
        chunk["i1"] = self.begin_chunk(ti, "i", "w1")
        chunk["t1"] = self.begin_chunk(tt, "t", "w1")
        chunk["i2"] = self.begin_chunk(ti, "i", "w2")
        chunk["t2"] = self.begin_chunk(tt, "t", "w2")
        w3 = self.ref["w3"]
        chunk["map"] = self.gather_begin(
            lambda chip: w3.at[self.core, pl.ds(pl.multiple_of(chip * ti.chip_rows, 16), ti.chip_rows)],
            w3.at[self.core],
        )
        widen = {t: self.widen_begin(tower, t) for t, tower in (("i", ti), ("t", tt))}
        self.standardize(ti, "i", 0, ti.tokens)
        self.gather_middle(vectors)
        for name in ("i1", "t1", "i2", "t2", "map"):
            self.gather_middle(chunk[name])
        self.gather_end(vectors)
        self.gather_done(vectors)
        self.unpack_vectors()
        self.queries(ti, "i")
        self.queries(tt, "t")
        self.gather_end(chunk["i1"])
        self.gather_end(chunk["t1"])
        for t, tower in (("i", ti), ("t", tt)):
            self.widen_middle(tower, t, widen[t])
        self.gather_done(chunk["i1"])
        self.attend(ti, "i")
        self.gather_end(chunk["i2"])
        self.gather_done(chunk["t1"])
        self.attend(tt, "t")
        self.gather_end(chunk["t2"])
        self.gather_done(chunk["i2"])
        line = {}
        line["i"] = self.mix(ti, "i")
        self.gather_done(chunk["t2"])
        line["t"] = self.mix(tt, "t")
        self.gather_end(chunk["map"])
        scattered = {}
        for t, tower in (("i", ti), ("t", tt)):
            self.wait(widen[t])
            self.wait(line[t])
            scattered[t] = self.feed(tower, t)
        self.gather_done(chunk["map"])
        for t, tower in (("i", ti), ("t", tt)):
            self.wait(scattered[t])
            self.embed(tower, t)
        eb, sc = self.ref["eb"], self.ref["sc"]
        rows = self.gather_begin(lambda chip: eb.at[:, self.core, chip], eb.at[:, self.core])
        scales = self.line_gather(sc)
        early = {t: self.early_operands(tower, t) for t, tower in (("i", ti), ("t", tt))}
        self.gather_middle(rows)
        self.gather_end(rows)
        self.gather_done(rows)
        self.wait(scales)
        self.contrast()
        scattered = {t: self.feed_back(tower, t) for t, tower in (("i", ti), ("t", tt))}
        sent = {t: self.feed_weights(tower, t) for t, tower in (("i", ti), ("t", tt))}
        middle = {}
        for t, tower in (("i", ti), ("t", tt)):
            self.wait(scattered[t])
            middle[t] = self.attend_back(tower, t)
        late = {t: self.attend_back_end(tower, t) for t, tower in (("i", ti), ("t", tt))}
        for t, tower in (("i", ti), ("t", tt)):
            self.input_gradient(tower, t)
        first = self.vector_sum_begin()
        for t, tower in (("i", ti), ("t", tt)):
            self.feed_weights_middle(tower, t, sent[t])
        for t, tower in (("i", ti), ("t", tt)):
            self.round_one(tower, t, early[t], middle[t])
        second = self.vector_sum_middle(first)
        for t, tower in (("i", ti), ("t", tt)):
            self.round_two(tower, t, late[t])
        third = self.vector_sum_end(second)
        for t, tower in (("i", ti), ("t", tt)):
            self.feed_weights_end(tower, t, sent[t])
            self.rounds_end(tower, t)
        self.vector_sum_done(third)
        for t, tower in (("i", ti), ("t", tt)):
            self.rounds_done(tower, t)
        for copy in self.copies:
            copy.wait_send()

    def pack(self, tower, t, map_ref=None):
        pk, qkv, out, fc = (self.ref[t + name] for name in ("pk", "qkv", "out", "fc"))
        d, b = tower.width, tower.block
        pad = tower.row_pad - tower.rows

        def padded(values):
            values = values.astype(F32)
            if pad:
                values = jnp.concatenate([values, jnp.zeros((pad, values.shape[1]), F32)], 0)
            return values.astype(BF16)

        pk[0, :, 0:d] = padded(qkv[:, 0:d])
        pk[1, :, 0:d] = padded(qkv[:, d : 2 * d])
        pk[0, :, d : 2 * d] = padded(qkv[:, 2 * d : 3 * d])
        pk[1, :, d : 2 * d] = padded(out[...])
        if tower.extra:
            for half in range(2):
                cols = slice(half * tower.extra, (half + 1) * tower.extra)
                pk[half, :, 2 * d : 2 * d + tower.extra] = padded(map_ref[:, cols])
        base = 2 * d + tower.extra
        values = padded(fc[...]).astype(F32)
        for half in range(2):
            for zed in range(4):
                pieces = []
                for plane in range(4):
                    device = 8 * zed + 2 * plane + half
                    pieces.append(values[:, b * device : b * (device + 1)])
                start = base + zed * tower.group
                pk[half, :, start : start + tower.group] = jnp.concatenate(pieces, 1).astype(BF16)

    def pack_vectors(self):
        ivec, tvec, ifcb, tfcb, match = (self.ref[n] for n in ("ivec", "tvec", "ifcb", "tfcb", "match"))
        wi, wt = ivec.shape[1], tvec.shape[1]

        def widen(values, at, rows):
            values = values.astype(F32)
            parts = [values, jnp.zeros((values.shape[0], 128 - at - values.shape[1]), F32)]
            if at:
                parts = [jnp.zeros((values.shape[0], at), F32)] + parts
            return jnp.concatenate(parts, 1)

        top = widen(ivec[...], 0, 8) + widen(tvec[...], 32, 8)
        row = iota((8, 128), 0)
        bottom = jnp.where(row == 0, widen(ifcb[...], 0, 1), 0.0)
        bottom = bottom + jnp.where(row == 1, widen(tfcb[...], 0, 1), 0.0)
        block = jnp.concatenate([top, bottom], 0)
        row, lane = iota((PAD, 128), 0), iota((PAD, 128), 1)
        for caption in range(self.images):
            image = match[caption]
            device = image // self.images
            high = lax.rem(device, 2) * 16 + device // 2
            low = image - device * self.images
            block = jnp.where((row == caption) & (lane == 120), high.astype(F32), block)
            block = jnp.where((row == caption) & (lane == 121), low.astype(F32), block)
        self.ref["vb"][self.core, self.chip] = block.astype(BF16)

    def unpack_vectors(self):
        vb = self.ref["vb"]
        for core in range(2):
            for chip in range(16):
                block = vb[core, chip].astype(F32)
                device = 2 * chip + core
                for t, tower, at in (("i", self.ti, 0), ("t", self.tt, 32)):
                    rows = tower.rows
                    self.ref[t + "vecs"][:, rows * device : rows * (device + 1)] = block[0:8, at : at + rows]
        for plane in range(4):
            block = vb[self.core, 4 * self.zed + plane].astype(F32)
            for t, tower, row in (("i", self.ti, 8), ("t", self.tt, 9)):
                b = tower.block
                self.ref[t + "bias"][0:1, b * plane : b * (plane + 1)] = block[row : row + 1, 0:b]

    def standardize(self, tower, t, start, stop):
        x, xh, inv = (self.ref[t + name] for name in ("x", "xh", "inv"))
        step = 32

        def body(index, carry):
            rows = pl.ds(pl.multiple_of(index * step, step), step)
            hidden = x[rows, :].astype(F32)
            centred = hidden - jnp.mean(hidden, -1, keepdims=True)
            inverse = lax.rsqrt(jnp.mean(centred * centred, -1, keepdims=True) + 1e-05)
            xh[rows, :] = centred * inverse
            inv[rows, :] = jnp.broadcast_to(inverse, (step, 128))
            return carry

        lax.fori_loop(start // step, stop // step, body, 0)

    def merge(self, tower, t):
        self.pair[t].wait_recv()
        pk, pr = self.ref[t + "pk"], self.ref[t + "pr"]
        d, g = tower.width, tower.group
        rows = pl.ds(pl.multiple_of(self.chip * tower.chip_rows, 16), tower.chip_rows)
        first = self.core == 0

        def merged(cols):
            own = pk[self.core, :, cols].astype(F32)
            got = pr[:, cols].astype(F32)
            upper = jnp.where(first, own, got)[: tower.rows]
            lower = jnp.where(first, got, own)[: tower.rows]
            return jnp.concatenate([upper, lower], 0).astype(BF16)

        self.ref[t + "w1"][self.core, rows, :] = merged(slice(0, d))
        self.ref[t + "w2"][self.core, rows, :] = merged(slice(d, 2 * d))
        base = 2 * d
        if tower.extra:
            self.ref["w3"][self.core, rows, :] = merged(slice(base, base + tower.extra))
            base += tower.extra
        for zed in range(4):
            self.ref[t + "mf"][zed] = merged(slice(base + zed * g, base + (zed + 1) * g))

    def begin_chunk(self, tower, t, name):
        buffer = self.ref[t + name]
        rows = tower.chip_rows
        return self.gather_begin(
            lambda chip: buffer.at[self.core, pl.ds(pl.multiple_of(chip * rows, 16), rows)],
            buffer.at[self.core],
        )

    def widen_begin(self, tower, t):
        mf, fa = self.ref[t + "mf"], self.ref[t + "fa"]
        copies = []
        for mask in Z_PEERS:
            copies.append(self.send(mf.at[self.at_peer(mask) // 8], fa.at[self.zed, self.plane], mask))
        fa[self.zed, self.plane] = mf[self.zed]
        return copies

    def widen_middle(self, tower, t, copies):
        fa, wp, proj = self.ref[t + "fa"], self.ref[t + "wp"], self.ref[t + "proj"]
        self.wait(copies)
        copies.clear()
        for mask in PLANE_PEERS:
            part = fa.at[:, self.plane]
            copies.append(self.send(part, part, mask))
        for mask in PLANE_PEERS:
            copies.append(self.send(proj, wp.at[self.plane], mask))
        wp[self.plane] = proj[...]

    def queries(self, tower, t):
        a, xh, vec = self.ref[t + "a"], self.ref[t + "xh"], self.ref[t + "vecs"]
        step = 32

        def body(index, carry):
            rows = pl.ds(pl.multiple_of(index * step, step), step)
            a[rows, :] = (xh[rows, :] * vec[0:1, :] + vec[1:2, :]).astype(BF16)
            return carry

        lax.fori_loop(0, tower.tokens // step, body, 0)
        n = tower.tokens
        row, token = iota((PAD, n), 0), iota((PAD, n), 1)
        if t == "i":
            real = row < self.images
            at = jnp.where(real, row * TOK_I, -1)
            low, high = jnp.where(real, row * TOK_I, -1), jnp.where(real, (row + 1) * TOK_I, -1)
        else:
            counts = self.ref["counts"]
            column = iota((PAD, 1), 0)
            low, high = jnp.full((PAD, 1), -1, jnp.int32), jnp.full((PAD, 1), -1, jnp.int32)
            for line in range(counts.shape[0]):
                end = line * TOK_T
                for member in range(CAP_ROW):
                    begin, end = end, end + counts[line, member]
                    chosen = column == line * CAP_ROW + member
                    low, high = jnp.where(chosen, begin, low), jnp.where(chosen, end, high)
            at = jnp.where(high > 0, high - 1, -1)
        chosen = (token == at).astype(F32).astype(BF16)
        lh, r = self.ref[t + "lh"], tower.queries
        lh[2 * r : 2 * r + PAD, :] = chosen
        lh[2 * r + PAD : 2 * r + 2 * PAD, :] = chosen
        seen = ((token >= low) & (token < high)).astype(F32)
        self.ref[t + "seen"] = seen
        self.ref[t + "x0"] = dot(chosen, self.ref[t + "x"][...])
        self.ref[t + "a0"] = dot(chosen, a[...]).astype(BF16)

    def attend(self, tower, t):
        w1, vec, a = self.ref[t + "w1"], self.ref[t + "vecs"], self.ref[t + "a"]
        p32, lh, rh = self.ref[t + "p32"], self.ref[t + "lh"], self.ref[t + "rh"]
        r = tower.queries
        q = (dot(self.ref[t + "a0"], w1[0]) + vec[2:3, :]).astype(BF16)
        self.ref[t + "q"][...] = q
        qt = dot_nt(expand_heads(q), w1[1]).astype(BF16)
        rh[0:r, :] = qt
        scores = dot_nt(qt, a[...]) * 0.125
        seen = jnp.concatenate([self.ref[t + "seen"]] * tower.heads, 0) > 0.5
        scores = jnp.where(seen, scores, -1000000000.0)
        top = jnp.max(scores, -1, keepdims=True)
        raw = jnp.where(seen, jnp.exp(scores - top), 0.0)
        total = jnp.sum(raw, -1, keepdims=True)
        probs = raw / jnp.where(total > 0.0, total, 1.0)
        p32[...] = probs
        low = probs.astype(BF16)
        lh[r : 2 * r, :] = low
        self.ref[t + "pa"] = dot(low, a[...])

    def mix(self, tower, t):
        w2, vec, ci = self.ref[t + "w2"], self.ref[t + "vecs"], self.ref[t + "ci"]
        context = (join_heads(dot(self.ref[t + "pa"].astype(BF16), w2[0])) + vec[3:4, :]).astype(BF16)
        self.ref[t + "o"] = context
        middle = self.ref[t + "x0"] + (dot(context, w2[1]) + vec[4:5, :])
        normed, inverse, second = small_norm(middle, vec[5:6, :], vec[6:7, :])
        self.ref[t + "h1"], self.ref[t + "xh2"], self.ref[t + "inv2"] = middle, normed, inverse
        ci[self.core, self.zed] = second.astype(BF16)
        return self.line_gather(ci)

    def feed(self, tower, t):
        ci, fa, wp, bias = (self.ref[t + name] for name in ("ci", "fa", "wp", "bias"))
        hpf, hps = self.ref[t + "hpf"], self.ref[t + "hps"]
        d, g = tower.width, tower.group
        c = ci[...].reshape(8 * PAD, d)
        up = dot(c, fa[...].reshape(d, g)) + bias[0:1, :]
        active = (up * jax.nn.sigmoid(1.702 * up)).astype(BF16)
        self.ref[t + "u"][...] = up
        self.ref[t + "m"][...] = active
        part = dot(active, wp[...].reshape(g, d)).reshape(2, 4, PAD, d)
        hpf[...] = part
        hps[...] = part.astype(BF16)
        return self.line_scatter(hps, self.ref[t + "hr"])

    def line_total(self, own, landing):
        total = own
        for slot in range(len(LINE_PEERS)):
            total = total + landing[slot].astype(F32)
        return total

    def embed(self, tower, t):
        vec = self.ref[t + "vecs"]
        total = self.line_total(self.ref[t + "hpf"][self.core, self.zed], self.ref[t + "hr"])
        hidden = self.ref[t + "h1"] + (total + vec[7:8, :])
        which = 0 if t == "i" else 1
        if t == "i":
            pooled = hidden.astype(BF16)
            self.ref["pooled"] = pooled
            w3 = self.ref["w3"]
            raw = jnp.concatenate([dot(pooled, w3[0]), dot(pooled, w3[1])], 1)
        else:
            raw = hidden
        scale = lax.rsqrt(jnp.sum(raw * raw, -1, keepdims=True) + 1e-06)
        self.ref["eb"][which, self.core, self.chip] = (raw * scale).astype(BF16)
        self.ref["sc"][self.core, self.zed, which] = jnp.broadcast_to(scale, (PAD, 128))

    def to_z_line(self, block, landing):
        rows = landing.shape[1]
        copies = []
        for mask in Z_PEERS:
            start = pl.multiple_of(self.at_peer(mask) // 8 * rows, 16)
            copies.append(self.send(block.at[pl.ds(start, rows)], landing.at[self.zed], mask))
        landing[self.zed] = block[pl.ds(pl.multiple_of(self.zed * rows, 16), rows), :]
        return copies

    def share_z_line(self, buffer, values):
        buffer[self.zed] = values
        here = buffer.at[self.zed]
        return [self.send(here, here, mask) for mask in Z_PEERS]

    def early_operands(self, tower, t):
        d, r = tower.width, tower.queries
        parts = [self.ref[t + "pa"], self.ref[t + "o"].astype(F32), self.ref[t + "a0"].astype(F32)]
        if t == "i":
            parts.append(self.ref["pooled"].astype(F32))
        rest = 256 - r - PAD * (len(parts) - 1)
        parts.append(jnp.zeros((rest, d), F32))
        self.ref[t + "in1t"][...] = jnp.concatenate(parts, 0).T.astype(BF16)
        copies = self.to_z_line(self.ref[t + "in1t"], self.ref[t + "in1r"])
        return copies + self.share_z_line(self.ref[t + "qg"], self.ref[t + "q"][...])

    def contrast(self):
        eb, vb, sc = self.ref["eb"], self.ref["vb"], self.ref["sc"]
        gtxt, gimg = self.ref["gtxt"], self.ref["gimg"]
        total = self.images * 32
        e_img, e_txt = eb[0].reshape(512, 512), eb[1].reshape(512, 512)
        sharp = jnp.exp(jnp.full((8, 128), self.ref["sharp"][0], F32))[0:1, 0:1]
        logits = sharp * dot_nt(e_txt, e_img)
        marks = vb[...].reshape(512, 128).astype(F32)
        target = marks[:, 120:121] * float(PAD) + marks[:, 121:122]
        row, col = iota((512, 512), 0), iota((512, 512), 1)
        real_row, real_col = lax.rem(row, PAD) < self.images, lax.rem(col, PAD) < self.images
        real = real_row & real_col
        hit = real & (col.astype(F32) == target)
        powers = jnp.where(real, jnp.exp(logits), 0.0)
        row_sum, col_sums = jnp.sum(powers, 1, keepdims=True), col_sum(powers)
        real_line = lax.rem(iota((512, 1), 0), PAD) < self.images
        real_lane = lax.rem(iota((1, 512), 1), PAD) < self.images
        row_sum, col_sums = jnp.where(real_line, row_sum, 1.0), jnp.where(real_lane, col_sums, 1.0)
        grad = powers * ((1.0 / row_sum + 1.0 / col_sums) * (0.5 / total))
        grad = grad - jnp.where(hit, 1.0 / total, 0.0)
        safe = jnp.where(real, logits, 0.0)
        logs = jnp.sum(jnp.log(row_sum), 0, keepdims=True) + jnp.sum(jnp.log(col_sums), 1, keepdims=True)

        def whole(values):
            return jnp.sum(jnp.sum(values, 1, keepdims=True), 0, keepdims=True)

        self.ref["loss"][...] = logs * (0.5 / total) - whole(jnp.where(hit, safe, 0.0)) * (1.0 / total)
        self.ref["dls"][...] = whole(grad * safe)
        gtxt[...] = grad
        gimg[...] = grad.T
        for which, t, rows, others in ((0, "i", gimg, e_txt), (1, "t", gtxt, e_img)):
            parts, own, scales = [], [], []
            for core in range(2):
                for zed in range(4):
                    chip = 4 * zed + self.plane
                    start = pl.multiple_of((core * 16 + chip) * PAD, PAD)
                    parts.append(rows[pl.ds(start, PAD), :])
                    own.append(eb[which, core, chip].astype(F32))
                    scales.append(sc[core, zed, which])
            part, unit = jnp.concatenate(parts, 0), jnp.concatenate(own, 0)
            scale = jnp.concatenate(scales, 0)[:, 0:1]
            high, low = split_two(part)
            d_unit = sharp * (dot(high, others) + dot(low, others))
            d_raw = scale * (d_unit - unit * jnp.sum(d_unit * unit, -1, keepdims=True))
            if t == "i":
                w3 = self.ref["w3"]
                rounded = d_raw.astype(BF16)
                self.ref["drb"][...] = rounded.reshape(2, 4, PAD, 512)
                d_raw = dot_nt(rounded[:, 0:256], w3[0]) + dot_nt(rounded[:, 256:512], w3[1])
            self.ref[t + "g2"][...] = d_raw.reshape(2, 4, PAD, d_raw.shape[1])

    def feed_back(self, tower, t):
        d, g = tower.width, tower.group
        fa, wp, u, dcs, hpf = (self.ref[t + name] for name in ("fa", "wp", "u", "dcs", "hpf"))
        branch = self.ref[t + "g2"][...].reshape(8 * PAD, d).astype(BF16)
        up = u[...]
        gate = jax.nn.sigmoid(1.702 * up)
        d_active = dot_nt(branch, wp[...].reshape(g, d))
        d_up = (d_active * (gate + 1.702 * up * gate * (1.0 - gate))).astype(BF16)
        part = dot_nt(d_up, fa[...].reshape(d, g)).reshape(2, 4, PAD, d)
        hpf[...] = part
        dcs[...] = part.astype(BF16)
        copies = self.line_scatter(dcs, self.ref[t + "dcr"])
        self.ref[t + "du"], self.ref[t + "y"] = d_up, branch
        return copies

    def feed_weights(self, tower, t):
        d, g, b, cr = tower.width, tower.group, tower.block, tower.chip_rows
        m, ci = self.ref[t + "m"], self.ref[t + "ci"]
        gpf, gpb, gpr = (self.ref[t + name] for name in ("gpf", "gpb", "gpr"))
        gff, gfb, gfr = (self.ref[t + name] for name in ("gff", "gfb", "gfr"))
        dbs, dbr = self.ref[t + "dbs"], self.ref[t + "dbr"]
        d_up, branch = self.ref[t + "du"], self.ref[t + "y"]
        grad = dot_tn(ci[...].reshape(8 * PAD, d), d_up).reshape(4, 4, cr, g)
        gff[...] = grad
        gfb[...] = grad.astype(BF16)
        wide = []
        for slot, mask in enumerate(PLANE_PEERS):
            wide.append(self.send(gfb.at[:, lax.rem(self.at_peer(mask) // 2, 4)], gfr.at[slot], mask))
        grad = dot_tn(m[...], branch).reshape(4, b, d)
        gpf[...] = grad
        gpb[...] = grad.astype(BF16)
        dbs[...] = jnp.broadcast_to(col_sum(d_up.astype(F32)), (8, g))
        narrow = []
        for slot, mask in enumerate(PLANE_PEERS):
            narrow.append(self.send(gpb.at[lax.rem(self.at_peer(mask) // 2, 4)], gpr.at[slot], mask))
            narrow.append(self.send(dbs, dbr.at[slot], mask))
        return dict(wide=wide, narrow=narrow)

    def feed_weights_middle(self, tower, t, sent):
        b = tower.block
        gpf, gpr = self.ref[t + "gpf"], self.ref[t + "gpr"]
        gff, gfr, gf2, gf3r = (self.ref[t + name] for name in ("gff", "gfr", "gf2", "gf3r"))
        self.wait(sent["wide"])
        total = gff[:, self.plane]
        for slot in range(3):
            total = total + gfr[slot].astype(F32)
        gf2[...] = total.astype(BF16)
        self.ref[t + "gf3"][...] = total
        sent["line"] = []
        for mask in Z_PEERS:
            sent["line"].append(self.send(gf2.at[self.at_peer(mask) // 8], gf3r.at[self.zed], mask))
        self.wait(sent["narrow"])
        total = gpf[self.plane]
        for slot in range(3):
            total = total + gpr[slot].astype(F32)
        self.ref["d" + t + "proj"][...] = total
        bias = self.ref[t + "dbs"][0:1, :]
        for slot in range(3):
            bias = bias + self.ref[t + "dbr"][slot, 0:1, :]
        mine = jnp.zeros((1, b), F32)
        for plane in range(4):
            mine = jnp.where(self.plane == plane, bias[:, b * plane : b * (plane + 1)], mine)
        self.ref["d" + t + "fcb"][...] = mine

    def feed_weights_end(self, tower, t, sent):
        gf3, gf3r, gf4 = (self.ref[t + name] for name in ("gf3", "gf3r", "gf4"))
        self.wait(sent["line"])
        own = gf3[self.zed]
        for zed in range(4):
            gf3[zed] = jnp.where(self.zed == zed, own, gf3r[zed].astype(F32))
        rows = tower.rows
        start = pl.multiple_of((1 - self.core) * rows, 8)
        sent["last"] = self.send(gf3.at[:, pl.ds(start, rows)], gf4, 1)
        self.ref[t + "fc_last"] = sent["last"]

    def attend_back(self, tower, t):
        vec, w2 = self.ref[t + "vecs"], self.ref[t + "w2"]
        g2 = self.ref[t + "g2"][self.core, self.zed]
        total = self.line_total(self.ref[t + "hpf"][self.core, self.zed], self.ref[t + "dcr"])
        normed, inverse = self.ref[t + "xh2"], self.ref[t + "inv2"]
        scaled = total * vec[5:6, :]
        inner = (
            scaled
            - jnp.mean(scaled, -1, keepdims=True)
            - normed * jnp.mean(scaled * normed, -1, keepdims=True)
        )
        g1 = g2 + inverse * inner
        branch = g1.astype(BF16)
        d_context = dot_nt(branch, w2[1]).astype(BF16)
        self.ref[t + "g1"], self.ref[t + "do"] = g1, d_context
        self.ref[t + "sums"] = dict(
            dg2=col_sum(total * normed),
            db2=col_sum(total),
            dbo=col_sum(branch.astype(F32)),
            dbp=col_sum(g2.astype(BF16).astype(F32)),
            dbv=col_sum(d_context.astype(F32)),
        )
        copies = self.share_z_line(self.ref[t + "wg"], branch)
        return copies + self.share_z_line(self.ref[t + "dog"], d_context)

    def attend_back_end(self, tower, t):
        r = tower.queries
        w1, w2, a = self.ref[t + "w1"], self.ref[t + "w2"], self.ref[t + "a"]
        p32, lh, rh = self.ref[t + "p32"], self.ref[t + "lh"], self.ref[t + "rh"]
        dvt = dot_nt(expand_heads(self.ref[t + "do"]), w2[0]).astype(BF16)
        rh[r : 2 * r, :] = dvt
        d_probs = dot_nt(dvt, a[...])
        probs = p32[...]
        weighted = probs * d_probs
        d_scores = (weighted - probs * jnp.sum(weighted, -1, keepdims=True)).astype(BF16)
        d_scores = (d_scores.astype(F32) * 0.125).astype(BF16)
        lh[0:r, :] = d_scores
        moved = dot(d_scores, a[...])
        self.ref[t + "in2t"][...] = moved.T.astype(BF16)
        copies = self.to_z_line(self.ref[t + "in2t"], self.ref[t + "in2r"])
        d_query = join_heads(dot(moved.astype(BF16), w1[1])).astype(BF16)
        copies += self.share_z_line(self.ref[t + "dqg"], d_query)
        self.ref[t + "sums"]["dbq"] = col_sum(d_query.astype(F32))
        high, low = split_two(dot_nt(d_query, w1[0]))
        rh[2 * r : 2 * r + PAD, :] = high
        rh[2 * r + PAD : 2 * r + 2 * PAD, :] = low
        return copies

    def input_gradient(self, tower, t):
        r, d = tower.queries, tower.width
        lh, rh, da, gp, xh, inv, vec = (
            self.ref[t + name] for name in ("lh", "rh", "da", "gp", "xh", "inv", "vecs")
        )
        out = self.ref["dx" + t]
        da[...] = dot_tn(lh[...], rh[...])
        high, low = split_two(self.ref[t + "g1"])
        gp[...] = dot_tn(lh[2 * r : 2 * r + 2 * PAD, :], jnp.concatenate([high, low], 0))
        step = 32

        def body(index, carry):
            rows = pl.ds(pl.multiple_of(index * step, step), step)
            z, normed = da[rows, :], xh[rows, :]
            scaled = z * vec[0:1, :]
            inner = (
                scaled
                - jnp.mean(scaled, -1, keepdims=True)
                - normed * jnp.mean(scaled * normed, -1, keepdims=True)
            )
            out[rows, :] = inv[rows, 0:1] * inner + gp[rows, :]
            return (
                carry[0] + jnp.sum((z * normed).reshape(step // 8, 8, d), 0),
                carry[1] + jnp.sum(z.reshape(step // 8, 8, d), 0),
            )

        zero = jnp.zeros((8, d), F32)
        gain, shift = lax.fori_loop(0, tower.tokens // step, body, (zero, zero))
        sums = self.ref[t + "sums"]
        rows = [col_sum(gain), col_sum(shift)]
        rows += [sums[name] for name in ("dbq", "dbv", "dbo", "dg2", "db2", "dbp")]
        self.ref[t + "rows"] = jnp.concatenate(rows, 0)

    def vector_sum_begin(self):
        vz, vzr = self.ref["vz"], self.ref["vzr"]
        vz[...] = jnp.concatenate([self.ref["irows"], self.ref["trows"]], 1)
        return [self.send(vz, vzr.at[slot], mask) for slot, mask in enumerate(Z_PEERS)]

    def vector_sum_middle(self, copies):
        self.wait(copies)
        vz, vzr, vp, vpr = (self.ref[name] for name in ("vz", "vzr", "vp", "vpr"))
        vp[...] = vz[...] + vzr[0] + vzr[1] + vzr[2]
        return [self.send(vp, vpr.at[slot], mask) for slot, mask in enumerate(PLANE_PEERS)]

    def vector_sum_end(self, copies):
        self.wait(copies)
        vp, vpr, vc, vcr = (self.ref[name] for name in ("vp", "vpr", "vc", "vcr"))
        vc[...] = vp[...] + vpr[0] + vpr[1] + vpr[2]
        return [self.send(vc, vcr, 1)]

    def vector_sum_done(self, copies):
        self.wait(copies)
        total = self.ref["vc"][...] + self.ref["vcr"][...]
        at = 0
        for t, tower in (("i", self.ti), ("t", self.tt)):
            d, rows = tower.width, tower.rows
            values = total[:, at : at + d]
            at += d
            high, rest = split_two(values)
            rest_high, rest_low = split_two(values - high.astype(F32))
            pick = iota((d, 128), 0) == iota((d, 128), 1) + self.me * rows
            pick = pick.astype(F32).astype(BF16)
            picked = dot(high, pick) + dot(rest_high, pick) + dot(rest_low, pick)
            self.ref["d" + t + "vec"][...] = picked[:, 0:rows]

    def place(self, rows, at, tower):
        parts = []
        if at:
            parts.append(jnp.zeros((at, rows.shape[1]), BF16))
        parts.append(rows)
        if 256 - at - rows.shape[0]:
            parts.append(jnp.zeros((256 - at - rows.shape[0], rows.shape[1]), BF16))
        return jnp.concatenate(parts, 0)

    def in_plane(self, tower, t, name, grad):
        f, b, landing = (self.ref[t + name + suffix] for suffix in ("f", "b", "r"))
        grad = grad.reshape(4, tower.chip_rows, grad.shape[1])
        f[...] = grad
        b[...] = grad.astype(BF16)
        copies = []
        for slot, mask in enumerate(PLANE_PEERS):
            copies.append(self.send(b.at[lax.rem(self.at_peer(mask) // 2, 4)], landing.at[slot], mask))
        self.ref[t + name + "copies"] = copies

    def round_one(self, tower, t, early, middle):
        r = tower.queries
        in1r, dog, wg, drb = self.ref[t + "in1r"], self.ref[t + "dog"], self.ref[t + "wg"], self.ref["drb"]
        self.wait(early)
        self.wait(middle)
        value = out = proj = 0.0
        for zed in range(4):
            operand = in1r[zed]
            value = value + dot(operand, self.place(expand_heads(dog[zed]), 0, tower))
            out = out + dot(operand, self.place(wg[zed], r, tower))
            if tower.extra:
                proj = proj + dot(operand, self.place(drb[self.core, zed], r + 2 * PAD, tower))
        parts = [value, out] + ([proj] if tower.extra else [])
        self.in_plane(tower, t, "r1", jnp.concatenate(parts, 1))

    def round_two(self, tower, t, late):
        r = tower.queries
        in1r, in2r, qg, dqg = (self.ref[t + name] for name in ("in1r", "in2r", "qg", "dqg"))
        self.wait(late)
        query = key = 0.0
        for zed in range(4):
            query = query + dot(in1r[zed], self.place(dqg[zed], r + PAD, tower))
            key = key + dot(in2r[zed], expand_heads(qg[zed]))
        self.in_plane(tower, t, "r2", jnp.concatenate([query, key], 1))

    def rounds_end(self, tower, t):
        rows = tower.rows
        for name in ("r1", "r2"):
            f, landing, total, last = (self.ref[t + name + suffix] for suffix in ("f", "r", "s", "p"))
            self.wait(self.ref[t + name + "copies"])
            values = f[self.plane]
            for slot in range(3):
                values = values + landing[slot].astype(F32)
            total[...] = values
            start = pl.multiple_of((1 - self.core) * rows, 8)
            self.ref[t + name + "last"] = self.send(total.at[pl.ds(start, rows)], last, 1)

    def rounds_done(self, tower, t):
        rows, d, b, g = tower.rows, tower.width, tower.block, tower.group
        start = pl.multiple_of(self.core * rows, 8)
        done = {}
        for name in ("r1", "r2"):
            self.ref[t + name + "last"].wait_recv()
            done[name] = self.ref[t + name + "s"][pl.ds(start, rows), :] + self.ref[t + name + "p"][...]
        qkv = self.ref["d" + t + "qkv"]
        qkv[:, 0 : 2 * d] = done["r2"]
        qkv[:, 2 * d : 3 * d] = done["r1"][:, 0:d]
        self.ref["d" + t + "out"][...] = done["r1"][:, d : 2 * d]
        if tower.extra:
            self.ref["dmap"][...] = done["r1"][:, 2 * d :]
        self.ref[t + "fc_last"].wait_recv()
        gf3, gf4, out = self.ref[t + "gf3"], self.ref[t + "gf4"], self.ref["d" + t + "fc"]
        for zed in range(4):
            own, got = gf3[zed, pl.ds(start, rows), :], gf4[zed]
            for half in range(2):
                values = jnp.where(self.core == half, own, got)
                for plane in range(4):
                    device = 8 * zed + 2 * plane + half
                    out[:, b * device : b * (device + 1)] = values[:, b * plane : b * (plane + 1)]


def local_fused(
    picture_patch_inputs,
    caption_packed_inputs,
    picture_attend_entry_weight,
    picture_attend_exit_weight,
    picture_widening_weight,
    picture_narrowing_weight,
    picture_affine_entries,
    picture_widening_offset,
    caption_attend_entry_weight,
    caption_attend_exit_weight,
    caption_widening_weight,
    caption_narrowing_weight,
    caption_affine_entries,
    caption_widening_offset,
    picture_feature_mapping,
    sharpness_exponent,
    caption_token_counts,
    matching_picture_index,
):
    n_img, d_img = picture_patch_inputs.shape
    n_txt, d_txt = caption_packed_inputs.shape
    pad_img, pad_txt = -(-n_img // 128) * 128, -(-n_txt // 128) * 128
    ti = Tower(
        d_img, pad_img, picture_attend_entry_weight.shape[1], picture_widening_offset.shape[1], n_img,
        picture_feature_mapping.shape[1] // 2,
    )
    tt = Tower(d_txt, pad_txt, caption_attend_entry_weight.shape[1], caption_widening_offset.shape[1], n_txt, 0)
    args = (
        jnp.pad(picture_patch_inputs, ((0, pad_img - n_img), (0, 0))),
        jnp.pad(caption_packed_inputs, ((0, pad_txt - n_txt), (0, 0))),
        picture_attend_entry_weight[0],
        picture_attend_exit_weight[0],
        picture_widening_weight[0],
        picture_narrowing_weight[0],
        picture_affine_entries[0],
        picture_widening_offset,
        caption_attend_entry_weight[0],
        caption_attend_exit_weight[0],
        caption_widening_weight[0],
        caption_narrowing_weight[0],
        caption_affine_entries[0],
        caption_widening_offset,
        picture_feature_mapping,
        sharpness_exponent.reshape(1),
        caption_token_counts,
        matching_picture_index,
    )
    names, shapes = [], []
    for t, tower in (("i", ti), ("t", tt)):
        for name, shape in tower.scratch().items():
            names.append(t + name)
            shapes.append(shape)
    for name, (shape, kind) in SHARED.items():
        names.append(name)
        shapes.append(pltpu.VMEM(shape, kind))
    names += ["ssem", "rsem"]
    shapes += [pltpu.SemaphoreType.DMA((N_SEMS,)), pltpu.SemaphoreType.DMA((N_SEMS,))]
    images = n_img // TOK_I

    def kernel(*refs):
        Step(ti, tt, images, list(INPUTS) + list(OUTPUTS) + names, refs).run()

    def out(*shape):
        return jax.ShapeDtypeStruct(shape, F32)

    scalars = ("sharp", "counts", "match")
    results = pl.pallas_call(
        kernel,
        out_shape=(
            out(1, 1), out(1, 1), out(pad_img, d_img), out(pad_txt, d_txt),
            out(ti.rows, 3 * d_img), out(ti.rows, d_img), out(ti.rows, 32 * ti.block), out(ti.block, d_img),
            out(8, ti.rows), out(1, ti.block),
            out(tt.rows, 3 * d_txt), out(tt.rows, d_txt), out(tt.rows, 32 * tt.block), out(tt.block, d_txt),
            out(8, tt.rows), out(1, tt.block), out(ti.rows, 2 * ti.extra),
        ),
        in_specs=[
            pl.BlockSpec(memory_space=pltpu.SMEM if name in scalars else pltpu.VMEM) for name in INPUTS
        ],
        out_specs=tuple(pl.BlockSpec(memory_space=pltpu.VMEM) for _ in OUTPUTS),
        scratch_shapes=shapes,
        compiler_params=pltpu.CompilerParams(
            collective_id=0, has_side_effects=True, vmem_limit_bytes=60 * 2**20
        ),
        name="contrastive_step",
    )(*args)
    got = dict(zip(OUTPUTS, results, strict=True))
    stacked = ("iqkv", "iout", "ifc", "iproj", "ivec", "tqkv", "tout", "tfc", "tproj", "tvec")
    final = []
    for name in OUTPUTS:
        value = got[name]
        if name in ("loss", "dls"):
            value = value.reshape(())
        elif name == "dxi":
            value = value[:n_img]
        elif name == "dxt":
            value = value[:n_txt]
        elif name[1:] in stacked:
            value = value[None]
        final.append(value)
    return tuple(final)


def solution(mesh):
    placed = (
        P("dp", None),
        P("dp", None),
        P(None, "dp", None),
        P(None, "dp", None),
        P(None, "dp", None),
        P(None, "dp", None),
        P(None, None, "dp"),
        P(None, "dp"),
        P(None, "dp", None),
        P(None, "dp", None),
        P(None, "dp", None),
        P(None, "dp", None),
        P(None, None, "dp"),
        P(None, "dp"),
        P("dp", None),
        P(),
        P("dp", None),
        P("dp"),
    )
    return jax.shard_map(
        local_fused if fits(mesh) else local_plain,
        mesh=mesh,
        in_specs=placed,
        out_specs=(
            P(),
            P(),
            P("dp", None),
            P("dp", None),
            P(None, "dp", None),
            P(None, "dp", None),
            P(None, "dp", None),
            P(None, "dp", None),
            P(None, None, "dp"),
            P(None, "dp"),
            P(None, "dp", None),
            P(None, "dp", None),
            P(None, "dp", None),
            P(None, "dp", None),
            P(None, None, "dp"),
            P(None, "dp"),
            P("dp", None),
        ),
        check_vma=False,
    )
```

```python
import jax
import jax.numpy as jnp
from jax import lax
from jax.experimental import pallas as pl
from jax.experimental.pallas import tpu as pltpu
from jax.sharding import PartitionSpec as P

HD = 64
TOK_I = 50
TOK_T = 77
CAP_ROW = 4


def norm_forward(hidden, norm_gain, norm_shift):
    row_mean = jnp.mean(hidden, -1, keepdims=True)
    centred = hidden - row_mean
    inverse = lax.rsqrt(jnp.mean(centred * centred, -1, keepdims=True) + 1e-05)
    normed = centred * inverse
    return (normed, inverse, normed * norm_gain + norm_shift)


def norm_backward(upstream, normed, inverse, norm_gain):
    scaled = upstream * norm_gain
    inner_sum = (
        scaled
        - jnp.mean(scaled, -1, keepdims=True)
        - normed * jnp.mean(scaled * normed, -1, keepdims=True)
    )
    return (inverse * inner_sum, jnp.sum(upstream * normed, (0, 1)), jnp.sum(upstream, (0, 1)))


def split_heads(values):
    return values.reshape(values.shape[0], values.shape[1], values.shape[2] // HD, HD)


def attention_scores(queries, key_heads, allowed):
    scores = (
        jnp.einsum("sqhd,skhd->shqk", queries, key_heads, preferred_element_type=jnp.float32)
        * 0.125
    )
    return jnp.where(allowed[:, None], scores, -1000000000.0)


def block_forward(hidden, weights, allowed):
    w_qkv, w_out, w_fc, w_proj, vectors, fc_bias = weights
    vectors = vectors.astype(jnp.float32)
    fc_bias = fc_bias.astype(jnp.float32)
    feature_width = hidden.shape[-1]
    normed_first, inverse_first, first = norm_forward(hidden, vectors[0], vectors[1])
    first_low = first.astype(jnp.bfloat16)
    projected = jnp.einsum("std,de->ste", first_low, w_qkv, preferred_element_type=jnp.float32)
    queries = (projected[..., :feature_width] + vectors[2]).astype(jnp.bfloat16)
    key_heads = projected[..., feature_width : 2 * feature_width].astype(jnp.bfloat16)
    values = (projected[..., 2 * feature_width :] + vectors[3]).astype(jnp.bfloat16)
    scores = attention_scores(split_heads(queries), split_heads(key_heads), allowed)
    totals = jax.nn.logsumexp(scores, -1, keepdims=True)
    attn_probs = jnp.exp(scores - totals).astype(jnp.bfloat16)
    context = jnp.einsum(
        "shqk,skhd->sqhd", attn_probs, split_heads(values), preferred_element_type=jnp.float32
    )
    context = context.reshape(hidden.shape).astype(jnp.bfloat16)
    middle = hidden + (
        jnp.einsum("std,de->ste", context, w_out, preferred_element_type=jnp.float32) + vectors[4]
    )
    normed_second, inverse_second, second = norm_forward(middle, vectors[5], vectors[6])
    second_low = second.astype(jnp.bfloat16)
    upward = (
        jnp.einsum("std,df->stf", second_low, w_fc, preferred_element_type=jnp.float32) + fc_bias
    )
    activated = (upward * jax.nn.sigmoid(1.702 * upward)).astype(jnp.bfloat16)
    output = middle + (
        jnp.einsum("stf,fd->std", activated, w_proj, preferred_element_type=jnp.float32)
        + vectors[7]
    )
    stored = (
        normed_first,
        inverse_first,
        first_low,
        queries,
        key_heads,
        values,
        totals,
        context,
        normed_second,
        inverse_second,
        second_low,
        upward,
        activated,
    )
    return (output, stored)


def block_backward(upstream, weights, stored, allowed):
    w_qkv, w_out, w_fc, w_proj, vectors, fc_bias = weights
    vectors = vectors.astype(jnp.float32)
    (
        normed_first,
        inverse_first,
        first_low,
        queries,
        key_heads,
        values,
        totals,
        context,
        normed_second,
        inverse_second,
        second_low,
        upward,
        activated,
    ) = stored
    feature_width = queries.shape[-1]
    branch = upstream.astype(jnp.bfloat16)
    d_proj_bias = jnp.sum(branch.astype(jnp.float32), (0, 1))
    d_w_proj = jnp.einsum("stf,std->fd", activated, branch, preferred_element_type=jnp.float32)
    d_activated = jnp.einsum("std,fd->stf", branch, w_proj, preferred_element_type=jnp.float32)
    sigmoid_up = jax.nn.sigmoid(1.702 * upward)
    d_upward = (
        d_activated * (sigmoid_up + 1.702 * upward * sigmoid_up * (1.0 - sigmoid_up))
    ).astype(jnp.bfloat16)
    d_fc_bias = jnp.sum(d_upward.astype(jnp.float32), (0, 1))
    d_w_fc = jnp.einsum("std,stf->df", second_low, d_upward, preferred_element_type=jnp.float32)
    d_second = jnp.einsum("stf,df->std", d_upward, w_fc, preferred_element_type=jnp.float32)
    d_middle_norm, d_gain_second, d_shift_second = norm_backward(
        d_second, normed_second, inverse_second, vectors[5]
    )
    d_middle = upstream + d_middle_norm
    attn_branch = d_middle.astype(jnp.bfloat16)
    d_out_bias = jnp.sum(attn_branch.astype(jnp.float32), (0, 1))
    d_w_out = jnp.einsum("std,ste->de", context, attn_branch, preferred_element_type=jnp.float32)
    d_context = jnp.einsum("ste,de->std", attn_branch, w_out, preferred_element_type=jnp.float32)
    d_context = split_heads(d_context.astype(jnp.bfloat16))
    query_heads = split_heads(queries)
    key_split = split_heads(key_heads)
    scores = attention_scores(query_heads, key_split, allowed)
    attn_probs = jnp.exp(scores - totals)
    d_probs = jnp.einsum(
        "sqhd,skhd->shqk", d_context, split_heads(values), preferred_element_type=jnp.float32
    )
    d_scores = (attn_probs * (d_probs - jnp.sum(attn_probs * d_probs, -1, keepdims=True))).astype(
        jnp.bfloat16
    )
    d_queries = (
        jnp.einsum("shqk,skhd->sqhd", d_scores, key_split, preferred_element_type=jnp.float32)
        * 0.125
    ).astype(jnp.bfloat16)
    d_keys = (
        jnp.einsum("shqk,sqhd->skhd", d_scores, query_heads, preferred_element_type=jnp.float32)
        * 0.125
    ).astype(jnp.bfloat16)
    d_values = jnp.einsum(
        "shqk,sqhd->skhd",
        attn_probs.astype(jnp.bfloat16),
        d_context,
        preferred_element_type=jnp.float32,
    ).astype(jnp.bfloat16)
    flat_shape = (queries.shape[0], queries.shape[1], feature_width)
    d_queries = d_queries.reshape(flat_shape)
    d_keys = d_keys.reshape(flat_shape)
    d_values = d_values.reshape(flat_shape)
    d_mixed = jnp.concatenate([d_queries, d_keys, d_values], -1)
    d_w_qkv = jnp.einsum("std,ste->de", first_low, d_mixed, preferred_element_type=jnp.float32)
    d_first = jnp.einsum("ste,de->std", d_mixed, w_qkv, preferred_element_type=jnp.float32)
    d_input_norm, d_gain_first, d_shift_first = norm_backward(
        d_first, normed_first, inverse_first, vectors[0]
    )
    d_hidden = d_middle + d_input_norm
    d_vectors = jnp.stack(
        [
            d_gain_first,
            d_shift_first,
            jnp.sum(d_queries.astype(jnp.float32), (0, 1)),
            jnp.sum(d_values.astype(jnp.float32), (0, 1)),
            d_out_bias,
            d_gain_second,
            d_shift_second,
            d_proj_bias,
        ]
    )
    return (d_hidden, (d_w_qkv, d_w_out, d_w_fc, d_w_proj, d_vectors, d_fc_bias))


def gather_first(img_stack, txt_stack, picture_feature_mapping):
    return (
        lax.all_gather(img_stack[0], "dp", axis=1, tiled=True),
        lax.all_gather(img_stack[1], "dp", axis=1, tiled=True),
        lax.all_gather(img_stack[2], "dp", axis=1, tiled=True),
        lax.all_gather(img_stack[3], "dp", axis=1, tiled=True),
        lax.all_gather(img_stack[4], "dp", axis=2, tiled=True),
        lax.all_gather(img_stack[5], "dp", axis=1, tiled=True),
        lax.all_gather(txt_stack[0], "dp", axis=1, tiled=True),
        lax.all_gather(txt_stack[1], "dp", axis=1, tiled=True),
        lax.all_gather(txt_stack[2], "dp", axis=1, tiled=True),
        lax.all_gather(txt_stack[3], "dp", axis=1, tiled=True),
        lax.all_gather(txt_stack[4], "dp", axis=2, tiled=True),
        lax.all_gather(txt_stack[5], "dp", axis=1, tiled=True),
        lax.all_gather(picture_feature_mapping, "dp", axis=0, tiled=True),
    )


def layer_of(stacks, layer_index):
    return tuple((stacked[layer_index] for stacked in stacks))


def local_plain(
    picture_patch_inputs,
    caption_packed_inputs,
    picture_attend_entry_weight,
    picture_attend_exit_weight,
    picture_widening_weight,
    picture_narrowing_weight,
    picture_affine_entries,
    picture_widening_offset,
    caption_attend_entry_weight,
    caption_attend_exit_weight,
    caption_widening_weight,
    caption_narrowing_weight,
    caption_affine_entries,
    caption_widening_offset,
    picture_feature_mapping,
    sharpness_exponent,
    caption_token_counts,
    matching_picture_index,
):
    img_stack = (
        picture_attend_entry_weight,
        picture_attend_exit_weight,
        picture_widening_weight,
        picture_narrowing_weight,
        picture_affine_entries,
        picture_widening_offset,
    )
    txt_stack = (
        caption_attend_entry_weight,
        caption_attend_exit_weight,
        caption_widening_weight,
        caption_narrowing_weight,
        caption_affine_entries,
        caption_widening_offset,
    )
    images = picture_patch_inputs.shape[0] // TOK_I
    row_count = caption_packed_inputs.shape[0] // TOK_T
    img_hidden = picture_patch_inputs.astype(jnp.float32).reshape(images, TOK_I, -1)
    txt_hidden = caption_packed_inputs.astype(jnp.float32).reshape(row_count, TOK_T, -1)
    img_allowed = jnp.ones((images, TOK_I, TOK_I), dtype=jnp.bool_)
    seg_ends = jnp.cumsum(caption_token_counts, axis=1)
    position = jnp.arange(TOK_T, dtype=jnp.int32)
    segment = jnp.sum((position[None, :, None] >= seg_ends[:, None, :]).astype(jnp.int32), -1)
    txt_allowed = (segment[:, :, None] == segment[:, None, :]) & (
        position[None, None, :] <= position[None, :, None]
    )
    pooling = (position[None, None, :] == seg_ends[:, :, None] - 1).astype(jnp.float32)
    gathered = gather_first(img_stack, txt_stack, picture_feature_mapping)
    img_full = gathered[0:6]
    txt_full = gathered[6:12]
    projection = gathered[12]
    img_stored, txt_stored = ([], [])
    layer_index = 0
    img_hidden, stored = block_forward(img_hidden, layer_of(img_full, layer_index), img_allowed)
    img_stored.append(stored)
    layer_index = 0
    txt_hidden, stored = block_forward(txt_hidden, layer_of(txt_full, layer_index), txt_allowed)
    txt_stored.append(stored)
    pooled_img = img_hidden[:, 0, :].astype(jnp.bfloat16)
    raw_img = jnp.dot(pooled_img, projection, preferred_element_type=jnp.float32)
    scale_img = lax.rsqrt(jnp.sum(raw_img * raw_img, -1, keepdims=True) + 1e-06)
    unit_img = raw_img * scale_img
    raw_txt = jnp.einsum("sct,std->scd", pooling, txt_hidden, precision=lax.Precision.HIGHEST)
    raw_txt = raw_txt.reshape(-1, raw_txt.shape[-1])
    scale_txt = lax.rsqrt(jnp.sum(raw_txt * raw_txt, -1, keepdims=True) + 1e-06)
    unit_txt = raw_txt * scale_txt
    image_embedding_rows = unit_img.astype(jnp.bfloat16)
    text_embedding_rows = unit_txt.astype(jnp.bfloat16)
    all_img, all_txt = (
        lax.all_gather(image_embedding_rows, "dp", axis=0, tiled=True),
        lax.all_gather(text_embedding_rows, "dp", axis=0, tiled=True),
    )
    batch_total = all_img.shape[0]
    affinity_sharpness = jnp.exp(sharpness_exponent)
    picture_wise_affinity_table = affinity_sharpness * jnp.einsum(
        "ce,ie->ci", text_embedding_rows, all_img, preferred_element_type=jnp.float32
    )
    caption_wise_affinity_table = affinity_sharpness * jnp.einsum(
        "ce,ie->ci", all_txt, image_embedding_rows, preferred_element_type=jnp.float32
    )
    lse_rows = jax.nn.logsumexp(picture_wise_affinity_table, 1)
    lse_cols = jax.nn.logsumexp(caption_wise_affinity_table, 0)
    columns = jnp.arange(batch_total, dtype=jnp.int32)
    target_rows = (matching_picture_index[:, None] == columns[None, :]).astype(jnp.float32)
    loss_part = (jnp.sum(lse_rows) + jnp.sum(lse_cols)) / (2 * batch_total) - jnp.sum(
        target_rows * picture_wise_affinity_table
    ) / batch_total
    probs_rows = jnp.exp(picture_wise_affinity_table - lse_rows[:, None])
    probs_cols = jnp.exp(caption_wise_affinity_table - lse_cols[None, :])
    gathered_image_matrix = all_img.astype(jnp.float32)
    gathered_text_matrix = all_txt.astype(jnp.float32)
    highest_precision = lax.Precision.HIGHEST
    row_gradient = probs_rows / (2 * batch_total) - target_rows / batch_total
    column_gradient = probs_cols / (2 * batch_total)
    caption_normalized_adjoint = affinity_sharpness * jnp.dot(
        row_gradient, gathered_image_matrix, precision=highest_precision
    )
    picture_normalized_adjoint = affinity_sharpness * jnp.dot(
        column_gradient.T, gathered_text_matrix, precision=highest_precision
    )
    picture_distributed_adjoint = affinity_sharpness * jnp.dot(
        row_gradient.T, text_embedding_rows.astype(jnp.float32), precision=highest_precision
    )
    caption_distributed_adjoint = affinity_sharpness * jnp.dot(
        column_gradient, image_embedding_rows.astype(jnp.float32), precision=highest_precision
    )
    back_img, back_txt = (
        lax.psum_scatter(picture_distributed_adjoint, "dp", scatter_dimension=0, tiled=True),
        lax.psum_scatter(caption_distributed_adjoint, "dp", scatter_dimension=0, tiled=True),
    )
    picture_normalized_adjoint = picture_normalized_adjoint + back_img
    caption_normalized_adjoint = caption_normalized_adjoint + back_txt
    scale_part = jnp.sum(row_gradient * picture_wise_affinity_table) + jnp.sum(
        column_gradient * caption_wise_affinity_table
    )
    loss, d_scale = lax.psum((loss_part, scale_part), "dp")
    img_back = gathered[0:6]
    txt_back = gathered[6:12]
    back_projection = gathered[12]
    d_raw_img = scale_img * (
        picture_normalized_adjoint
        - unit_img * jnp.sum(picture_normalized_adjoint * unit_img, -1, keepdims=True)
    )
    d_raw_low = d_raw_img.astype(jnp.bfloat16)
    d_projection = jnp.dot(pooled_img.T, d_raw_low, preferred_element_type=jnp.float32)
    d_pooled = jnp.dot(d_raw_low, back_projection.T, preferred_element_type=jnp.float32)
    d_img_hidden = jnp.concatenate(
        [d_pooled[:, None, :], jnp.zeros((images, TOK_I - 1, d_pooled.shape[-1]), jnp.float32)], 1
    )
    d_raw_txt = scale_txt * (
        caption_normalized_adjoint
        - unit_txt * jnp.sum(caption_normalized_adjoint * unit_txt, -1, keepdims=True)
    )
    d_txt_hidden = jnp.einsum(
        "sct,scd->std",
        pooling,
        d_raw_txt.reshape(row_count, CAP_ROW, -1),
        precision=highest_precision,
    )
    img_layer_grads, txt_layer_grads = ([], [])
    layer_index = 0
    d_img_hidden, layer_grads = block_backward(
        d_img_hidden, layer_of(img_back, layer_index), img_stored[layer_index], img_allowed
    )
    img_layer_grads.append(layer_grads)
    img_layer_grads = img_layer_grads[::-1]
    img_local = tuple(
        (jnp.stack([grads[member] for grads in img_layer_grads]) for member in range(6))
    )
    layer_index = 0
    d_txt_hidden, layer_grads = block_backward(
        d_txt_hidden, layer_of(txt_back, layer_index), txt_stored[layer_index], txt_allowed
    )
    txt_layer_grads.append(layer_grads)
    txt_layer_grads = txt_layer_grads[::-1]
    txt_local = tuple(
        (jnp.stack([grads[member] for grads in txt_layer_grads]) for member in range(6))
    )
    summed = (
        lax.psum_scatter(img_local[0], "dp", scatter_dimension=1, tiled=True),
        lax.psum_scatter(img_local[1], "dp", scatter_dimension=1, tiled=True),
        lax.psum_scatter(img_local[2], "dp", scatter_dimension=1, tiled=True),
        lax.psum_scatter(img_local[3], "dp", scatter_dimension=1, tiled=True),
        lax.psum_scatter(img_local[4], "dp", scatter_dimension=2, tiled=True),
        lax.psum_scatter(img_local[5], "dp", scatter_dimension=1, tiled=True),
        lax.psum_scatter(txt_local[0], "dp", scatter_dimension=1, tiled=True),
        lax.psum_scatter(txt_local[1], "dp", scatter_dimension=1, tiled=True),
        lax.psum_scatter(txt_local[2], "dp", scatter_dimension=1, tiled=True),
        lax.psum_scatter(txt_local[3], "dp", scatter_dimension=1, tiled=True),
        lax.psum_scatter(txt_local[4], "dp", scatter_dimension=2, tiled=True),
        lax.psum_scatter(txt_local[5], "dp", scatter_dimension=1, tiled=True),
        lax.psum_scatter(d_projection, "dp", scatter_dimension=0, tiled=True),
    )
    return (
        loss,
        d_scale,
        d_img_hidden.reshape(images * TOK_I, -1),
        d_txt_hidden.reshape(row_count * TOK_T, -1),
        summed[0],
        summed[1],
        summed[2],
        summed[3],
        summed[4],
        summed[5],
        summed[6],
        summed[7],
        summed[8],
        summed[9],
        summed[10],
        summed[11],
        summed[12],
    )


F32 = jnp.float32
BF16 = jnp.bfloat16
Z_PEERS = (8, 16, 24)
PLANE_PEERS = (2, 4, 6)
ALL_PEERS = (1, 2, 3, 4, 5, 6, 7, 8, 9, 16, 17, 24, 25)
PAD = 16
N_SEMS = 100
STEP_ROWS = 32


def fits(mesh):
    return mesh.size == 32


def dot(left, right):
    return lax.dot_general(left, right, (((1,), (0,)), ((), ())), preferred_element_type=F32)


def dot_nt(left, right):
    return lax.dot_general(left, right, (((1,), (1,)), ((), ())), preferred_element_type=F32)


def dot_tn(left, right):
    return lax.dot_general(left, right, (((0,), (0,)), ((), ())), preferred_element_type=F32)


def split_two(values):
    high = values.astype(BF16)
    return high, (values - high.astype(F32)).astype(BF16)


def iota(shape, dim):
    return lax.broadcasted_iota(jnp.int32, shape, dim)


def expand_heads(rows):
    lanes = iota(rows.shape, 1) // HD
    heads = rows.shape[1] // HD
    zero = jnp.zeros_like(rows)
    return jnp.concatenate([jnp.where(lanes == head, rows, zero) for head in range(heads)], 0)


def join_heads(stacked):
    heads = stacked.shape[1] // HD
    lanes = iota((PAD, stacked.shape[1]), 1) // HD
    total = jnp.zeros((PAD, stacked.shape[1]), F32)
    for head in range(heads):
        total = jnp.where(lanes == head, stacked[PAD * head : PAD * (head + 1)], total)
    return total


def small_norm(hidden, gain, shift):
    centred = hidden - jnp.mean(hidden, -1, keepdims=True)
    inverse = lax.rsqrt(jnp.mean(centred * centred, -1, keepdims=True) + 1e-05)
    normed = centred * inverse
    return normed, inverse, normed * gain + shift


def small_norm_back(upstream, normed, inverse, gain):
    scaled = upstream * gain
    return inverse * (
        scaled
        - jnp.mean(scaled, -1, keepdims=True)
        - normed * jnp.mean(scaled * normed, -1, keepdims=True)
    )


def col_sum(values):
    return jnp.sum(values, 0, keepdims=True)


class Tower:
    def __init__(self, along_z, width, real_tokens, rows, block, extra):
        self.along_z = along_z
        self.width = width
        self.real_tokens = real_tokens
        self.tokens = -(-real_tokens // 128) * 128
        self.rows = rows
        self.chip_rows = 2 * rows
        self.block = block
        self.group = 4 * block
        self.heads = width // HD
        self.queries = PAD * self.heads
        self.extra = extra
        self.packed = 2 * width + extra + 4 * self.group
        self.row_pad = -(-rows // 16) * 16
        self.group_peers = Z_PEERS if along_z else PLANE_PEERS
        self.copy_peers = PLANE_PEERS if along_z else Z_PEERS
        self.line_peers = (1,) + tuple(mask + core for mask in self.group_peers for core in range(2))
        self.sums = {}

    def chip_of(self, group, copy):
        return 4 * group + copy if self.along_z else 4 * copy + group

    def device_of(self, group, copy, core):
        return 2 * self.chip_of(group, copy) + core

    def group_of(self, device):
        return device // 8 if self.along_z else lax.rem(device // 2, 4)

    def copy_of(self, device):
        return lax.rem(device // 2, 4) if self.along_z else device // 8

    def chips_of_group(self, ref, group):
        return ref.at[group] if self.along_z else ref.at[:, group]

    def chips_of_copy(self, ref, copy):
        return ref.at[:, copy] if self.along_z else ref.at[copy]

    def scratch(self):
        d, n, r, g, b, cr = self.width, self.tokens, self.queries, self.group, self.block, self.chip_rows
        c1, c2 = 2 * d + 2 * self.extra, 2 * d
        v = pltpu.VMEM
        return dict(
            pk=v((2, self.row_pad, self.packed), BF16),
            pr=v((self.row_pad, self.packed), BF16),
            w1=v((2, 16 * cr, d), BF16),
            w2=v((2, 16 * cr, d), BF16),
            mf=v((4, cr, g), BF16),
            fa=v((4, 4, cr, g), BF16),
            wp=v((4, b, d), BF16),
            vecs=v((8, d), F32),
            bias=v((8, g), F32),
            xp=v((n, d), BF16),
            xh=v((n, d), F32),
            inv=v((n, 128), F32),
            a=v((n, d), BF16),
            p32=v((r, n), F32),
            lh=v((2 * r + 2 * PAD, n), BF16),
            rh=v((2 * r + 2 * PAD, d), BF16),
            ci=v((8, PAD, d), BF16),
            hpf=v((8, PAD, d), F32),
            hps=v((8, PAD, d), BF16),
            hr=v((7, PAD, d), BF16),
            dcf=v((8, PAD, d), F32),
            dcs=v((8, PAD, d), BF16),
            dcr=v((7, PAD, d), BF16),
            sc=v((8, PAD, 128), F32),
            u=v((8 * PAD, g), F32),
            m=v((8 * PAD, g), BF16),
            gpf=v((4, b, d), F32),
            gpb=v((4, b, d), BF16),
            gpr=v((3, b, d), BF16),
            gff=v((4, 4, cr, g), F32),
            gfb=v((4, 4, cr, g), BF16),
            gfr=v((3, 4, cr, g), BF16),
            gf2=v((4, cr, g), BF16),
            gf3=v((4, cr, g), F32),
            gf3r=v((4, cr, g), BF16),
            gf4=v((4, self.rows, g), F32),
            in1t=v((4, 4, cr, 256), BF16),
            in1r=v((4, 4, cr, 256), BF16),
            in2t=v((4, 4, cr, r), BF16),
            in2r=v((4, 4, cr, r), BF16),
            qg=v((4, PAD, d), BF16),
            wg=v((4, PAD, d), BF16),
            dog=v((4, PAD, d), BF16),
            dqg=v((4, PAD, d), BF16),
            r1f=v((4, cr, c1), F32),
            r1b=v((4, cr, c1), BF16),
            r1r=v((3, cr, c1), BF16),
            r1s=v((cr, c1), F32),
            r1p=v((self.rows, c1), F32),
            r2f=v((4, cr, c2), F32),
            r2b=v((4, cr, c2), BF16),
            r2r=v((3, cr, c2), BF16),
            r2s=v((cr, c2), F32),
            r2p=v((self.rows, c2), F32),
            da=v((n, d), F32),
            gp=v((n, d), F32),
            dxs=v((self.real_tokens, d), F32),
            g2=v((8, PAD, d), F32),
            dbs=v((8, g), F32),
            dbr=v((3, 8, g), F32),
        )


def shared_scratch(ti, tt):
    v = pltpu.VMEM
    wide = ti.width + tt.width
    e = tt.width
    rows = 32 * PAD
    return dict(
        vb=v((2, 16, PAD, 128), BF16),
        w3=v((2, ti.width, ti.extra), BF16),
        eb=v((2, 2, 16, PAD, e), BF16),
        gtxt=v((rows, rows), F32),
        gimg=v((rows, rows), F32),
        drb=v((8, PAD, e), BF16),
        vz=v((8, wide), F32),
        vzr=v((3, 8, wide), F32),
        vp=v((8, wide), F32),
        vpr=v((3, 8, wide), F32),
        vc=v((8, wide), F32),
        vcr=v((8, wide), F32),
    )


class Group:
    def __init__(self, step):
        self.step = step
        self.index = step.used
        step.used += 1
        step.groups.append(self)

    def copy(self, src, dst, mask):
        return pltpu.make_async_remote_copy(
            src_ref=src,
            dst_ref=dst,
            send_sem=self.step.ssem.at[self.index],
            recv_sem=self.step.rsem.at[self.index],
            device_id=(self.step.at_peer(mask),),
            device_id_type=pl.DeviceIdType.MESH,
        )

    def send(self, src, dst, mask):
        self.copy(src, dst, mask).start()

    def wait(self, view):
        self.view = view
        self.copy(view, view, 1).wait_recv()

    def finish(self):
        self.copy(self.view, self.view, 1).wait_send()


class Gather:
    def __init__(self, step, slot, span, whole, relay):
        self.step, self.slot, self.span, self.whole, self.relayed = step, slot, span, whole, relay
        self.own = self.step.chip

    def chip(self, mask):
        return self.step.at_peer(mask) // 2

    def spread(self, group, chip):
        here = self.slot(chip)
        for mask in PLANE_PEERS[:2] if self.relayed else PLANE_PEERS:
            group.send(here, here, mask)

    def begin_z(self):
        self.g_z = Group(self.step)
        here = self.slot(self.own)
        for mask in Z_PEERS:
            self.g_z.send(here, here, mask)

    def begin_plane(self):
        self.g_own = Group(self.step)
        self.spread(self.g_own, self.own)

    def middle(self):
        self.g_z.wait(self.span(3))
        self.g_mid = Group(self.step)
        for mask in Z_PEERS:
            self.spread(self.g_mid, self.chip(mask))

    def hand_on(self, mask):
        for half, near, to in ((0, 2, 4), (1, 4, 2)):
            there = self.slot(self.chip(near | mask), half)
            self.g_relay.send(there, there, to)

    def relay_own(self):
        self.g_own.wait(self.span(2))
        self.g_relay = Group(self.step)
        self.hand_on(0)

    def relay(self):
        self.g_mid.wait(self.span(6))
        for mask in Z_PEERS:
            self.hand_on(mask)

    def end(self):
        if self.relayed:
            self.g_relay.wait(self.span(4))
        else:
            self.g_own.wait(self.span(3))
            self.g_mid.wait(self.span(9))
        self.g_core = Group(self.step)
        self.g_core.send(self.whole, self.whole, 1)

    def done(self):
        self.g_core.wait(self.whole)


class Step:
    def __init__(self, ti, tt, images):
        self.ti, self.tt, self.images = ti, tt, images
        me = lax.axis_index("dp")
        self.bits = [lax.rem(me // (1 << bit), 2) for bit in range(5)]
        self.me = me
        self.core = lax.rem(me, 2)
        self.chip = me // 2
        self.plane = lax.rem(me // 2, 4)
        self.zed = me // 8
        for t in (ti, tt):
            t.g, t.r = (self.zed, self.plane) if t.along_z else (self.plane, self.zed)
            t.spot = self.core * 4 + t.g
        self.used = 0
        self.groups = []

    def at_peer(self, mask):
        total = 0
        for bit in range(5):
            value = 1 - self.bits[bit] if mask >> bit & 1 else self.bits[bit]
            total = total + value * (1 << bit)
        return total

    def barrier(self):
        semaphore = pltpu.get_barrier_semaphore()
        for mask in ALL_PEERS:
            pl.semaphore_signal(
                semaphore, inc=1, device_id=(self.at_peer(mask),), device_id_type=pl.DeviceIdType.MESH
            )
        pl.semaphore_wait(semaphore, len(ALL_PEERS))

    def row_gather(self, buffer, rows):
        cols = buffer.shape[2] // 2

        def slot(chip, half=None):
            at = pl.ds(pl.multiple_of(chip * rows, 16), rows)
            if half is None:
                return buffer.at[self.core, at]
            return buffer.at[self.core, at, half * cols : (half + 1) * cols]

        return Gather(
            self, slot, lambda count: buffer.at[self.core, 0 : count * rows], buffer.at[self.core], True
        )

    def line_gather(self, t, buffer):
        group = Group(self)
        here = buffer.at[t.spot]
        for mask in t.line_peers:
            group.send(here, here, mask)
        return group

    def line_scatter(self, t, parts, landing):
        group = Group(self)
        for slot, mask in enumerate(t.line_peers):
            peer = self.at_peer(mask)
            group.send(parts.at[lax.rem(peer, 2) * 4 + t.group_of(peer)], landing.at[slot], mask)
        return group

    def to_group(self, t, block, landing):
        group = Group(self)
        for mask in t.group_peers:
            group.send(t.chips_of_group(block, t.group_of(self.at_peer(mask))), landing.at[t.g], mask)
        landing[t.g] = t.chips_of_group(block, t.g)[...]
        return group

    def share_group(self, t, buffer, values):
        group = Group(self)
        buffer[t.g] = values
        here = buffer.at[t.g]
        for mask in t.group_peers:
            group.send(here, here, mask)
        return group

    def to_copies(self, t, block, landing):
        group = Group(self)
        for slot, mask in enumerate(t.copy_peers):
            group.send(block.at[t.copy_of(self.at_peer(mask))], landing.at[slot], mask)
        return group

    def run(self):
        ti, tt = self.ti, self.tt
        both = (ti, tt)
        self.pack(ti)
        self.pack(tt)
        self.pack_vectors()
        self.barrier()
        for t in both:
            t.pair = Group(self)
            t.pair.send(t.pk.at[1 - self.core], t.pr, 1)
        vb, eb = self.vb, self.eb
        vectors = Gather(
            self,
            lambda chip: vb.at[self.core, chip],
            lambda count: vb.at[self.core, 0:count],
            vb.at[self.core],
            False,
        )
        vectors.begin_z()
        vectors.begin_plane()
        for t in both:
            t.first = self.row_gather(t.w1, t.chip_rows)
            t.second = self.row_gather(t.w2, t.chip_rows)
        third = self.row_gather(self.w3, ti.chip_rows)
        for t in both:
            self.merge(t)
            t.first.begin_z()
            t.first.begin_plane()
        for t in both:
            t.second.begin_z()
        for t in both:
            self.widen_begin(t)
        third.begin_z()
        self.standardize(tt)
        vectors.middle()
        for t in both:
            t.first.middle()
        for t in both:
            t.first.relay_own()
        for t in both:
            t.second.begin_plane()
        for t in both:
            t.second.middle()
        self.standardize(ti)
        for t in both:
            t.first.relay()
        for t in both:
            t.second.relay_own()
        for t in both:
            self.widen_middle(t)
        vectors.end()
        third.begin_plane()
        third.middle()
        vectors.done()
        self.unpack_vectors()
        self.queries(ti)
        self.queries(tt)
        for t in both:
            t.first.end()
        for t in both:
            t.second.relay()
        third.relay_own()
        ti.first.done()
        self.attend(ti)
        tt.first.done()
        self.attend(tt)
        for t in both:
            t.second.end()
        third.relay()
        for t in both:
            t.second.done()
            self.mix(t)
        third.end()
        for t in both:
            self.feed(t)
        third.done()
        for t in both:
            self.embed(t)
        rows = Gather(
            self,
            lambda chip: eb.at[:, self.core, chip],
            lambda count: eb.at[:, self.core, 0:count],
            eb.at[:, self.core],
            False,
        )
        rows.begin_z()
        rows.begin_plane()
        for t in both:
            t.scales = self.line_gather(t, t.sc)
        rows.middle()
        for t in both:
            self.early_operands(t)
        rows.end()
        rows.done()
        for t in both:
            t.scales.wait(t.sc.at[0:7])
        self.contrast()
        for t in both:
            self.feed_back(t)
        for t in both:
            self.feed_weights(t)
        for t in both:
            self.attend_back(t)
        for t in both:
            self.attend_back_end(t)
        for t in both:
            self.input_gradient(t)
        copies = self.vector_sum_begin()
        for t in both:
            self.feed_weights_middle(t)
        for t in both:
            self.round_one(t)
        copies = self.vector_sum_middle(copies)
        for t in both:
            self.round_two(t)
        copies = self.vector_sum_end(copies)
        for t in both:
            self.feed_weights_end(t)
        for t in both:
            self.rounds_end(t)
        self.vector_sum_done(copies)
        for t in both:
            self.rounds_done(t)
        for t in both:
            self.copy_out(t).wait()
        for group in self.groups:
            group.finish()

    def pack(self, t):
        pk, qkv, out, fc = t.pk, t.qkv, t.out, t.fc
        d, b = t.width, t.block
        pad = t.row_pad - t.rows

        def padded(values):
            values = values.astype(F32)
            if pad:
                values = jnp.concatenate([values, jnp.zeros((pad, values.shape[1]), F32)], 0)
            return values.astype(BF16)

        pk[0, :, 0:d] = padded(qkv[:, 0:d])
        pk[1, :, 0:d] = padded(qkv[:, d : 2 * d])
        pk[0, :, d : 2 * d] = padded(qkv[:, 2 * d : 3 * d])
        pk[1, :, d : 2 * d] = padded(out[...])
        if t.extra:
            for half in range(2):
                cols = slice(half * t.extra, (half + 1) * t.extra)
                pk[half, :, 2 * d : 2 * d + t.extra] = padded(self.map[:, cols])
        base = 2 * d + t.extra
        values = padded(fc[...]).astype(F32)
        for half in range(2):
            for group in range(4):
                pieces = []
                for copy in range(4):
                    device = t.device_of(group, copy, half)
                    pieces.append(values[:, b * device : b * (device + 1)])
                start = base + group * t.group
                pk[half, :, start : start + t.group] = jnp.concatenate(pieces, 1).astype(BF16)

    def pack_vectors(self):
        def widen(values, at):
            values = values.astype(F32)
            parts = [values, jnp.zeros((values.shape[0], 128 - at - values.shape[1]), F32)]
            if at:
                parts = [jnp.zeros((values.shape[0], at), F32)] + parts
            return jnp.concatenate(parts, 1)

        top = widen(self.ti.vec[...], 0) + widen(self.tt.vec[...], 32)
        row = iota((8, 128), 0)
        bottom = jnp.where(row == 0, widen(self.ti.fcb[...], 0), 0.0)
        bottom = bottom + jnp.where(row == 1, widen(self.tt.fcb[...], 0), 0.0)
        block = jnp.concatenate([top, bottom], 0)
        row, lane = iota((PAD, 128), 0), iota((PAD, 128), 1)
        for caption in range(self.images):
            image = self.match[caption]
            device = image // self.images
            high = lax.rem(device, 2) * 16 + device // 2
            low = image - device * self.images
            block = jnp.where((row == caption) & (lane == 120), high.astype(F32), block)
            block = jnp.where((row == caption) & (lane == 121), low.astype(F32), block)
        self.vb[self.core, self.chip] = block.astype(BF16)

    def unpack_vectors(self):
        vb = self.vb
        for core in range(2):
            for chip in range(16):
                block = vb[core, chip].astype(F32)
                device = 2 * chip + core
                for t, at in ((self.ti, 0), (self.tt, 32)):
                    rows = t.rows
                    t.vecs[:, rows * device : rows * (device + 1)] = block[0:8, at : at + rows]
        for t, row in ((self.ti, 8), (self.tt, 9)):
            for copy in range(4):
                block = vb[self.core, t.chip_of(t.g, copy)].astype(F32)
                b = t.block
                t.bias[0:1, b * copy : b * (copy + 1)] = block[row : row + 1, 0:b]

    def standardize(self, t):
        x, xp, xh, inv = t.x, t.xp, t.xh, t.inv
        step = STEP_ROWS
        full = t.real_tokens // step

        def norm(hidden, rows):
            xp[rows, :] = hidden.astype(BF16)
            centred = hidden - jnp.mean(hidden, -1, keepdims=True)
            inverse = lax.rsqrt(jnp.mean(centred * centred, -1, keepdims=True) + 1e-05)
            xh[rows, :] = centred * inverse
            inv[rows, :] = jnp.broadcast_to(inverse, (step, 128))

        def body(index, carry):
            rows = pl.ds(pl.multiple_of(index * step, step), step)
            norm(x[rows, :].astype(F32), rows)
            return carry

        lax.fori_loop(0, full, body, 0)
        start, rest = full * step, t.real_tokens - full * step
        if rest:
            last = x[start : t.real_tokens, :].astype(F32)
            last = jnp.concatenate([last, jnp.zeros((step - rest, t.width), F32)], 0)
            norm(last, slice(start, start + step))
            start += step
        while start < t.tokens:
            norm(jnp.zeros((step, t.width), F32), slice(start, start + step))
            start += step

    def merge(self, t):
        t.pair.wait(t.pr)
        pk, pr = t.pk, t.pr
        d, g = t.width, t.group
        rows = pl.ds(pl.multiple_of(self.chip * t.chip_rows, 16), t.chip_rows)
        first = self.core == 0

        def merged(cols):
            own = pk[self.core, :, cols].astype(F32)
            got = pr[:, cols].astype(F32)
            upper = jnp.where(first, own, got)[: t.rows]
            lower = jnp.where(first, got, own)[: t.rows]
            return jnp.concatenate([upper, lower], 0).astype(BF16)

        t.w1[self.core, rows, :] = merged(slice(0, d))
        t.w2[self.core, rows, :] = merged(slice(d, 2 * d))
        base = 2 * d
        if t.extra:
            self.w3[self.core, rows, :] = merged(slice(base, base + t.extra))
            base += t.extra
        for group in range(4):
            t.mf[group] = merged(slice(base + group * g, base + (group + 1) * g))

    def widen_begin(self, t):
        t.widen = Group(self)
        for mask in t.group_peers:
            t.widen.send(t.mf.at[t.group_of(self.at_peer(mask))], t.fa.at[self.zed, self.plane], mask)
        t.fa[self.zed, self.plane] = t.mf[t.g]

    def widen_middle(self, t):
        t.widen.wait(t.mf.at[0:3])
        t.widen, t.narrow = Group(self), Group(self)
        part = t.chips_of_copy(t.fa, t.r)
        for mask in t.copy_peers:
            t.widen.send(part, part, mask)
        for mask in t.copy_peers:
            t.narrow.send(t.proj, t.wp.at[t.r], mask)
        t.wp[t.r] = t.proj[...]

    def queries(self, t):
        a, xh, vec = t.a, t.xh, t.vecs
        step = STEP_ROWS

        def body(index, carry):
            rows = pl.ds(pl.multiple_of(index * step, step), step)
            a[rows, :] = (xh[rows, :] * vec[0:1, :] + vec[1:2, :]).astype(BF16)
            return carry

        lax.fori_loop(0, t.tokens // step, body, 0)
        n = t.tokens
        row, token = iota((PAD, n), 0), iota((PAD, n), 1)
        if t is self.ti:
            real = row < self.images
            at = jnp.where(real, row * TOK_I, -1)
            low, high = jnp.where(real, row * TOK_I, -1), jnp.where(real, (row + 1) * TOK_I, -1)
        else:
            counts = self.counts
            column = iota((PAD, 1), 0)
            low, high = jnp.full((PAD, 1), -1, jnp.int32), jnp.full((PAD, 1), -1, jnp.int32)
            for line in range(counts.shape[0]):
                end = line * TOK_T
                for member in range(CAP_ROW):
                    begin, end = end, end + counts[line, member]
                    chosen = column == line * CAP_ROW + member
                    low, high = jnp.where(chosen, begin, low), jnp.where(chosen, end, high)
            at = jnp.where(high > 0, high - 1, -1)
        chosen = (token == at).astype(F32).astype(BF16)
        lh, r = t.lh, t.queries
        lh[2 * r : 2 * r + PAD, :] = chosen
        lh[2 * r + PAD : 2 * r + 2 * PAD, :] = chosen
        t.seen = ((token >= low) & (token < high)).astype(F32)
        t.x0 = dot(chosen, t.xp[...])
        t.a0 = dot(chosen, a[...]).astype(BF16)

    def attend(self, t):
        w1, vec, a, r = t.w1, t.vecs, t.a, t.queries
        t.q = (dot(t.a0, w1[0]) + vec[2:3, :]).astype(BF16)
        qt = dot_nt(expand_heads(t.q), w1[1]).astype(BF16)
        t.rh[0:r, :] = qt
        scores = dot_nt(qt, a[...]) * 0.125
        seen = jnp.concatenate([t.seen] * t.heads, 0) > 0.5
        scores = jnp.where(seen, scores, -1000000000.0)
        top = jnp.max(scores, -1, keepdims=True)
        raw = jnp.where(seen, jnp.exp(scores - top), 0.0)
        total = jnp.sum(raw, -1, keepdims=True)
        probs = raw / jnp.where(total > 0.0, total, 1.0)
        t.p32[...] = probs
        low = probs.astype(BF16)
        t.lh[r : 2 * r, :] = low
        t.pa = dot(low, a[...])

    def mix(self, t):
        w2, vec = t.w2, t.vecs
        context = (join_heads(dot(t.pa.astype(BF16), w2[0])) + vec[3:4, :]).astype(BF16)
        t.o = context
        t.h1 = t.x0 + (dot(context, w2[1]) + vec[4:5, :])
        t.xh2, t.inv2, second = small_norm(t.h1, vec[5:6, :], vec[6:7, :])
        t.ci[t.spot] = second.astype(BF16)
        t.line = self.line_gather(t, t.ci)

    def feed(self, t):
        d, g = t.width, t.group
        t.widen.wait(t.fa.at[0:3])
        t.narrow.wait(t.wp.at[0:3])
        t.line.wait(t.ci.at[0:7])
        c = t.ci[...].reshape(8 * PAD, d)
        up = dot(c, t.fa[...].reshape(d, g)) + t.bias[0:1, :]
        active = (up * jax.nn.sigmoid(1.702 * up)).astype(BF16)
        t.u[...] = up
        t.m[...] = active
        part = dot(active, t.wp[...].reshape(g, d)).reshape(8, PAD, d)
        t.hpf[...] = part
        t.hps[...] = part.astype(BF16)
        t.line = self.line_scatter(t, t.hps, t.hr)

    def line_total(self, t, own, landing):
        t.line.wait(landing)
        total = own[t.spot]
        for slot in range(7):
            total = total + landing[slot].astype(F32)
        return total

    def embed(self, t):
        hidden = t.h1 + (self.line_total(t, t.hpf, t.hr) + t.vecs[7:8, :])
        which = 1
        raw = hidden
        if t is self.ti:
            which = 0
            self.pooled = hidden.astype(BF16)
            raw = jnp.concatenate([dot(self.pooled, self.w3[0]), dot(self.pooled, self.w3[1])], 1)
        scale = lax.rsqrt(jnp.sum(raw * raw, -1, keepdims=True) + 1e-06)
        self.eb[which, self.core, self.chip] = (raw * scale).astype(BF16)
        t.sc[t.spot] = jnp.broadcast_to(scale, (PAD, 128))

    def early_operands(self, t):
        d, r = t.width, t.queries
        parts = [t.pa, t.o.astype(F32), t.a0.astype(F32)]
        if t is self.ti:
            parts.append(self.pooled.astype(F32))
        rest = 256 - r - PAD * (len(parts) - 1)
        parts.append(jnp.zeros((rest, d), F32))
        t.in1t[...] = jnp.concatenate(parts, 0).T.astype(BF16).reshape(4, 4, t.chip_rows, 256)
        t.c_in1 = self.to_group(t, t.in1t, t.in1r)
        t.c_q = self.share_group(t, t.qg, t.q)

    def contrast(self):
        eb, gtxt, gimg = self.eb, self.gtxt, self.gimg
        size = 32 * PAD
        total = self.images * 32
        e_img, e_txt = eb[0].reshape(size, eb.shape[-1]), eb[1].reshape(size, eb.shape[-1])
        sharp = jnp.exp(jnp.full((8, 128), self.sharp[0], F32))[0:1, 0:1]
        logits = sharp * dot_nt(e_txt, e_img)
        marks = self.vb[...].reshape(size, 128).astype(F32)
        target = marks[:, 120:121] * float(PAD) + marks[:, 121:122]
        row, col = iota((size, size), 0), iota((size, size), 1)
        real = (lax.rem(row, PAD) < self.images) & (lax.rem(col, PAD) < self.images)
        hit = real & (col.astype(F32) == target)
        powers = jnp.where(real, jnp.exp(logits), 0.0)
        row_sum, col_sums = jnp.sum(powers, 1, keepdims=True), col_sum(powers)
        real_line = lax.rem(iota((size, 1), 0), PAD) < self.images
        real_lane = lax.rem(iota((1, size), 1), PAD) < self.images
        row_sum, col_sums = jnp.where(real_line, row_sum, 1.0), jnp.where(real_lane, col_sums, 1.0)
        grad = powers * ((1.0 / row_sum + 1.0 / col_sums) * (0.5 / total))
        grad = grad - jnp.where(hit, 1.0 / total, 0.0)
        safe = jnp.where(real, logits, 0.0)
        logs = jnp.sum(jnp.log(row_sum), 0, keepdims=True) + jnp.sum(jnp.log(col_sums), 1, keepdims=True)

        def whole(values):
            return jnp.sum(jnp.sum(values, 1, keepdims=True), 0, keepdims=True)

        self.loss[...] = logs * (0.5 / total) - whole(jnp.where(hit, safe, 0.0)) * (1.0 / total)
        self.dls[...] = whole(grad * safe)
        gtxt[...] = grad
        gimg[...] = grad.T
        for which, t, rows, others in ((0, self.ti, gimg, e_txt), (1, self.tt, gtxt, e_img)):
            parts, own = [], []
            for core in range(2):
                for group in range(4):
                    chip = t.chip_of(group, t.r)
                    start = pl.multiple_of((core * 16 + chip) * PAD, PAD)
                    parts.append(rows[pl.ds(start, PAD), :])
                    own.append(eb[which, core, chip].astype(F32))
            part, unit = jnp.concatenate(parts, 0), jnp.concatenate(own, 0)
            scale = t.sc[...].reshape(8 * PAD, 128)[:, 0:1]
            high, low = split_two(part)
            d_unit = sharp * (dot(high, others) + dot(low, others))
            d_raw = scale * (d_unit - unit * jnp.sum(d_unit * unit, -1, keepdims=True))
            if t is self.ti:
                w3, half = self.w3, t.extra
                rounded = d_raw.astype(BF16)
                self.drb[...] = rounded.reshape(self.drb.shape)
                d_raw = dot_nt(rounded[:, 0:half], w3[0]) + dot_nt(rounded[:, half : 2 * half], w3[1])
            t.g2[...] = d_raw.reshape(t.g2.shape)

    def feed_back(self, t):
        d, g = t.width, t.group
        t.y = t.g2[...].reshape(8 * PAD, d).astype(BF16)
        up = t.u[...]
        gate = jax.nn.sigmoid(1.702 * up)
        d_active = dot_nt(t.y, t.wp[...].reshape(g, d))
        t.du = (d_active * (gate + 1.702 * up * gate * (1.0 - gate))).astype(BF16)
        part = dot_nt(t.du, t.fa[...].reshape(d, g)).reshape(8, PAD, d)
        t.dcf[...] = part
        t.dcs[...] = part.astype(BF16)
        t.line = self.line_scatter(t, t.dcs, t.dcr)

    def feed_weights(self, t):
        d, g, b, cr = t.width, t.group, t.block, t.chip_rows
        grad = dot_tn(t.ci[...].reshape(8 * PAD, d), t.du).reshape(4, 4, cr, g)
        t.gff[...] = grad
        t.gfb[...] = grad.astype(BF16)
        t.c_wide, t.c_narrow, t.c_bias = Group(self), Group(self), Group(self)
        for slot, mask in enumerate(t.copy_peers):
            t.c_wide.send(t.chips_of_copy(t.gfb, t.copy_of(self.at_peer(mask))), t.gfr.at[slot], mask)
        grad = dot_tn(t.m[...], t.y).reshape(4, b, d)
        t.gpf[...] = grad
        t.gpb[...] = grad.astype(BF16)
        t.dbs[...] = jnp.broadcast_to(col_sum(t.du.astype(F32)), (8, g))
        for slot, mask in enumerate(t.copy_peers):
            t.c_narrow.send(t.gpb.at[t.copy_of(self.at_peer(mask))], t.gpr.at[slot], mask)
            t.c_bias.send(t.dbs, t.dbr.at[slot], mask)

    def feed_weights_middle(self, t):
        b = t.block
        t.c_wide.wait(t.gfr)
        total = t.chips_of_copy(t.gff, t.r)[...]
        for slot in range(3):
            total = total + t.gfr[slot].astype(F32)
        t.gf2[...] = total.astype(BF16)
        t.gf3[...] = total
        t.c_line = Group(self)
        for mask in t.group_peers:
            t.c_line.send(t.gf2.at[t.group_of(self.at_peer(mask))], t.gf3r.at[t.g], mask)
        t.c_narrow.wait(t.gpr)
        total = t.gpf[t.r]
        for slot in range(3):
            total = total + t.gpr[slot].astype(F32)
        t.d_proj[...] = total
        t.c_bias.wait(t.dbr)
        bias = t.dbs[0:1, :]
        for slot in range(3):
            bias = bias + t.dbr[slot, 0:1, :]
        mine = jnp.zeros((1, b), F32)
        for copy in range(4):
            mine = jnp.where(t.r == copy, bias[:, b * copy : b * (copy + 1)], mine)
        t.d_fcb[...] = mine

    def feed_weights_end(self, t):
        t.c_line.wait(t.gf2.at[0:3])
        own = t.gf3[t.g]
        for group in range(4):
            t.gf3[group] = jnp.where(t.g == group, own, t.gf3r[group].astype(F32))
        start = pl.multiple_of((1 - self.core) * t.rows, 8)
        t.c_fc = Group(self)
        t.c_fc.send(t.gf3.at[:, pl.ds(start, t.rows)], t.gf4, 1)

    def attend_back(self, t):
        vec = t.vecs
        total = self.line_total(t, t.dcf, t.dcr)
        g2 = t.g2[t.spot]
        t.g1 = g2 + small_norm_back(total, t.xh2, t.inv2, vec[5:6, :])
        branch = t.g1.astype(BF16)
        t.do = dot_nt(branch, t.w2[1]).astype(BF16)
        t.sums.update(
            dbv=col_sum(t.do.astype(F32)),
            dbo=col_sum(branch.astype(F32)),
            dg2=col_sum(total * t.xh2),
            db2=col_sum(total),
            dbp=col_sum(g2.astype(BF16).astype(F32)),
        )
        t.c_w = self.share_group(t, t.wg, branch)
        t.c_do = self.share_group(t, t.dog, t.do)

    def attend_back_end(self, t):
        r, w1, a, lh, rh = t.queries, t.w1, t.a, t.lh, t.rh
        dvt = dot_nt(expand_heads(t.do), t.w2[0]).astype(BF16)
        rh[r : 2 * r, :] = dvt
        d_probs = dot_nt(dvt, a[...])
        probs = t.p32[...]
        weighted = probs * d_probs
        d_scores = (weighted - probs * jnp.sum(weighted, -1, keepdims=True)).astype(BF16)
        d_scores = (d_scores.astype(F32) * 0.125).astype(BF16)
        lh[0:r, :] = d_scores
        moved = dot(d_scores, a[...])
        t.in2t[...] = moved.T.astype(BF16).reshape(t.in2t.shape)
        t.c_in2 = self.to_group(t, t.in2t, t.in2r)
        d_query = join_heads(dot(moved.astype(BF16), w1[1])).astype(BF16)
        t.c_dq = self.share_group(t, t.dqg, d_query)
        t.sums.update(dbq=col_sum(d_query.astype(F32)))
        high, low = split_two(dot_nt(d_query, w1[0]))
        rh[2 * r : 2 * r + PAD, :] = high
        rh[2 * r + PAD : 2 * r + 2 * PAD, :] = low

    def copy_out(self, t):
        return pltpu.make_async_copy(t.dxs, t.d_x, self.osem.at[0 if t is self.ti else 1])

    def input_gradient(self, t):
        r, d = t.queries, t.width
        lh, da, gp, xh, inv, vec, out = t.lh, t.da, t.gp, t.xh, t.inv, t.vecs, t.dxs
        da[...] = dot_tn(lh[...], t.rh[...])
        high, low = split_two(t.g1)
        gp[...] = dot_tn(lh[2 * r : 2 * r + 2 * PAD, :], jnp.concatenate([high, low], 0))
        step = STEP_ROWS
        full = t.real_tokens // step

        def one(rows, carry):
            z, normed = da[rows, :], xh[rows, :]
            inner = small_norm_back(z, normed, inv[rows, 0:1], vec[0:1, :])
            return inner + gp[rows, :], (
                carry[0] + jnp.sum((z * normed).reshape(step // 8, 8, d), 0),
                carry[1] + jnp.sum(z.reshape(step // 8, 8, d), 0),
            )

        def body(index, carry):
            rows = pl.ds(pl.multiple_of(index * step, step), step)
            out[rows, :], carry = one(rows, carry)
            return carry

        zero = jnp.zeros((8, d), F32)
        carry = lax.fori_loop(0, full, body, (zero, zero))
        start, rest = full * step, t.real_tokens - full * step
        if rest:
            last, carry = one(slice(start, start + step), carry)
            out[start : start + rest, :] = last[:rest]
        self.copy_out(t).start()
        s = t.sums
        rows = [col_sum(carry[0]), col_sum(carry[1])]
        rows += [s.pop(name) for name in list(dict(dbq=0, dbv=0, dbo=0, dg2=0, db2=0, dbp=0))]
        t.vector_rows = jnp.concatenate(rows, 0)

    def vector_sum_begin(self):
        self.vz[...] = jnp.concatenate([self.ti.vector_rows, self.tt.vector_rows], 1)
        group = Group(self)
        for slot, mask in enumerate(Z_PEERS):
            group.send(self.vz, self.vzr.at[slot], mask)
        return group

    def vector_sum_middle(self, group):
        group.wait(self.vzr)
        self.vp[...] = self.vz[...] + self.vzr[0] + self.vzr[1] + self.vzr[2]
        group = Group(self)
        for slot, mask in enumerate(PLANE_PEERS):
            group.send(self.vp, self.vpr.at[slot], mask)
        return group

    def vector_sum_end(self, group):
        group.wait(self.vpr)
        self.vc[...] = self.vp[...] + self.vpr[0] + self.vpr[1] + self.vpr[2]
        group = Group(self)
        group.send(self.vc, self.vcr, 1)
        return group

    def vector_sum_done(self, group):
        group.wait(self.vcr)
        total = self.vc[...] + self.vcr[...]
        at = 0
        for t in (self.ti, self.tt):
            d, rows = t.width, t.rows
            values = total[:, at : at + d]
            at += d
            high, rest = split_two(values)
            rest_high, rest_low = split_two(values - high.astype(F32))
            pick = iota((d, 128), 0) == iota((d, 128), 1) + self.me * rows
            pick = pick.astype(F32).astype(BF16)
            picked = dot(high, pick) + dot(rest_high, pick) + dot(rest_low, pick)
            t.d_vec[...] = picked[:, 0:rows]

    def place(self, rows, at):
        parts = []
        if at:
            parts.append(jnp.zeros((at, rows.shape[1]), BF16))
        parts.append(rows)
        if 256 - at - rows.shape[0]:
            parts.append(jnp.zeros((256 - at - rows.shape[0], rows.shape[1]), BF16))
        return jnp.concatenate(parts, 0)

    def round_one(self, t):
        r = t.queries
        t.c_in1.wait(t.in1r.at[0:3])
        t.c_w.wait(t.wg.at[0:3])
        t.c_do.wait(t.dog.at[0:3])
        value = out = proj = 0.0
        for group in range(4):
            operand = t.in1r[group].reshape(4 * t.chip_rows, 256)
            value = value + dot(operand, self.place(expand_heads(t.dog[group]), 0))
            out = out + dot(operand, self.place(t.wg[group], r))
            if t.extra:
                proj = proj + dot(operand, self.place(self.drb[self.core * 4 + group], r + 2 * PAD))
        parts = [value, out] + ([proj] if t.extra else [])
        grad = jnp.concatenate(parts, 1).reshape(t.r1f.shape)
        t.r1f[...] = grad
        t.r1b[...] = grad.astype(BF16)
        t.c_r1 = self.to_copies(t, t.r1b, t.r1r)

    def round_two(self, t):
        r = t.queries
        t.c_q.wait(t.qg.at[0:3])
        t.c_in2.wait(t.in2r.at[0:3])
        t.c_dq.wait(t.dqg.at[0:3])
        query = key = 0.0
        for group in range(4):
            operand = t.in1r[group].reshape(4 * t.chip_rows, 256)
            query = query + dot(operand, self.place(t.dqg[group], r + PAD))
            key = key + dot(t.in2r[group].reshape(4 * t.chip_rows, r), expand_heads(t.qg[group]))
        grad = jnp.concatenate([query, key], 1).reshape(t.r2f.shape)
        t.r2f[...] = grad
        t.r2b[...] = grad.astype(BF16)
        t.c_r2 = self.to_copies(t, t.r2b, t.r2r)

    def rounds_end(self, t):
        start = pl.multiple_of((1 - self.core) * t.rows, 8)
        t.c_last = []
        for group, f, landing, total, last in (
            (t.c_r1, t.r1f, t.r1r, t.r1s, t.r1p),
            (t.c_r2, t.r2f, t.r2r, t.r2s, t.r2p),
        ):
            group.wait(landing)
            values = f[t.r]
            for slot in range(3):
                values = values + landing[slot].astype(F32)
            total[...] = values
            pair = Group(self)
            pair.send(total.at[pl.ds(start, t.rows)], last, 1)
            t.c_last.append(pair)

    def rounds_done(self, t):
        rows, d, b = t.rows, t.width, t.block
        start = pl.multiple_of(self.core * rows, 8)
        done = []
        for pair, total, last in zip(t.c_last, (t.r1s, t.r2s), (t.r1p, t.r2p), strict=True):
            pair.wait(last)
            done.append(total[pl.ds(start, rows), :] + last[...])
        t.d_qkv[:, 0 : 2 * d] = done[1]
        t.d_qkv[:, 2 * d : 3 * d] = done[0][:, 0:d]
        t.d_out[...] = done[0][:, d : 2 * d]
        if t.extra:
            self.dmap[...] = done[0][:, 2 * d :]
        t.c_fc.wait(t.gf4)
        for group in range(4):
            own, got = t.gf3[group, pl.ds(start, rows), :], t.gf4[group]
            for half in range(2):
                values = jnp.where(self.core == half, own, got)
                for copy in range(4):
                    device = t.device_of(group, copy, half)
                    t.d_fc[:, b * device : b * (device + 1)] = values[:, b * copy : b * (copy + 1)]


def set_all(target, names, refs):
    for name, ref in zip(names, refs, strict=True):
        setattr(target, name, ref)


def hand_over(results):
    count = len(results)

    def kernel(*refs):
        came, went = refs[3 * count], refs[3 * count + 1]
        reads = [
            pltpu.make_async_copy(refs[index], refs[2 * count + index], came.at[index])
            for index in range(count)
        ]
        writes = [
            pltpu.make_async_copy(refs[2 * count + index], refs[count + index], went.at[index])
            for index in range(count)
        ]
        for read in reads:
            read.start()
        for read, write in zip(reads, writes, strict=True):
            read.wait()
            write.start()
        for write in writes:
            write.wait()

    sems = pltpu.SemaphoreType.DMA((count,))
    return pl.pallas_call(
        kernel,
        out_shape=tuple(jax.ShapeDtypeStruct(value.shape, value.dtype) for value in results),
        in_specs=[pl.BlockSpec(memory_space=pl.ANY)] * count,
        out_specs=tuple([pl.BlockSpec(memory_space=pl.ANY)] * count),
        scratch_shapes=[pltpu.VMEM(value.shape, value.dtype) for value in results] + [sems, sems],
        compiler_params=pltpu.CompilerParams(vmem_limit_bytes=60 * 2**20),
        name="hand_over",
    )(*results)


def local_fused(
    picture_patch_inputs,
    caption_packed_inputs,
    picture_attend_entry_weight,
    picture_attend_exit_weight,
    picture_widening_weight,
    picture_narrowing_weight,
    picture_affine_entries,
    picture_widening_offset,
    caption_attend_entry_weight,
    caption_attend_exit_weight,
    caption_widening_weight,
    caption_narrowing_weight,
    caption_affine_entries,
    caption_widening_offset,
    picture_feature_mapping,
    sharpness_exponent,
    caption_token_counts,
    matching_picture_index,
):
    n_img, d_img = picture_patch_inputs.shape
    n_txt, d_txt = caption_packed_inputs.shape
    images = n_img // TOK_I
    ti = Tower(
        True,
        d_img,
        n_img,
        picture_attend_entry_weight.shape[1],
        picture_widening_offset.shape[1],
        picture_feature_mapping.shape[1] // 2,
    )
    tt = Tower(
        False, d_txt, n_txt, caption_attend_entry_weight.shape[1], caption_widening_offset.shape[1], 0
    )
    img_args = dict(
        x=picture_patch_inputs,
        qkv=picture_attend_entry_weight[0],
        out=picture_attend_exit_weight[0],
        fc=picture_widening_weight[0],
        proj=picture_narrowing_weight[0],
        vec=picture_affine_entries[0],
        fcb=picture_widening_offset,
    )
    txt_args = dict(
        x=caption_packed_inputs,
        qkv=caption_attend_entry_weight[0],
        out=caption_attend_exit_weight[0],
        fc=caption_widening_weight[0],
        proj=caption_narrowing_weight[0],
        vec=caption_affine_entries[0],
        fcb=caption_widening_offset,
    )
    more_args = dict(
        map=picture_feature_mapping,
        sharp=sharpness_exponent.reshape(1),
        counts=caption_token_counts,
        match=matching_picture_index,
    )

    def out(*shape):
        return jax.ShapeDtypeStruct(shape, F32)

    def tower_outs(t):
        return dict(
            d_x=out(t.real_tokens, t.width),
            d_qkv=out(t.rows, 3 * t.width),
            d_out=out(t.rows, t.width),
            d_fc=out(t.rows, 32 * t.block),
            d_proj=out(t.block, t.width),
            d_vec=out(8, t.rows),
            d_fcb=out(1, t.block),
        )

    more_outs = dict(loss=out(1, 1), dls=out(1, 1), dmap=out(ti.rows, 2 * ti.extra))
    in_vmem, in_smem = pl.BlockSpec(memory_space=pltpu.VMEM), pl.BlockSpec(memory_space=pltpu.SMEM)
    anywhere = pl.BlockSpec(memory_space=pl.ANY)
    parts = [
        (ti, img_args, [in_vmem] * 7),
        (tt, txt_args, [in_vmem] * 7),
        (None, more_args, [in_vmem, in_smem, in_smem, in_smem]),
        (ti, tower_outs(ti), [anywhere] + [in_vmem] * 6),
        (tt, tower_outs(tt), [anywhere] + [in_vmem] * 6),
        (None, more_outs, [in_vmem] * 3),
        (ti, ti.scratch(), None),
        (tt, tt.scratch(), None),
        (None, shared_scratch(ti, tt), None),
        (
            None,
            dict(
                ssem=pltpu.SemaphoreType.DMA((N_SEMS,)),
                rsem=pltpu.SemaphoreType.DMA((N_SEMS,)),
                osem=pltpu.SemaphoreType.DMA((2,)),
            ),
            None,
        ),
    ]

    def kernel(*refs):
        step = Step(ti, tt, images)
        at = 0
        for owner, values, _ in parts:
            set_all(step if owner is None else owner, values, refs[at : at + len(values)])
            at += len(values)
        step.run()

    def joined(chosen, field):
        return [item for part in chosen for item in (part[field] if field == 2 else part[field].values())]

    results = pl.pallas_call(
        kernel,
        out_shape=tuple(joined(parts[3:6], 1)),
        in_specs=joined(parts[0:3], 2),
        out_specs=tuple(joined(parts[3:6], 2)),
        scratch_shapes=joined(parts[6:], 1),
        compiler_params=pltpu.CompilerParams(
            collective_id=0, has_side_effects=True, vmem_limit_bytes=60 * 2**20
        ),
        name="contrastive_step",
    )(*joined(parts[0:3], 1))
    results = hand_over(results)
    img, txt, (loss, d_scale, d_map) = results[0:7], results[7:14], results[14:17]
    return (
        loss.reshape(()),
        d_scale.reshape(()),
        img[0],
        txt[0],
        img[1][None],
        img[2][None],
        img[3][None],
        img[4][None],
        img[5][None],
        img[6],
        txt[1][None],
        txt[2][None],
        txt[3][None],
        txt[4][None],
        txt[5][None],
        txt[6],
        d_map,
    )


def solution(mesh):
    placed = (
        P("dp", None),
        P("dp", None),
        P(None, "dp", None),
        P(None, "dp", None),
        P(None, "dp", None),
        P(None, "dp", None),
        P(None, None, "dp"),
        P(None, "dp"),
        P(None, "dp", None),
        P(None, "dp", None),
        P(None, "dp", None),
        P(None, "dp", None),
        P(None, None, "dp"),
        P(None, "dp"),
        P("dp", None),
        P(),
        P("dp", None),
        P("dp"),
    )
    return jax.shard_map(
        local_fused if fits(mesh) else local_plain,
        mesh=mesh,
        in_specs=placed,
        out_specs=(
            P(),
            P(),
            P("dp", None),
            P("dp", None),
            P(None, "dp", None),
            P(None, "dp", None),
            P(None, "dp", None),
            P(None, "dp", None),
            P(None, None, "dp"),
            P(None, "dp"),
            P(None, "dp", None),
            P(None, "dp", None),
            P(None, "dp", None),
            P(None, "dp", None),
            P(None, None, "dp"),
            P(None, "dp"),
            P("dp", None),
        ),
        check_vma=False,
    )
```

```python
import jax
import jax.numpy as jnp
from jax import lax
from jax.experimental import pallas as pl
from jax.experimental.pallas import tpu as pltpu
from jax.sharding import PartitionSpec as P

HD = 64
TOK_I = 50
TOK_T = 77
CAP_ROW = 4


def norm_forward(hidden, norm_gain, norm_shift):
    row_mean = jnp.mean(hidden, -1, keepdims=True)
    centred = hidden - row_mean
    inverse = lax.rsqrt(jnp.mean(centred * centred, -1, keepdims=True) + 1e-05)
    normed = centred * inverse
    return (normed, inverse, normed * norm_gain + norm_shift)


def norm_backward(upstream, normed, inverse, norm_gain):
    scaled = upstream * norm_gain
    inner_sum = (
        scaled
        - jnp.mean(scaled, -1, keepdims=True)
        - normed * jnp.mean(scaled * normed, -1, keepdims=True)
    )
    return (inverse * inner_sum, jnp.sum(upstream * normed, (0, 1)), jnp.sum(upstream, (0, 1)))


def split_heads(values):
    return values.reshape(values.shape[0], values.shape[1], values.shape[2] // HD, HD)


def attention_scores(queries, key_heads, allowed):
    scores = (
        jnp.einsum("sqhd,skhd->shqk", queries, key_heads, preferred_element_type=jnp.float32)
        * 0.125
    )
    return jnp.where(allowed[:, None], scores, -1000000000.0)


def block_forward(hidden, weights, allowed):
    w_qkv, w_out, w_fc, w_proj, vectors, fc_bias = weights
    vectors = vectors.astype(jnp.float32)
    fc_bias = fc_bias.astype(jnp.float32)
    feature_width = hidden.shape[-1]
    normed_first, inverse_first, first = norm_forward(hidden, vectors[0], vectors[1])
    first_low = first.astype(jnp.bfloat16)
    projected = jnp.einsum("std,de->ste", first_low, w_qkv, preferred_element_type=jnp.float32)
    queries = (projected[..., :feature_width] + vectors[2]).astype(jnp.bfloat16)
    key_heads = projected[..., feature_width : 2 * feature_width].astype(jnp.bfloat16)
    values = (projected[..., 2 * feature_width :] + vectors[3]).astype(jnp.bfloat16)
    scores = attention_scores(split_heads(queries), split_heads(key_heads), allowed)
    totals = jax.nn.logsumexp(scores, -1, keepdims=True)
    attn_probs = jnp.exp(scores - totals).astype(jnp.bfloat16)
    context = jnp.einsum(
        "shqk,skhd->sqhd", attn_probs, split_heads(values), preferred_element_type=jnp.float32
    )
    context = context.reshape(hidden.shape).astype(jnp.bfloat16)
    middle = hidden + (
        jnp.einsum("std,de->ste", context, w_out, preferred_element_type=jnp.float32) + vectors[4]
    )
    normed_second, inverse_second, second = norm_forward(middle, vectors[5], vectors[6])
    second_low = second.astype(jnp.bfloat16)
    upward = (
        jnp.einsum("std,df->stf", second_low, w_fc, preferred_element_type=jnp.float32) + fc_bias
    )
    activated = (upward * jax.nn.sigmoid(1.702 * upward)).astype(jnp.bfloat16)
    output = middle + (
        jnp.einsum("stf,fd->std", activated, w_proj, preferred_element_type=jnp.float32)
        + vectors[7]
    )
    stored = (
        normed_first,
        inverse_first,
        first_low,
        queries,
        key_heads,
        values,
        totals,
        context,
        normed_second,
        inverse_second,
        second_low,
        upward,
        activated,
    )
    return (output, stored)


def block_backward(upstream, weights, stored, allowed):
    w_qkv, w_out, w_fc, w_proj, vectors, fc_bias = weights
    vectors = vectors.astype(jnp.float32)
    (
        normed_first,
        inverse_first,
        first_low,
        queries,
        key_heads,
        values,
        totals,
        context,
        normed_second,
        inverse_second,
        second_low,
        upward,
        activated,
    ) = stored
    feature_width = queries.shape[-1]
    branch = upstream.astype(jnp.bfloat16)
    d_proj_bias = jnp.sum(branch.astype(jnp.float32), (0, 1))
    d_w_proj = jnp.einsum("stf,std->fd", activated, branch, preferred_element_type=jnp.float32)
    d_activated = jnp.einsum("std,fd->stf", branch, w_proj, preferred_element_type=jnp.float32)
    sigmoid_up = jax.nn.sigmoid(1.702 * upward)
    d_upward = (
        d_activated * (sigmoid_up + 1.702 * upward * sigmoid_up * (1.0 - sigmoid_up))
    ).astype(jnp.bfloat16)
    d_fc_bias = jnp.sum(d_upward.astype(jnp.float32), (0, 1))
    d_w_fc = jnp.einsum("std,stf->df", second_low, d_upward, preferred_element_type=jnp.float32)
    d_second = jnp.einsum("stf,df->std", d_upward, w_fc, preferred_element_type=jnp.float32)
    d_middle_norm, d_gain_second, d_shift_second = norm_backward(
        d_second, normed_second, inverse_second, vectors[5]
    )
    d_middle = upstream + d_middle_norm
    attn_branch = d_middle.astype(jnp.bfloat16)
    d_out_bias = jnp.sum(attn_branch.astype(jnp.float32), (0, 1))
    d_w_out = jnp.einsum("std,ste->de", context, attn_branch, preferred_element_type=jnp.float32)
    d_context = jnp.einsum("ste,de->std", attn_branch, w_out, preferred_element_type=jnp.float32)
    d_context = split_heads(d_context.astype(jnp.bfloat16))
    query_heads = split_heads(queries)
    key_split = split_heads(key_heads)
    scores = attention_scores(query_heads, key_split, allowed)
    attn_probs = jnp.exp(scores - totals)
    d_probs = jnp.einsum(
        "sqhd,skhd->shqk", d_context, split_heads(values), preferred_element_type=jnp.float32
    )
    d_scores = (attn_probs * (d_probs - jnp.sum(attn_probs * d_probs, -1, keepdims=True))).astype(
        jnp.bfloat16
    )
    d_queries = (
        jnp.einsum("shqk,skhd->sqhd", d_scores, key_split, preferred_element_type=jnp.float32)
        * 0.125
    ).astype(jnp.bfloat16)
    d_keys = (
        jnp.einsum("shqk,sqhd->skhd", d_scores, query_heads, preferred_element_type=jnp.float32)
        * 0.125
    ).astype(jnp.bfloat16)
    d_values = jnp.einsum(
        "shqk,sqhd->skhd",
        attn_probs.astype(jnp.bfloat16),
        d_context,
        preferred_element_type=jnp.float32,
    ).astype(jnp.bfloat16)
    flat_shape = (queries.shape[0], queries.shape[1], feature_width)
    d_queries = d_queries.reshape(flat_shape)
    d_keys = d_keys.reshape(flat_shape)
    d_values = d_values.reshape(flat_shape)
    d_mixed = jnp.concatenate([d_queries, d_keys, d_values], -1)
    d_w_qkv = jnp.einsum("std,ste->de", first_low, d_mixed, preferred_element_type=jnp.float32)
    d_first = jnp.einsum("ste,de->std", d_mixed, w_qkv, preferred_element_type=jnp.float32)
    d_input_norm, d_gain_first, d_shift_first = norm_backward(
        d_first, normed_first, inverse_first, vectors[0]
    )
    d_hidden = d_middle + d_input_norm
    d_vectors = jnp.stack(
        [
            d_gain_first,
            d_shift_first,
            jnp.sum(d_queries.astype(jnp.float32), (0, 1)),
            jnp.sum(d_values.astype(jnp.float32), (0, 1)),
            d_out_bias,
            d_gain_second,
            d_shift_second,
            d_proj_bias,
        ]
    )
    return (d_hidden, (d_w_qkv, d_w_out, d_w_fc, d_w_proj, d_vectors, d_fc_bias))


def gather_first(img_stack, txt_stack, picture_feature_mapping):
    return (
        lax.all_gather(img_stack[0], "dp", axis=1, tiled=True),
        lax.all_gather(img_stack[1], "dp", axis=1, tiled=True),
        lax.all_gather(img_stack[2], "dp", axis=1, tiled=True),
        lax.all_gather(img_stack[3], "dp", axis=1, tiled=True),
        lax.all_gather(img_stack[4], "dp", axis=2, tiled=True),
        lax.all_gather(img_stack[5], "dp", axis=1, tiled=True),
        lax.all_gather(txt_stack[0], "dp", axis=1, tiled=True),
        lax.all_gather(txt_stack[1], "dp", axis=1, tiled=True),
        lax.all_gather(txt_stack[2], "dp", axis=1, tiled=True),
        lax.all_gather(txt_stack[3], "dp", axis=1, tiled=True),
        lax.all_gather(txt_stack[4], "dp", axis=2, tiled=True),
        lax.all_gather(txt_stack[5], "dp", axis=1, tiled=True),
        lax.all_gather(picture_feature_mapping, "dp", axis=0, tiled=True),
    )


def layer_of(stacks, layer_index):
    return tuple((stacked[layer_index] for stacked in stacks))


def local_plain(
    picture_patch_inputs,
    caption_packed_inputs,
    picture_attend_entry_weight,
    picture_attend_exit_weight,
    picture_widening_weight,
    picture_narrowing_weight,
    picture_affine_entries,
    picture_widening_offset,
    caption_attend_entry_weight,
    caption_attend_exit_weight,
    caption_widening_weight,
    caption_narrowing_weight,
    caption_affine_entries,
    caption_widening_offset,
    picture_feature_mapping,
    sharpness_exponent,
    caption_token_counts,
    matching_picture_index,
):
    img_stack = (
        picture_attend_entry_weight,
        picture_attend_exit_weight,
        picture_widening_weight,
        picture_narrowing_weight,
        picture_affine_entries,
        picture_widening_offset,
    )
    txt_stack = (
        caption_attend_entry_weight,
        caption_attend_exit_weight,
        caption_widening_weight,
        caption_narrowing_weight,
        caption_affine_entries,
        caption_widening_offset,
    )
    images = picture_patch_inputs.shape[0] // TOK_I
    row_count = caption_packed_inputs.shape[0] // TOK_T
    img_hidden = picture_patch_inputs.astype(jnp.float32).reshape(images, TOK_I, -1)
    txt_hidden = caption_packed_inputs.astype(jnp.float32).reshape(row_count, TOK_T, -1)
    img_allowed = jnp.ones((images, TOK_I, TOK_I), dtype=jnp.bool_)
    seg_ends = jnp.cumsum(caption_token_counts, axis=1)
    position = jnp.arange(TOK_T, dtype=jnp.int32)
    segment = jnp.sum((position[None, :, None] >= seg_ends[:, None, :]).astype(jnp.int32), -1)
    txt_allowed = (segment[:, :, None] == segment[:, None, :]) & (
        position[None, None, :] <= position[None, :, None]
    )
    pooling = (position[None, None, :] == seg_ends[:, :, None] - 1).astype(jnp.float32)
    gathered = gather_first(img_stack, txt_stack, picture_feature_mapping)
    img_full = gathered[0:6]
    txt_full = gathered[6:12]
    projection = gathered[12]
    img_stored, txt_stored = ([], [])
    layer_index = 0
    img_hidden, stored = block_forward(img_hidden, layer_of(img_full, layer_index), img_allowed)
    img_stored.append(stored)
    layer_index = 0
    txt_hidden, stored = block_forward(txt_hidden, layer_of(txt_full, layer_index), txt_allowed)
    txt_stored.append(stored)
    pooled_img = img_hidden[:, 0, :].astype(jnp.bfloat16)
    raw_img = jnp.dot(pooled_img, projection, preferred_element_type=jnp.float32)
    scale_img = lax.rsqrt(jnp.sum(raw_img * raw_img, -1, keepdims=True) + 1e-06)
    unit_img = raw_img * scale_img
    raw_txt = jnp.einsum("sct,std->scd", pooling, txt_hidden, precision=lax.Precision.HIGHEST)
    raw_txt = raw_txt.reshape(-1, raw_txt.shape[-1])
    scale_txt = lax.rsqrt(jnp.sum(raw_txt * raw_txt, -1, keepdims=True) + 1e-06)
    unit_txt = raw_txt * scale_txt
    image_embedding_rows = unit_img.astype(jnp.bfloat16)
    text_embedding_rows = unit_txt.astype(jnp.bfloat16)
    all_img, all_txt = (
        lax.all_gather(image_embedding_rows, "dp", axis=0, tiled=True),
        lax.all_gather(text_embedding_rows, "dp", axis=0, tiled=True),
    )
    batch_total = all_img.shape[0]
    affinity_sharpness = jnp.exp(sharpness_exponent)
    picture_wise_affinity_table = affinity_sharpness * jnp.einsum(
        "ce,ie->ci", text_embedding_rows, all_img, preferred_element_type=jnp.float32
    )
    caption_wise_affinity_table = affinity_sharpness * jnp.einsum(
        "ce,ie->ci", all_txt, image_embedding_rows, preferred_element_type=jnp.float32
    )
    lse_rows = jax.nn.logsumexp(picture_wise_affinity_table, 1)
    lse_cols = jax.nn.logsumexp(caption_wise_affinity_table, 0)
    columns = jnp.arange(batch_total, dtype=jnp.int32)
    target_rows = (matching_picture_index[:, None] == columns[None, :]).astype(jnp.float32)
    loss_part = (jnp.sum(lse_rows) + jnp.sum(lse_cols)) / (2 * batch_total) - jnp.sum(
        target_rows * picture_wise_affinity_table
    ) / batch_total
    probs_rows = jnp.exp(picture_wise_affinity_table - lse_rows[:, None])
    probs_cols = jnp.exp(caption_wise_affinity_table - lse_cols[None, :])
    gathered_image_matrix = all_img.astype(jnp.float32)
    gathered_text_matrix = all_txt.astype(jnp.float32)
    highest_precision = lax.Precision.HIGHEST
    row_gradient = probs_rows / (2 * batch_total) - target_rows / batch_total
    column_gradient = probs_cols / (2 * batch_total)
    caption_normalized_adjoint = affinity_sharpness * jnp.dot(
        row_gradient, gathered_image_matrix, precision=highest_precision
    )
    picture_normalized_adjoint = affinity_sharpness * jnp.dot(
        column_gradient.T, gathered_text_matrix, precision=highest_precision
    )
    picture_distributed_adjoint = affinity_sharpness * jnp.dot(
        row_gradient.T, text_embedding_rows.astype(jnp.float32), precision=highest_precision
    )
    caption_distributed_adjoint = affinity_sharpness * jnp.dot(
        column_gradient, image_embedding_rows.astype(jnp.float32), precision=highest_precision
    )
    back_img, back_txt = (
        lax.psum_scatter(picture_distributed_adjoint, "dp", scatter_dimension=0, tiled=True),
        lax.psum_scatter(caption_distributed_adjoint, "dp", scatter_dimension=0, tiled=True),
    )
    picture_normalized_adjoint = picture_normalized_adjoint + back_img
    caption_normalized_adjoint = caption_normalized_adjoint + back_txt
    scale_part = jnp.sum(row_gradient * picture_wise_affinity_table) + jnp.sum(
        column_gradient * caption_wise_affinity_table
    )
    loss, d_scale = lax.psum((loss_part, scale_part), "dp")
    img_back = gathered[0:6]
    txt_back = gathered[6:12]
    back_projection = gathered[12]
    d_raw_img = scale_img * (
        picture_normalized_adjoint
        - unit_img * jnp.sum(picture_normalized_adjoint * unit_img, -1, keepdims=True)
    )
    d_raw_low = d_raw_img.astype(jnp.bfloat16)
    d_projection = jnp.dot(pooled_img.T, d_raw_low, preferred_element_type=jnp.float32)
    d_pooled = jnp.dot(d_raw_low, back_projection.T, preferred_element_type=jnp.float32)
    d_img_hidden = jnp.concatenate(
        [d_pooled[:, None, :], jnp.zeros((images, TOK_I - 1, d_pooled.shape[-1]), jnp.float32)], 1
    )
    d_raw_txt = scale_txt * (
        caption_normalized_adjoint
        - unit_txt * jnp.sum(caption_normalized_adjoint * unit_txt, -1, keepdims=True)
    )
    d_txt_hidden = jnp.einsum(
        "sct,scd->std",
        pooling,
        d_raw_txt.reshape(row_count, CAP_ROW, -1),
        precision=highest_precision,
    )
    img_layer_grads, txt_layer_grads = ([], [])
    layer_index = 0
    d_img_hidden, layer_grads = block_backward(
        d_img_hidden, layer_of(img_back, layer_index), img_stored[layer_index], img_allowed
    )
    img_layer_grads.append(layer_grads)
    img_layer_grads = img_layer_grads[::-1]
    img_local = tuple(
        (jnp.stack([grads[member] for grads in img_layer_grads]) for member in range(6))
    )
    layer_index = 0
    d_txt_hidden, layer_grads = block_backward(
        d_txt_hidden, layer_of(txt_back, layer_index), txt_stored[layer_index], txt_allowed
    )
    txt_layer_grads.append(layer_grads)
    txt_layer_grads = txt_layer_grads[::-1]
    txt_local = tuple(
        (jnp.stack([grads[member] for grads in txt_layer_grads]) for member in range(6))
    )
    summed = (
        lax.psum_scatter(img_local[0], "dp", scatter_dimension=1, tiled=True),
        lax.psum_scatter(img_local[1], "dp", scatter_dimension=1, tiled=True),
        lax.psum_scatter(img_local[2], "dp", scatter_dimension=1, tiled=True),
        lax.psum_scatter(img_local[3], "dp", scatter_dimension=1, tiled=True),
        lax.psum_scatter(img_local[4], "dp", scatter_dimension=2, tiled=True),
        lax.psum_scatter(img_local[5], "dp", scatter_dimension=1, tiled=True),
        lax.psum_scatter(txt_local[0], "dp", scatter_dimension=1, tiled=True),
        lax.psum_scatter(txt_local[1], "dp", scatter_dimension=1, tiled=True),
        lax.psum_scatter(txt_local[2], "dp", scatter_dimension=1, tiled=True),
        lax.psum_scatter(txt_local[3], "dp", scatter_dimension=1, tiled=True),
        lax.psum_scatter(txt_local[4], "dp", scatter_dimension=2, tiled=True),
        lax.psum_scatter(txt_local[5], "dp", scatter_dimension=1, tiled=True),
        lax.psum_scatter(d_projection, "dp", scatter_dimension=0, tiled=True),
    )
    return (
        loss,
        d_scale,
        d_img_hidden.reshape(images * TOK_I, -1),
        d_txt_hidden.reshape(row_count * TOK_T, -1),
        summed[0],
        summed[1],
        summed[2],
        summed[3],
        summed[4],
        summed[5],
        summed[6],
        summed[7],
        summed[8],
        summed[9],
        summed[10],
        summed[11],
        summed[12],
    )


F32 = jnp.float32
BF16 = jnp.bfloat16
Z_PEERS = (8, 16, 24)
PLANE_PEERS = (2, 4, 6)
CHIP_PEERS = tuple(range(2, 32, 2))
ALL_PEERS = (1, 3, 5, 7, 9, 17, 25) + CHIP_PEERS
PAD = 16
N_SEMS = 100
STEP_ROWS = 32


def fits(mesh):
    return mesh.size == 32


def dot(left, right):
    return lax.dot_general(left, right, (((1,), (0,)), ((), ())), preferred_element_type=F32)


def dot_nt(left, right):
    return lax.dot_general(left, right, (((1,), (1,)), ((), ())), preferred_element_type=F32)


def dot_tn(left, right):
    return lax.dot_general(left, right, (((0,), (0,)), ((), ())), preferred_element_type=F32)


def split_two(values):
    high = values.astype(BF16)
    return high, (values - high.astype(F32)).astype(BF16)


def iota(shape, dim):
    return lax.broadcasted_iota(jnp.int32, shape, dim)


def expand_heads(rows):
    lanes = iota(rows.shape, 1) // HD
    heads = rows.shape[1] // HD
    zero = jnp.zeros_like(rows)
    return jnp.concatenate([jnp.where(lanes == head, rows, zero) for head in range(heads)], 0)


def join_heads(stacked):
    heads = stacked.shape[1] // HD
    lanes = iota((PAD, stacked.shape[1]), 1) // HD
    total = jnp.zeros((PAD, stacked.shape[1]), F32)
    for head in range(heads):
        total = jnp.where(lanes == head, stacked[PAD * head : PAD * (head + 1)], total)
    return total


def small_norm(hidden, gain, shift):
    centred = hidden - jnp.mean(hidden, -1, keepdims=True)
    inverse = lax.rsqrt(jnp.mean(centred * centred, -1, keepdims=True) + 1e-05)
    normed = centred * inverse
    return normed, inverse, normed * gain + shift


def small_norm_back(upstream, normed, inverse, gain):
    scaled = upstream * gain
    return inverse * (
        scaled
        - jnp.mean(scaled, -1, keepdims=True)
        - normed * jnp.mean(scaled * normed, -1, keepdims=True)
    )


def col_sum(values):
    return jnp.sum(values, 0, keepdims=True)


class Split:
    def __init__(self, along_z):
        self.along_z = along_z
        self.group_peers = Z_PEERS if along_z else PLANE_PEERS
        self.copy_peers = PLANE_PEERS if along_z else Z_PEERS
        self.line_peers = (1,) + tuple(mask + core for mask in self.group_peers for core in range(2))

    def stand(self, step):
        self.g, self.r = (step.zed, step.plane) if self.along_z else (step.plane, step.zed)
        self.spot = step.core * 4 + self.g

    def chip_of(self, group, copy):
        return 4 * group + copy if self.along_z else 4 * copy + group

    def device_of(self, group, copy, core):
        return 2 * self.chip_of(group, copy) + core

    def group_of(self, device):
        return device // 8 if self.along_z else lax.rem(device // 2, 4)

    def copy_of(self, device):
        return lax.rem(device // 2, 4) if self.along_z else device // 8

    def chips_of_group(self, ref, group):
        return ref.at[group] if self.along_z else ref.at[:, group]

    def chips_of_copy(self, ref, copy):
        return ref.at[:, copy] if self.along_z else ref.at[copy]


class Tower:
    def __init__(self, along_z, width, real_tokens, rows, block, extra):
        self.ff, self.at = Split(along_z), Split(along_z)
        self.width = width
        self.real_tokens = real_tokens
        self.tokens = -(-real_tokens // 128) * 128
        self.rows = rows
        self.chip_rows = 2 * rows
        self.block = block
        self.group = 4 * block
        self.heads = width // HD
        self.queries = PAD * self.heads
        self.extra = extra
        self.packed = 2 * width + extra + 4 * self.group
        self.row_pad = -(-rows // 16) * 16
        self.fold = 1 if rows % 16 == 0 else 2
        self.tiles = 4 * (self.queries // 128) + 2 * (self.queries % 128 // 64)
        self.sums = {}
        self.c_r1 = self.c_r2 = None

    def scratch(self):
        d, n, r, g, b, cr = self.width, self.tokens, self.queries, self.group, self.block, self.chip_rows
        c1, c2 = 2 * d + 2 * self.extra, 2 * d
        v = pltpu.VMEM
        return dict(
            pk=v((2, self.row_pad, self.packed), BF16),
            pr=v((self.row_pad, self.packed), BF16),
            w1=v((2, 16 * cr, d), BF16),
            w2=v((2, 16 * cr, d), BF16),
            mf=v((4, cr, g), BF16),
            fa=v((4, 4, cr, g), BF16),
            wp=v((4, b, d), BF16),
            vecs=v((8, d), F32),
            bias=v((8, g), F32),
            xp=v((n, d), BF16),
            xh=v((n, d), F32),
            inv=v((n, 128), F32),
            a=v((n, d), BF16),
            p32=v((r, n), F32),
            lh=v((2 * r + 2 * PAD, n), BF16),
            rh=v((2 * r + 2 * PAD, d), BF16),
            ci=v((8, PAD, d), BF16),
            hpf=v((8, PAD, d), F32),
            hps=v((8, PAD, d), BF16),
            hr=v((7, PAD, d), BF16),
            dcf=v((8, PAD, d), F32),
            dcs=v((8, PAD, d), BF16),
            dcr=v((7, PAD, d), BF16),
            u=v((8 * PAD, g), F32),
            mt=v((4, b, 8 * PAD), BF16),
            mtr=v((4, b, 8 * PAD), BF16),
            gff=v((4, 4, cr, g), F32),
            gfb=v((4, 4, cr, g), BF16),
            gfr=v((3, 4, cr, g), BF16),
            gf2=v((4, cr, g), BF16),
            gf3=v((4, cr, g), F32),
            gf3r=v((4, cr, g), BF16),
            gf4=v((4, self.rows, g), F32),
            in1t=v((self.tiles, 4, cr, 128), BF16),
            in1r=v((4, self.tiles, cr, 128), BF16),
            in2t=v((self.tiles, 4, cr, 128), BF16),
            in2r=v((4, self.tiles, cr, 128), BF16),
            ag=v((4, PAD, d), BF16),
            wg=v((4, PAD, d), BF16),
            dqg=v((4, PAD, d), BF16),
            pg=v((4, PAD, d), BF16),
            og=v((4, PAD, d), BF16),
            in3t=v((4, 4, cr, 8 * PAD), BF16),
            in4t=v((4, 4, cr, 8 * PAD), BF16),
            r1f=v((4, cr, c1), F32),
            r1p=v((4, self.rows, c1), F32),
            r1s=v((4, self.rows, c1), F32),
            r1b=v((4, self.fold * self.rows, c1 // self.fold), BF16),
            r1r=v((3, self.fold * self.rows, c1 // self.fold), BF16),
            r2f=v((4, cr, c2), F32),
            r2p=v((4, self.rows, c2), F32),
            r2s=v((4, self.rows, c2), F32),
            r2b=v((4, self.fold * self.rows, c2 // self.fold), BF16),
            r2r=v((3, self.fold * self.rows, c2 // self.fold), BF16),
            da=v((n, d), F32),
            gp=v((n, d), F32),
            dxs=v((self.real_tokens, d), F32),
            g2=v((8, PAD, d), F32),
            dbs=v((8, g), F32),
            dbr=v((3, 8, g), F32),
        )


def shared_scratch(ti, tt):
    v = pltpu.VMEM
    e = tt.width
    rows = 32 * PAD
    return dict(
        vb=v((2, 16, PAD, 128), BF16),
        w3=v((2, ti.width, ti.extra), BF16),
        eb=v((2, 2, 16, PAD, e), BF16),
        gtxt=v((rows, rows), F32),
        gimg=v((rows, rows), F32),
        drb=v((8, PAD, e), BF16),
        va=v((8, ti.width + tt.width), F32),
        var=v((8, ti.width + tt.width), F32),
        vs=v((16, 8, 128), F32),
        vl=v((16, 8, 128), F32),
    )


class Group:
    def __init__(self, step):
        self.step = step
        self.index = step.used
        step.used += 1
        step.groups.append(self)

    def copy(self, src, dst, mask):
        return pltpu.make_async_remote_copy(
            src_ref=src,
            dst_ref=dst,
            send_sem=self.step.ssem.at[self.index],
            recv_sem=self.step.rsem.at[self.index],
            device_id=(self.step.at_peer(mask),),
            device_id_type=pl.DeviceIdType.MESH,
        )

    def send(self, src, dst, mask):
        self.copy(src, dst, mask).start()

    def wait(self, view):
        self.view = view
        self.copy(view, view, 1).wait_recv()

    def finish(self):
        self.copy(self.view, self.view, 1).wait_send()


class Gather:
    def __init__(self, step, slot, span, whole, relay):
        self.step, self.slot, self.span, self.whole, self.relayed = step, slot, span, whole, relay
        self.own = self.step.chip

    def chip(self, mask):
        return self.step.at_peer(mask) // 2

    def spread(self, group, chip):
        here = self.slot(chip)
        for mask in PLANE_PEERS[:2] if self.relayed else PLANE_PEERS:
            group.send(here, here, mask)

    def begin_z(self):
        self.g_z = Group(self.step)
        here = self.slot(self.own)
        for mask in Z_PEERS:
            self.g_z.send(here, here, mask)

    def begin_plane(self):
        self.g_own = Group(self.step)
        self.spread(self.g_own, self.own)

    def middle(self):
        self.g_z.wait(self.span(3))
        self.g_mid = Group(self.step)
        for mask in Z_PEERS:
            self.spread(self.g_mid, self.chip(mask))

    def hand_on(self, mask):
        for half, near, to in ((0, 2, 4), (1, 4, 2)):
            there = self.slot(self.chip(near | mask), half)
            self.g_relay.send(there, there, to)

    def relay_own(self):
        self.g_own.wait(self.span(2))
        self.g_relay = Group(self.step)
        self.hand_on(0)

    def relay(self):
        self.g_mid.wait(self.span(6))
        for mask in Z_PEERS:
            self.hand_on(mask)

    def end(self):
        if self.relayed:
            self.g_relay.wait(self.span(4))
        else:
            self.g_own.wait(self.span(3))
            self.g_mid.wait(self.span(9))
        self.g_core = Group(self.step)
        self.g_core.send(self.whole, self.whole, 1)

    def done(self):
        self.g_core.wait(self.whole)


class Step:
    def __init__(self, ti, tt, images):
        self.ti, self.tt, self.images = ti, tt, images
        me = lax.axis_index("dp")
        self.bits = [lax.rem(me // (1 << bit), 2) for bit in range(5)]
        self.me = me
        self.core = lax.rem(me, 2)
        self.chip = me // 2
        self.plane = lax.rem(me // 2, 4)
        self.zed = me // 8
        for t in (ti, tt):
            t.ff.stand(self)
            t.at.stand(self)
        self.used = 0
        self.groups = []

    def at_peer(self, mask):
        total = 0
        for bit in range(5):
            value = 1 - self.bits[bit] if mask >> bit & 1 else self.bits[bit]
            total = total + value * (1 << bit)
        return total

    def barrier(self):
        semaphore = pltpu.get_barrier_semaphore()
        for mask in ALL_PEERS:
            pl.semaphore_signal(
                semaphore, inc=1, device_id=(self.at_peer(mask),), device_id_type=pl.DeviceIdType.MESH
            )
        pl.semaphore_wait(semaphore, len(ALL_PEERS))

    def row_gather(self, buffer, rows):
        cols = buffer.shape[2] // 2

        def slot(chip, half=None):
            at = pl.ds(pl.multiple_of(chip * rows, 16), rows)
            if half is None:
                return buffer.at[self.core, at]
            return buffer.at[self.core, at, half * cols : (half + 1) * cols]

        return Gather(
            self, slot, lambda count: buffer.at[self.core, 0 : count * rows], buffer.at[self.core], True
        )

    def line_gather(self, split, buffer):
        group = Group(self)
        here = buffer.at[split.spot]
        for mask in split.line_peers:
            group.send(here, here, mask)
        return group

    def line_scatter(self, split, parts, landing):
        group = Group(self)
        for slot, mask in enumerate(split.line_peers):
            peer = self.at_peer(mask)
            group.send(parts.at[lax.rem(peer, 2) * 4 + split.group_of(peer)], landing.at[slot], mask)
        return group

    def to_group(self, split, block, landing):
        group = Group(self)
        for mask in split.group_peers:
            group.send(block.at[:, split.group_of(self.at_peer(mask))], landing.at[split.g], mask)
        landing[split.g] = block[:, split.g]
        return group

    def share_group(self, split, buffer, values):
        group = Group(self)
        buffer[split.g] = values
        here = buffer.at[split.g]
        for mask in split.group_peers:
            group.send(here, here, mask)
        return group

    def to_copies(self, split, block, landing):
        group = Group(self)
        for slot, mask in enumerate(split.copy_peers):
            group.send(block.at[split.copy_of(self.at_peer(mask))], landing.at[slot], mask)
        return group

    def run(self):
        ti, tt = self.ti, self.tt
        both = (ti, tt)
        self.pack(ti)
        self.pack(tt)
        self.pack_vectors()
        self.barrier()
        for t in both:
            t.pair = Group(self)
            t.pair.send(t.pk.at[1 - self.core], t.pr, 1)
        vb, eb = self.vb, self.eb
        vectors = Gather(
            self,
            lambda chip: vb.at[self.core, chip],
            lambda count: vb.at[self.core, 0:count],
            vb.at[self.core],
            False,
        )
        vectors.begin_z()
        vectors.begin_plane()
        for t in both:
            t.first = self.row_gather(t.w1, t.chip_rows)
            t.second = self.row_gather(t.w2, t.chip_rows)
        third = self.row_gather(self.w3, ti.chip_rows)
        for t in both:
            self.merge(t)
            t.first.begin_z()
            t.first.begin_plane()
        for t in both:
            self.narrow_begin(t)
        self.standardize(tt)
        vectors.middle()
        self.standardize(ti)
        for t in both:
            t.first.relay_own()
        for t in both:
            t.second.begin_plane()
        for t in both:
            t.first.middle()
        for t in both:
            t.second.begin_z()
        for t in both:
            t.first.relay()
        vectors.end()
        for t in both:
            t.second.relay_own()
        vectors.done()
        self.unpack_vectors()
        self.queries(ti)
        self.queries(tt)
        for t in both:
            t.second.middle()
        for t in both:
            self.widen_begin(t)
        third.begin_z()
        for t in both:
            t.first.end()
        third.begin_plane()
        for t in both:
            t.second.relay()
        for t in both:
            t.first.done()
            self.attend(t)
            self.early_operands(t)
        for t in both:
            self.widen_middle(t)
        third.middle()
        third.relay_own()
        for t in both:
            t.second.end()
        third.relay()
        for t in both:
            t.second.done()
            self.mix(t)
        third.end()
        for t in both:
            t.c_o = self.share_group(t.at, t.og, t.o)
        for t in both:
            self.feed(t)
        third.done()
        for t in both:
            self.embed(t)
        rows = Gather(
            self,
            lambda chip: eb.at[:, self.core, chip],
            lambda count: eb.at[:, self.core, 0:count],
            eb.at[:, self.core],
            False,
        )
        rows.begin_z()
        rows.begin_plane()
        ti.c_p = self.share_group(ti.at, ti.pg, self.pooled)
        rows.middle()
        rows.end()
        rows.done()
        self.contrast()
        for t in both:
            self.feed_back(t)
        for t in both:
            self.feed_weights(t)
        for t in both:
            self.feed_proj(t)
        for t in both:
            self.attend_back(t)
        for t in both:
            self.attend_back_end(t)
        for t in both:
            self.input_gradient(t)
        self.vector_sum_begin()
        for t in both:
            self.round_one(t)
        self.vector_sum_spread()
        for t in both:
            self.feed_weights_middle(t)
        for t in both:
            self.round_spread(t, 0)
        for t in both:
            self.round_two(t)
        for t in both:
            self.round_spread(t, 1)
        for t in both:
            self.feed_weights_end(t)
        self.vector_sum_done()
        for t in both:
            self.round_end(t, 0)
        for t in both:
            self.feed_weights_done(t)
        for t in both:
            self.round_end(t, 1)
        for t in both:
            self.copy_out(t).wait()
        for group in self.groups:
            group.finish()

    def pack(self, t):
        pk, qkv, out, fc = t.pk, t.qkv, t.out, t.fc
        d, b = t.width, t.block
        pad = t.row_pad - t.rows

        def padded(values):
            values = values.astype(F32)
            if pad:
                values = jnp.concatenate([values, jnp.zeros((pad, values.shape[1]), F32)], 0)
            return values.astype(BF16)

        pk[0, :, 0:d] = padded(qkv[:, 0:d])
        pk[1, :, 0:d] = padded(qkv[:, d : 2 * d])
        pk[0, :, d : 2 * d] = padded(qkv[:, 2 * d : 3 * d])
        pk[1, :, d : 2 * d] = padded(out[...])
        if t.extra:
            for half in range(2):
                cols = slice(half * t.extra, (half + 1) * t.extra)
                pk[half, :, 2 * d : 2 * d + t.extra] = padded(self.map[:, cols])
        base = 2 * d + t.extra
        values = padded(fc[...]).astype(F32)
        for half in range(2):
            for group in range(4):
                pieces = []
                for copy in range(4):
                    device = t.ff.device_of(group, copy, half)
                    pieces.append(values[:, b * device : b * (device + 1)])
                start = base + group * t.group
                pk[half, :, start : start + t.group] = jnp.concatenate(pieces, 1).astype(BF16)

    def pack_vectors(self):
        def widen(values, at):
            values = values.astype(F32)
            parts = [values, jnp.zeros((values.shape[0], 128 - at - values.shape[1]), F32)]
            if at:
                parts = [jnp.zeros((values.shape[0], at), F32)] + parts
            return jnp.concatenate(parts, 1)

        top = widen(self.ti.vec[...], 0) + widen(self.tt.vec[...], 32)
        row = iota((8, 128), 0)
        bottom = jnp.where(row == 0, widen(self.ti.fcb[...], 0), 0.0)
        bottom = bottom + jnp.where(row == 1, widen(self.tt.fcb[...], 0), 0.0)
        block = jnp.concatenate([top, bottom], 0)
        row, lane = iota((PAD, 128), 0), iota((PAD, 128), 1)
        for caption in range(self.images):
            image = self.match[caption]
            device = image // self.images
            high = lax.rem(device, 2) * 16 + device // 2
            low = image - device * self.images
            block = jnp.where((row == caption) & (lane == 120), high.astype(F32), block)
            block = jnp.where((row == caption) & (lane == 121), low.astype(F32), block)
        self.vb[self.core, self.chip] = block.astype(BF16)

    def unpack_vectors(self):
        vb = self.vb
        for core in range(2):
            for chip in range(16):
                block = vb[core, chip].astype(F32)
                device = 2 * chip + core
                for t, at in ((self.ti, 0), (self.tt, 32)):
                    rows = t.rows
                    t.vecs[:, rows * device : rows * (device + 1)] = block[0:8, at : at + rows]
        for t, row in ((self.ti, 8), (self.tt, 9)):
            for copy in range(4):
                block = vb[self.core, t.ff.chip_of(t.ff.g, copy)].astype(F32)
                b = t.block
                t.bias[0:1, b * copy : b * (copy + 1)] = block[row : row + 1, 0:b]

    def standardize(self, t):
        x, xp, xh, inv = t.x, t.xp, t.xh, t.inv
        step = STEP_ROWS
        full = t.real_tokens // step

        def norm(hidden, rows):
            xp[rows, :] = hidden.astype(BF16)
            centred = hidden - jnp.mean(hidden, -1, keepdims=True)
            inverse = lax.rsqrt(jnp.mean(centred * centred, -1, keepdims=True) + 1e-05)
            xh[rows, :] = centred * inverse
            inv[rows, :] = jnp.broadcast_to(inverse, (step, 128))

        def body(index, carry):
            rows = pl.ds(pl.multiple_of(index * step, step), step)
            norm(x[rows, :].astype(F32), rows)
            return carry

        lax.fori_loop(0, full, body, 0)
        start, rest = full * step, t.real_tokens - full * step
        if rest:
            last = x[start : t.real_tokens, :].astype(F32)
            last = jnp.concatenate([last, jnp.zeros((step - rest, t.width), F32)], 0)
            norm(last, slice(start, start + step))
            start += step
        while start < t.tokens:
            norm(jnp.zeros((step, t.width), F32), slice(start, start + step))
            start += step

    def merge(self, t):
        t.pair.wait(t.pr)
        pk, pr = t.pk, t.pr
        d, g = t.width, t.group
        rows = pl.ds(pl.multiple_of(self.chip * t.chip_rows, 16), t.chip_rows)
        first = self.core == 0

        def merged(cols):
            own = pk[self.core, :, cols].astype(F32)
            got = pr[:, cols].astype(F32)
            upper = jnp.where(first, own, got)[: t.rows]
            lower = jnp.where(first, got, own)[: t.rows]
            return jnp.concatenate([upper, lower], 0).astype(BF16)

        t.w1[self.core, rows, :] = merged(slice(0, d))
        t.w2[self.core, rows, :] = merged(slice(d, 2 * d))
        base = 2 * d
        if t.extra:
            self.w3[self.core, rows, :] = merged(slice(base, base + t.extra))
            base += t.extra
        for group in range(4):
            t.mf[group] = merged(slice(base + group * g, base + (group + 1) * g))

    def widen_begin(self, t):
        t.widen = Group(self)
        for mask in t.ff.group_peers:
            t.widen.send(t.mf.at[t.ff.group_of(self.at_peer(mask))], t.fa.at[self.zed, self.plane], mask)
        t.fa[self.zed, self.plane] = t.mf[t.ff.g]

    def widen_middle(self, t):
        t.widen.wait(t.mf.at[0:3])
        t.widen = Group(self)
        part = t.ff.chips_of_copy(t.fa, t.ff.r)
        for mask in t.ff.copy_peers:
            t.widen.send(part, part, mask)

    def narrow_begin(self, t):
        t.narrow = Group(self)
        for mask in t.ff.copy_peers:
            t.narrow.send(t.proj, t.wp.at[t.ff.r], mask)
        t.wp[t.ff.r] = t.proj[...]

    def queries(self, t):
        a, xh, vec = t.a, t.xh, t.vecs
        step = STEP_ROWS

        def body(index, carry):
            rows = pl.ds(pl.multiple_of(index * step, step), step)
            a[rows, :] = (xh[rows, :] * vec[0:1, :] + vec[1:2, :]).astype(BF16)
            return carry

        lax.fori_loop(0, t.tokens // step, body, 0)
        n = t.tokens
        row, token = iota((PAD, n), 0), iota((PAD, n), 1)
        if t is self.ti:
            real = row < self.images
            at = jnp.where(real, row * TOK_I, -1)
            low, high = jnp.where(real, row * TOK_I, -1), jnp.where(real, (row + 1) * TOK_I, -1)
        else:
            counts = self.counts
            column = iota((PAD, 1), 0)
            low, high = jnp.full((PAD, 1), -1, jnp.int32), jnp.full((PAD, 1), -1, jnp.int32)
            for line in range(counts.shape[0]):
                end = line * TOK_T
                for member in range(CAP_ROW):
                    begin, end = end, end + counts[line, member]
                    chosen = column == line * CAP_ROW + member
                    low, high = jnp.where(chosen, begin, low), jnp.where(chosen, end, high)
            at = jnp.where(high > 0, high - 1, -1)
        chosen = (token == at).astype(F32).astype(BF16)
        lh, r = t.lh, t.queries
        lh[2 * r : 2 * r + PAD, :] = chosen
        lh[2 * r + PAD : 2 * r + 2 * PAD, :] = chosen
        t.seen = ((token >= low) & (token < high)).astype(F32)
        t.x0 = dot(chosen, t.xp[...])
        t.a0 = dot(chosen, a[...]).astype(BF16)

    def attend(self, t):
        w1, vec, a, r = t.w1, t.vecs, t.a, t.queries
        t.q = (dot(t.a0, w1[0]) + vec[2:3, :]).astype(BF16)
        qt = dot_nt(expand_heads(t.q), w1[1]).astype(BF16)
        t.rh[0:r, :] = qt
        scores = dot_nt(qt, a[...]) * 0.125
        seen = jnp.concatenate([t.seen] * t.heads, 0) > 0.5
        scores = jnp.where(seen, scores, -1000000000.0)
        top = jnp.max(scores, -1, keepdims=True)
        raw = jnp.where(seen, jnp.exp(scores - top), 0.0)
        total = jnp.sum(raw, -1, keepdims=True)
        probs = raw / jnp.where(total > 0.0, total, 1.0)
        t.p32[...] = probs
        low = probs.astype(BF16)
        t.lh[r : 2 * r, :] = low
        t.pa = dot(low, a[...])

    def mix(self, t):
        w2, vec = t.w2, t.vecs
        context = (join_heads(dot(t.pa.astype(BF16), w2[0])) + vec[3:4, :]).astype(BF16)
        t.o = context
        t.h1 = t.x0 + (dot(context, w2[1]) + vec[4:5, :])
        t.xh2, t.inv2, second = small_norm(t.h1, vec[5:6, :], vec[6:7, :])
        t.ci[t.ff.spot] = second.astype(BF16)
        t.line = self.line_gather(t.ff, t.ci)

    def feed(self, t):
        d, g = t.width, t.group
        t.widen.wait(t.fa.at[0:3])
        t.narrow.wait(t.wp.at[0:3])
        t.line.wait(t.ci.at[0:7])
        c = t.ci[...].reshape(8 * PAD, d)
        up = dot(c, t.fa[...].reshape(d, g)) + t.bias[0:1, :]
        active = up * jax.nn.sigmoid(1.702 * up)
        t.u[...] = up
        t.mt[...] = active.T.astype(BF16).reshape(t.mt.shape)
        active = active.astype(BF16)
        part = dot(active, t.wp[...].reshape(g, d)).reshape(8, PAD, d)
        t.hpf[...] = part
        t.hps[...] = part.astype(BF16)
        t.line = self.line_scatter(t.ff, t.hps, t.hr)
        t.mtr[t.ff.r] = t.mt[t.ff.r]
        t.c_m = Group(self)
        for mask in t.ff.copy_peers:
            t.c_m.send(t.mt.at[t.ff.copy_of(self.at_peer(mask))], t.mtr.at[t.ff.r], mask)

    def line_total(self, t, own, landing):
        t.line.wait(landing)
        total = own[t.ff.spot]
        for slot in range(7):
            total = total + landing[slot].astype(F32)
        return total

    def embed(self, t):
        hidden = t.h1 + (self.line_total(t, t.hpf, t.hr) + t.vecs[7:8, :])
        which = 1
        raw = hidden
        if t is self.ti:
            which = 0
            self.pooled = hidden.astype(BF16)
            raw = jnp.concatenate([dot(self.pooled, self.w3[0]), dot(self.pooled, self.w3[1])], 1)
        scale = lax.rsqrt(jnp.sum(raw * raw, -1, keepdims=True) + 1e-06)
        row, lane = iota(raw.shape, 0), iota(raw.shape, 1)
        across = col_sum(jnp.where(row == lane, scale, 0.0))
        high = across.astype(BF16).astype(F32)
        block = jnp.where(row == self.images, high, raw * scale)
        block = jnp.where(row == self.images + 1, across - high, block)
        self.eb[which, self.core, self.chip] = block.astype(BF16)

    def by_rows(self, t, values, buffer):
        turned = values.T.reshape(4, 4, t.chip_rows, t.queries)
        whole = t.queries // 128
        for tile in range(whole):
            part = turned[:, :, :, 128 * tile : 128 * (tile + 1)].astype(BF16)
            for copy in range(4):
                buffer[4 * tile + copy] = part[:, copy] if t.at.along_z else part[copy]
        if t.queries % 128:
            rest = turned[:, :, :, 128 * whole :]
            for pair in range(2):
                if t.at.along_z:
                    parts = [rest[:, 2 * pair], rest[:, 2 * pair + 1]]
                else:
                    parts = [rest[2 * pair], rest[2 * pair + 1]]
                buffer[4 * whole + pair] = jnp.concatenate(parts, 2).astype(BF16)

    def times_heads(self, t, landing, rows, out, start):
        cr, d = t.chip_rows, t.width
        whole = t.queries // 128
        total, paired = 0.0, 0.0
        for group in range(4):
            wide = expand_heads(rows[PAD * group : PAD * (group + 1)])
            for tile in range(whole):
                operand = landing[group, 4 * tile : 4 * (tile + 1)].reshape(4 * cr, 128)
                total = total + dot(operand, wide[128 * tile : 128 * (tile + 1)])
            if t.queries % 128:
                rest = wide[128 * whole :]
                blank = jnp.zeros_like(rest)
                rest = jnp.concatenate(
                    [jnp.concatenate([rest, blank], 0), jnp.concatenate([blank, rest], 0)], 1
                )
                paired = paired + dot(landing[group, 4 * whole : 4 * whole + 2].reshape(2 * cr, 128), rest)
        for z in range(4):
            values = total[cr * z : cr * (z + 1)]
            if t.queries % 128:
                pair = paired[cr * (z // 2) : cr * (z // 2 + 1)]
                values = values + pair[:, d * (z % 2) : d * (z % 2 + 1)]
            out[z, :, start : start + d] = values

    def early_operands(self, t):
        self.by_rows(t, t.pa, t.in1t)
        t.c_in1 = self.to_group(t.at, t.in1t, t.in1r)
        t.c_a = self.share_group(t.at, t.ag, t.a0)

    def contrast(self):
        eb, gtxt, gimg = self.eb, self.gtxt, self.gimg
        size = 32 * PAD
        total = self.images * 32
        e_img, e_txt = eb[0].reshape(size, eb.shape[-1]), eb[1].reshape(size, eb.shape[-1])
        sharp = jnp.exp(jnp.full((8, 128), self.sharp[0], F32))[0:1, 0:1]
        logits = sharp * dot_nt(e_txt, e_img)
        marks = self.vb[...].reshape(size, 128).astype(F32)
        target = marks[:, 120:121] * float(PAD) + marks[:, 121:122]
        row, col = iota((size, size), 0), iota((size, size), 1)
        real = (lax.rem(row, PAD) < self.images) & (lax.rem(col, PAD) < self.images)
        hit = real & (col.astype(F32) == target)
        powers = jnp.where(real, jnp.exp(logits), 0.0)
        row_sum, col_sums = jnp.sum(powers, 1, keepdims=True), col_sum(powers)
        real_line = lax.rem(iota((size, 1), 0), PAD) < self.images
        real_lane = lax.rem(iota((1, size), 1), PAD) < self.images
        row_sum, col_sums = jnp.where(real_line, row_sum, 1.0), jnp.where(real_lane, col_sums, 1.0)
        grad = powers * ((1.0 / row_sum + 1.0 / col_sums) * (0.5 / total))
        grad = grad - jnp.where(hit, 1.0 / total, 0.0)
        safe = jnp.where(real, logits, 0.0)
        logs = jnp.sum(jnp.log(row_sum), 0, keepdims=True) + jnp.sum(jnp.log(col_sums), 1, keepdims=True)

        def whole(values):
            return jnp.sum(jnp.sum(values, 1, keepdims=True), 0, keepdims=True)

        self.loss[...] = logs * (0.5 / total) - whole(jnp.where(hit, safe, 0.0)) * (1.0 / total)
        self.dls[...] = whole(grad * safe)
        gtxt[...] = grad
        gimg[...] = grad.T
        for t in (self.ti, self.tt):
            d_raw = self.raw_gradient(t, t.ff.r)
            if t is self.ti:
                d_raw, rounded = self.through_map(d_raw)
                self.drb[...] = rounded.reshape(self.drb.shape)
            t.g2[...] = d_raw.reshape(t.g2.shape)

    def raw_gradient(self, t, copy):
        eb = self.eb
        which, rows, others = (0, self.gimg, eb[1]) if t is self.ti else (1, self.gtxt, eb[0])
        others = others.reshape(32 * PAD, eb.shape[-1])
        sharp = jnp.exp(jnp.full((8, 128), self.sharp[0], F32))[0:1, 0:1]
        parts, units, scales = [], [], []
        for core in range(2):
            for group in range(4):
                chip = t.ff.chip_of(group, copy)
                start = (core * 16 + chip) * PAD
                if not isinstance(start, int):
                    start = pl.multiple_of(start, PAD)
                parts.append(rows[pl.ds(start, PAD), :])
                block = eb[which, core, chip].astype(F32)
                units.append(block)
                row, lane = iota((PAD, 128), 0), iota((PAD, 128), 1)
                spare = (row >= self.images) & (row < self.images + 2)
                across = col_sum(jnp.where(spare, block[:, 0:128], 0.0))
                scales.append(jnp.sum(jnp.where(row == lane, across, 0.0), 1, keepdims=True))
        part, unit, scale = (jnp.concatenate(pieces, 0) for pieces in (parts, units, scales))
        high, low = split_two(part)
        d_unit = sharp * (dot(high, others) + dot(low, others))
        return scale * (d_unit - unit * jnp.sum(d_unit * unit, -1, keepdims=True))

    def through_map(self, d_raw):
        w3, half = self.w3, self.ti.extra
        rounded = d_raw.astype(BF16)
        return dot_nt(rounded[:, 0:half], w3[0]) + dot_nt(rounded[:, half : 2 * half], w3[1]), rounded

    def feed_back(self, t):
        d, g = t.width, t.group
        t.y = t.g2[...].reshape(8 * PAD, d).astype(BF16)
        up = t.u[...]
        gate = jax.nn.sigmoid(1.702 * up)
        d_active = dot_nt(t.y, t.wp[...].reshape(g, d))
        t.du = (d_active * (gate + 1.702 * up * gate * (1.0 - gate))).astype(BF16)
        part = dot_nt(t.du, t.fa[...].reshape(d, g)).reshape(8, PAD, d)
        t.dcf[...] = part
        t.dcs[...] = part.astype(BF16)
        t.line = self.line_scatter(t.ff, t.dcs, t.dcr)

    def feed_weights(self, t):
        d, g, cr = t.width, t.group, t.chip_rows
        grad = dot_tn(t.ci[...].reshape(8 * PAD, d), t.du).reshape(4, 4, cr, g)
        t.gff[...] = grad
        t.gfb[...] = grad.astype(BF16)
        t.c_wide, t.c_bias = Group(self), Group(self)
        t.dbs[...] = jnp.broadcast_to(col_sum(t.du.astype(F32)), (8, g))
        for slot, mask in enumerate(t.ff.copy_peers):
            copy = t.ff.copy_of(self.at_peer(mask))
            t.c_wide.send(t.ff.chips_of_copy(t.gfb, copy), t.gfr.at[slot], mask)
            t.c_bias.send(t.dbs, t.dbr.at[slot], mask)

    def feed_proj(self, t):
        t.c_m.wait(t.mtr.at[0:3])
        total = 0.0
        for copy in range(4):
            d_raw = self.raw_gradient(t, copy)
            if t is self.ti:
                d_raw = self.through_map(d_raw)[0]
            total = total + dot(t.mtr[copy], d_raw.astype(BF16))
        t.d_proj[...] = total

    def feed_weights_middle(self, t):
        b = t.block
        t.c_wide.wait(t.gfr)
        total = t.ff.chips_of_copy(t.gff, t.ff.r)[...]
        for slot in range(3):
            total = total + t.gfr[slot].astype(F32)
        t.gf2[...] = total.astype(BF16)
        t.gf3[...] = total
        t.c_line = Group(self)
        for mask in t.ff.group_peers:
            t.c_line.send(t.gf2.at[t.ff.group_of(self.at_peer(mask))], t.gf3r.at[t.ff.g], mask)
        t.c_bias.wait(t.dbr)
        bias = t.dbs[0:1, :]
        for slot in range(3):
            bias = bias + t.dbr[slot, 0:1, :]
        mine = jnp.zeros((1, b), F32)
        for copy in range(4):
            mine = jnp.where(t.ff.r == copy, bias[:, b * copy : b * (copy + 1)], mine)
        t.d_fcb[...] = mine

    def feed_weights_end(self, t):
        t.c_line.wait(t.gf2.at[0:3])
        own = t.gf3[t.ff.g]
        for group in range(4):
            t.gf3[group] = jnp.where(t.ff.g == group, own, t.gf3r[group].astype(F32))
        start = pl.multiple_of((1 - self.core) * t.rows, 8)
        t.c_fc = Group(self)
        t.c_fc.send(t.gf3.at[:, pl.ds(start, t.rows)], t.gf4, 1)

    def attend_back(self, t):
        vec = t.vecs
        total = self.line_total(t, t.dcf, t.dcr)
        g2 = t.g2[t.ff.spot]
        t.g1 = g2 + small_norm_back(total, t.xh2, t.inv2, vec[5:6, :])
        branch = t.g1.astype(BF16)
        t.do = dot_nt(branch, t.w2[1]).astype(BF16)
        t.sums.update(
            dbv=col_sum(t.do.astype(F32)),
            dbo=col_sum(branch.astype(F32)),
            dg2=col_sum(total * t.xh2),
            db2=col_sum(total),
            dbp=col_sum(g2.astype(BF16).astype(F32)),
        )
        t.c_w = self.share_group(t.at, t.wg, branch)

    def attend_back_end(self, t):
        r, w1, a, lh, rh = t.queries, t.w1, t.a, t.lh, t.rh
        dvt = dot_nt(expand_heads(t.do), t.w2[0]).astype(BF16)
        rh[r : 2 * r, :] = dvt
        d_probs = dot_nt(dvt, a[...])
        probs = t.p32[...]
        weighted = probs * d_probs
        d_scores = (weighted - probs * jnp.sum(weighted, -1, keepdims=True)).astype(BF16)
        d_scores = (d_scores.astype(F32) * 0.125).astype(BF16)
        lh[0:r, :] = d_scores
        moved = dot(d_scores, a[...])
        self.by_rows(t, moved, t.in2t)
        t.c_in2 = self.to_group(t.at, t.in2t, t.in2r)
        d_query = join_heads(dot(moved.astype(BF16), w1[1])).astype(BF16)
        t.c_dq = self.share_group(t.at, t.dqg, d_query)
        t.sums.update(dbq=col_sum(d_query.astype(F32)))
        high, low = split_two(dot_nt(d_query, w1[0]))
        rh[2 * r : 2 * r + PAD, :] = high
        rh[2 * r + PAD : 2 * r + 2 * PAD, :] = low

    def copy_out(self, t):
        return pltpu.make_async_copy(t.dxs, t.d_x, self.osem.at[0 if t is self.ti else 1])

    def input_gradient(self, t):
        r, d = t.queries, t.width
        lh, da, gp, xh, inv, vec, out = t.lh, t.da, t.gp, t.xh, t.inv, t.vecs, t.dxs
        da[...] = dot_tn(lh[...], t.rh[...])
        high, low = split_two(t.g1)
        gp[...] = dot_tn(lh[2 * r : 2 * r + 2 * PAD, :], jnp.concatenate([high, low], 0))
        step = STEP_ROWS
        full = t.real_tokens // step

        def one(rows, carry):
            z, normed = da[rows, :], xh[rows, :]
            inner = small_norm_back(z, normed, inv[rows, 0:1], vec[0:1, :])
            return inner + gp[rows, :], (
                carry[0] + jnp.sum((z * normed).reshape(step // 8, 8, d), 0),
                carry[1] + jnp.sum(z.reshape(step // 8, 8, d), 0),
            )

        def body(index, carry):
            rows = pl.ds(pl.multiple_of(index * step, step), step)
            out[rows, :], carry = one(rows, carry)
            return carry

        zero = jnp.zeros((8, d), F32)
        carry = lax.fori_loop(0, full, body, (zero, zero))
        start, rest = full * step, t.real_tokens - full * step
        if rest:
            last, carry = one(slice(start, start + step), carry)
            out[start : start + rest, :] = last[:rest]
        self.copy_out(t).start()
        s = t.sums
        rows = [col_sum(carry[0]), col_sum(carry[1])]
        rows += [s.pop(name) for name in list(dict(dbq=0, dbv=0, dbo=0, dg2=0, db2=0, dbp=0))]
        start = 0 if t is self.ti else self.ti.width
        self.va[:, start : start + d] = jnp.concatenate(rows, 0)

    def vector_sum_begin(self):
        self.c_vec = Group(self)
        self.c_vec.send(self.va, self.var, 1)

    def vector_sum_spread(self):
        self.c_vec.wait(self.var)
        total = self.va[...] + self.var[...]
        for chip in range(16):
            pieces, at = [], 0
            for t in (self.ti, self.tt):
                cols = t.chip_rows
                start = at + chip * cols
                pieces += [total[:, start : start + cols], jnp.zeros((8, 64 - cols), F32)]
                at += t.width
            self.vs[chip] = jnp.concatenate(pieces, 1)
        self.c_vec = Group(self)
        for mask in CHIP_PEERS:
            self.c_vec.send(self.vs.at[self.at_peer(mask) // 2], self.vl.at[self.chip], mask)
        self.vl[self.chip] = self.vs[self.chip]

    def vector_sum_done(self):
        self.c_vec.wait(self.vl.at[0:15])
        total = jnp.sum(self.vl[...], 0)
        for t, lane in ((self.ti, 0), (self.tt, 64)):
            rows = t.rows
            halves = [total[:, lane + rows * core : lane + rows * (core + 1)] for core in range(2)]
            t.d_vec[...] = jnp.where(self.core == 0, halves[0], halves[1])

    def turn_members(self, t, first, second, buffer):
        d = t.width
        rows = [part[...].reshape(4 * PAD, d) for part in (first, second)]
        buffer[...] = jnp.concatenate(rows, 0).astype(F32).T.astype(BF16).reshape(buffer.shape)
        return t.at.chips_of_group(buffer, t.at.g)[...].reshape(4 * t.chip_rows, 8 * PAD)

    def round_one(self, t):
        t.c_in1.wait(t.in1r.at[0:3])
        t.c_w.wait(t.wg.at[0:3])
        t.c_o.wait(t.og.at[0:3])
        t.c_a.wait(t.ag.at[0:3])
        d, cr = t.width, t.chip_rows
        members = 4 * PAD
        branch = t.wg[...].reshape(members, d)
        self.times_heads(t, t.in1r, dot_nt(branch, t.w2[1]).astype(BF16), t.r1f, 0)
        t.in3 = self.turn_members(t, t.og, t.ag, t.in3t)
        out = dot(t.in3, jnp.concatenate([branch, jnp.zeros_like(branch)], 0))
        t.r1f[:, :, d : 2 * d] = out.reshape(4, cr, d)
        if t.extra:
            t.c_p.wait(t.pg.at[0:3])
            operand = self.turn_members(t, t.pg, t.pg, t.in4t)
            units = self.drb[pl.ds(self.core * 4, 4)].reshape(members, 2 * t.extra)
            proj = dot(operand, jnp.concatenate([units, jnp.zeros_like(units)], 0))
            t.r1f[:, :, 2 * d :] = proj.reshape(4, cr, 2 * t.extra)
        t.c_r1 = self.round_pair(t, t.r1f, t.r1p)

    def round_two(self, t):
        t.c_in2.wait(t.in2r.at[0:3])
        d, cr = t.width, t.chip_rows
        members = 4 * PAD
        query = dot(t.ag[...].reshape(members, d), t.w1[0]) + t.vecs[2:3, :]
        self.times_heads(t, t.in2r, query.astype(BF16), t.r2f, d)
        t.c_dq.wait(t.dqg.at[0:3])
        d_query = t.dqg[...].reshape(members, d)
        d_query = jnp.concatenate([jnp.zeros_like(d_query), d_query], 0)
        t.r2f[:, :, 0:d] = dot(t.in3, d_query).reshape(4, cr, d)
        t.c_r2 = self.round_pair(t, t.r2f, t.r2p)

    def round_pair(self, t, grad, landing):
        start = pl.multiple_of((1 - self.core) * t.rows, 8)
        group = Group(self)
        group.send(grad.at[:, pl.ds(start, t.rows)], landing, 1)
        return group

    def round_spread(self, t, which):
        group, grad, came, total, packed, landing = (
            (t.c_r1, t.r1f, t.r1p, t.r1s, t.r1b, t.r1r),
            (t.c_r2, t.r2f, t.r2p, t.r2s, t.r2b, t.r2r),
        )[which]
        group.wait(came)
        start = pl.multiple_of(self.core * t.rows, 8)
        values = grad[:, pl.ds(start, t.rows), :] + came[...]
        total[...] = values
        cols = values.shape[2] // t.fold
        pieces = [values[:, :, cols * part : cols * (part + 1)] for part in range(t.fold)]
        packed[...] = jnp.concatenate(pieces, 1).astype(BF16)
        group = self.to_copies(t.at, packed, landing)
        if which:
            t.c_r2 = group
        else:
            t.c_r1 = group

    def round_end(self, t, which):
        group, total, landing = ((t.c_r1, t.r1s, t.r1r), (t.c_r2, t.r2s, t.r2r))[which]
        group.wait(landing)
        arrived = landing[0].astype(F32) + landing[1].astype(F32) + landing[2].astype(F32)
        pieces = [arrived[t.rows * part : t.rows * (part + 1)] for part in range(t.fold)]
        values = total[t.at.r] + jnp.concatenate(pieces, 1)
        d = t.width
        if which:
            t.d_qkv[:, 0 : 2 * d] = values
        else:
            t.d_qkv[:, 2 * d : 3 * d] = values[:, 0:d]
            t.d_out[...] = values[:, d : 2 * d]
            if t.extra:
                self.dmap[...] = values[:, 2 * d :]

    def feed_weights_done(self, t):
        rows, b = t.rows, t.block
        start = pl.multiple_of(self.core * rows, 8)
        t.c_fc.wait(t.gf4)
        for group in range(4):
            own, got = t.gf3[group, pl.ds(start, rows), :], t.gf4[group]
            for half in range(2):
                values = jnp.where(self.core == half, own, got)
                for copy in range(4):
                    device = t.ff.device_of(group, copy, half)
                    t.d_fc[:, b * device : b * (device + 1)] = values[:, b * copy : b * (copy + 1)]


def set_all(target, names, refs):
    for name, ref in zip(names, refs, strict=True):
        setattr(target, name, ref)


def hand_over(results):
    count = len(results)
    cuts = []
    for index, value in enumerate(results):
        rows = value.shape[0]
        step = 120 if rows > 120 and rows % 120 == 0 else rows
        cuts += [(index, start, step) for start in range(0, rows, step)]

    def kernel(*refs):
        came, went = refs[3 * count], refs[3 * count + 1]
        reads, writes = [], []
        for at, (index, start, rows) in enumerate(cuts):
            src, dst, mid = (refs[index + part * count] for part in range(3))
            if rows != src.shape[0]:
                src, dst, mid = (ref.at[start : start + rows] for ref in (src, dst, mid))
            reads.append(pltpu.make_async_copy(src, mid, came.at[at]))
            writes.append(pltpu.make_async_copy(mid, dst, went.at[at]))
        for read in reads:
            read.start()
        for read, write in zip(reads, writes, strict=True):
            read.wait()
            write.start()
        for write in writes:
            write.wait()

    sems = pltpu.SemaphoreType.DMA((len(cuts),))
    return pl.pallas_call(
        kernel,
        out_shape=tuple(jax.ShapeDtypeStruct(value.shape, value.dtype) for value in results),
        in_specs=[pl.BlockSpec(memory_space=pl.ANY)] * count,
        out_specs=tuple([pl.BlockSpec(memory_space=pl.ANY)] * count),
        scratch_shapes=[pltpu.VMEM(value.shape, value.dtype) for value in results] + [sems, sems],
        compiler_params=pltpu.CompilerParams(vmem_limit_bytes=60 * 2**20),
        name="hand_over",
    )(*results)


def local_fused(
    picture_patch_inputs,
    caption_packed_inputs,
    picture_attend_entry_weight,
    picture_attend_exit_weight,
    picture_widening_weight,
    picture_narrowing_weight,
    picture_affine_entries,
    picture_widening_offset,
    caption_attend_entry_weight,
    caption_attend_exit_weight,
    caption_widening_weight,
    caption_narrowing_weight,
    caption_affine_entries,
    caption_widening_offset,
    picture_feature_mapping,
    sharpness_exponent,
    caption_token_counts,
    matching_picture_index,
):
    n_img, d_img = picture_patch_inputs.shape
    n_txt, d_txt = caption_packed_inputs.shape
    images = n_img // TOK_I
    ti = Tower(
        True,
        d_img,
        n_img,
        picture_attend_entry_weight.shape[1],
        picture_widening_offset.shape[1],
        picture_feature_mapping.shape[1] // 2,
    )
    tt = Tower(
        False, d_txt, n_txt, caption_attend_entry_weight.shape[1], caption_widening_offset.shape[1], 0
    )
    img_args = dict(
        x=picture_patch_inputs,
        qkv=picture_attend_entry_weight[0],
        out=picture_attend_exit_weight[0],
        fc=picture_widening_weight[0],
        proj=picture_narrowing_weight[0],
        vec=picture_affine_entries[0],
        fcb=picture_widening_offset,
    )
    txt_args = dict(
        x=caption_packed_inputs,
        qkv=caption_attend_entry_weight[0],
        out=caption_attend_exit_weight[0],
        fc=caption_widening_weight[0],
        proj=caption_narrowing_weight[0],
        vec=caption_affine_entries[0],
        fcb=caption_widening_offset,
    )
    more_args = dict(
        map=picture_feature_mapping,
        sharp=sharpness_exponent.reshape(1),
        counts=caption_token_counts,
        match=matching_picture_index,
    )

    def out(*shape):
        return jax.ShapeDtypeStruct(shape, F32)

    def tower_outs(t):
        return dict(
            d_x=out(t.real_tokens, t.width),
            d_qkv=out(t.rows, 3 * t.width),
            d_out=out(t.rows, t.width),
            d_fc=out(t.rows, 32 * t.block),
            d_proj=out(t.block, t.width),
            d_vec=out(8, t.rows),
            d_fcb=out(1, t.block),
        )

    more_outs = dict(loss=out(1, 1), dls=out(1, 1), dmap=out(ti.rows, 2 * ti.extra))
    in_vmem, in_smem = pl.BlockSpec(memory_space=pltpu.VMEM), pl.BlockSpec(memory_space=pltpu.SMEM)
    anywhere = pl.BlockSpec(memory_space=pl.ANY)
    parts = [
        (ti, img_args, [in_vmem] * 7),
        (tt, txt_args, [in_vmem] * 7),
        (None, more_args, [in_vmem, in_smem, in_smem, in_smem]),
        (ti, tower_outs(ti), [anywhere] + [in_vmem] * 6),
        (tt, tower_outs(tt), [anywhere] + [in_vmem] * 6),
        (None, more_outs, [in_vmem] * 3),
        (ti, ti.scratch(), None),
        (tt, tt.scratch(), None),
        (None, shared_scratch(ti, tt), None),
        (
            None,
            dict(
                ssem=pltpu.SemaphoreType.DMA((N_SEMS,)),
                rsem=pltpu.SemaphoreType.DMA((N_SEMS,)),
                osem=pltpu.SemaphoreType.DMA((2,)),
            ),
            None,
        ),
    ]

    def kernel(*refs):
        step = Step(ti, tt, images)
        at = 0
        for owner, values, _ in parts:
            set_all(step if owner is None else owner, values, refs[at : at + len(values)])
            at += len(values)
        step.run()

    def joined(chosen, field):
        return [item for part in chosen for item in (part[field] if field == 2 else part[field].values())]

    results = pl.pallas_call(
        kernel,
        out_shape=tuple(joined(parts[3:6], 1)),
        in_specs=joined(parts[0:3], 2),
        out_specs=tuple(joined(parts[3:6], 2)),
        scratch_shapes=joined(parts[6:], 1),
        compiler_params=pltpu.CompilerParams(
            collective_id=0, has_side_effects=True, vmem_limit_bytes=60 * 2**20
        ),
        name="contrastive_step",
    )(*joined(parts[0:3], 1))
    results = hand_over(results)
    img, txt, (loss, d_scale, d_map) = results[0:7], results[7:14], results[14:17]
    return (
        loss.reshape(()),
        d_scale.reshape(()),
        img[0],
        txt[0],
        img[1][None],
        img[2][None],
        img[3][None],
        img[4][None],
        img[5][None],
        img[6],
        txt[1][None],
        txt[2][None],
        txt[3][None],
        txt[4][None],
        txt[5][None],
        txt[6],
        d_map,
    )


def solution(mesh):
    placed = (
        P("dp", None),
        P("dp", None),
        P(None, "dp", None),
        P(None, "dp", None),
        P(None, "dp", None),
        P(None, "dp", None),
        P(None, None, "dp"),
        P(None, "dp"),
        P(None, "dp", None),
        P(None, "dp", None),
        P(None, "dp", None),
        P(None, "dp", None),
        P(None, None, "dp"),
        P(None, "dp"),
        P("dp", None),
        P(),
        P("dp", None),
        P("dp"),
    )
    return jax.shard_map(
        local_fused if fits(mesh) else local_plain,
        mesh=mesh,
        in_specs=placed,
        out_specs=(
            P(),
            P(),
            P("dp", None),
            P("dp", None),
            P(None, "dp", None),
            P(None, "dp", None),
            P(None, "dp", None),
            P(None, "dp", None),
            P(None, None, "dp"),
            P(None, "dp"),
            P(None, "dp", None),
            P(None, "dp", None),
            P(None, "dp", None),
            P(None, "dp", None),
            P(None, None, "dp"),
            P(None, "dp"),
            P("dp", None),
        ),
        check_vma=False,
    )
```

```python
import jax
import jax.numpy as jnp
from jax import lax
from jax.experimental import pallas as pl
from jax.experimental.pallas import tpu as pltpu
from jax.sharding import PartitionSpec as P

HD = 64
TOK_I = 50
TOK_T = 77
CAP_ROW = 4


def norm_forward(hidden, norm_gain, norm_shift):
    row_mean = jnp.mean(hidden, -1, keepdims=True)
    centred = hidden - row_mean
    inverse = lax.rsqrt(jnp.mean(centred * centred, -1, keepdims=True) + 1e-05)
    normed = centred * inverse
    return (normed, inverse, normed * norm_gain + norm_shift)


def norm_backward(upstream, normed, inverse, norm_gain):
    scaled = upstream * norm_gain
    inner_sum = (
        scaled
        - jnp.mean(scaled, -1, keepdims=True)
        - normed * jnp.mean(scaled * normed, -1, keepdims=True)
    )
    return (inverse * inner_sum, jnp.sum(upstream * normed, (0, 1)), jnp.sum(upstream, (0, 1)))


def split_heads(values):
    return values.reshape(values.shape[0], values.shape[1], values.shape[2] // HD, HD)


def attention_scores(queries, key_heads, allowed):
    scores = (
        jnp.einsum("sqhd,skhd->shqk", queries, key_heads, preferred_element_type=jnp.float32)
        * 0.125
    )
    return jnp.where(allowed[:, None], scores, -1000000000.0)


def block_forward(hidden, weights, allowed):
    w_qkv, w_out, w_fc, w_proj, vectors, fc_bias = weights
    vectors = vectors.astype(jnp.float32)
    fc_bias = fc_bias.astype(jnp.float32)
    feature_width = hidden.shape[-1]
    normed_first, inverse_first, first = norm_forward(hidden, vectors[0], vectors[1])
    first_low = first.astype(jnp.bfloat16)
    projected = jnp.einsum("std,de->ste", first_low, w_qkv, preferred_element_type=jnp.float32)
    queries = (projected[..., :feature_width] + vectors[2]).astype(jnp.bfloat16)
    key_heads = projected[..., feature_width : 2 * feature_width].astype(jnp.bfloat16)
    values = (projected[..., 2 * feature_width :] + vectors[3]).astype(jnp.bfloat16)
    scores = attention_scores(split_heads(queries), split_heads(key_heads), allowed)
    totals = jax.nn.logsumexp(scores, -1, keepdims=True)
    attn_probs = jnp.exp(scores - totals).astype(jnp.bfloat16)
    context = jnp.einsum(
        "shqk,skhd->sqhd", attn_probs, split_heads(values), preferred_element_type=jnp.float32
    )
    context = context.reshape(hidden.shape).astype(jnp.bfloat16)
    middle = hidden + (
        jnp.einsum("std,de->ste", context, w_out, preferred_element_type=jnp.float32) + vectors[4]
    )
    normed_second, inverse_second, second = norm_forward(middle, vectors[5], vectors[6])
    second_low = second.astype(jnp.bfloat16)
    upward = (
        jnp.einsum("std,df->stf", second_low, w_fc, preferred_element_type=jnp.float32) + fc_bias
    )
    activated = (upward * jax.nn.sigmoid(1.702 * upward)).astype(jnp.bfloat16)
    output = middle + (
        jnp.einsum("stf,fd->std", activated, w_proj, preferred_element_type=jnp.float32)
        + vectors[7]
    )
    stored = (
        normed_first,
        inverse_first,
        first_low,
        queries,
        key_heads,
        values,
        totals,
        context,
        normed_second,
        inverse_second,
        second_low,
        upward,
        activated,
    )
    return (output, stored)


def block_backward(upstream, weights, stored, allowed):
    w_qkv, w_out, w_fc, w_proj, vectors, fc_bias = weights
    vectors = vectors.astype(jnp.float32)
    (
        normed_first,
        inverse_first,
        first_low,
        queries,
        key_heads,
        values,
        totals,
        context,
        normed_second,
        inverse_second,
        second_low,
        upward,
        activated,
    ) = stored
    feature_width = queries.shape[-1]
    branch = upstream.astype(jnp.bfloat16)
    d_proj_bias = jnp.sum(branch.astype(jnp.float32), (0, 1))
    d_w_proj = jnp.einsum("stf,std->fd", activated, branch, preferred_element_type=jnp.float32)
    d_activated = jnp.einsum("std,fd->stf", branch, w_proj, preferred_element_type=jnp.float32)
    sigmoid_up = jax.nn.sigmoid(1.702 * upward)
    d_upward = (
        d_activated * (sigmoid_up + 1.702 * upward * sigmoid_up * (1.0 - sigmoid_up))
    ).astype(jnp.bfloat16)
    d_fc_bias = jnp.sum(d_upward.astype(jnp.float32), (0, 1))
    d_w_fc = jnp.einsum("std,stf->df", second_low, d_upward, preferred_element_type=jnp.float32)
    d_second = jnp.einsum("stf,df->std", d_upward, w_fc, preferred_element_type=jnp.float32)
    d_middle_norm, d_gain_second, d_shift_second = norm_backward(
        d_second, normed_second, inverse_second, vectors[5]
    )
    d_middle = upstream + d_middle_norm
    attn_branch = d_middle.astype(jnp.bfloat16)
    d_out_bias = jnp.sum(attn_branch.astype(jnp.float32), (0, 1))
    d_w_out = jnp.einsum("std,ste->de", context, attn_branch, preferred_element_type=jnp.float32)
    d_context = jnp.einsum("ste,de->std", attn_branch, w_out, preferred_element_type=jnp.float32)
    d_context = split_heads(d_context.astype(jnp.bfloat16))
    query_heads = split_heads(queries)
    key_split = split_heads(key_heads)
    scores = attention_scores(query_heads, key_split, allowed)
    attn_probs = jnp.exp(scores - totals)
    d_probs = jnp.einsum(
        "sqhd,skhd->shqk", d_context, split_heads(values), preferred_element_type=jnp.float32
    )
    d_scores = (attn_probs * (d_probs - jnp.sum(attn_probs * d_probs, -1, keepdims=True))).astype(
        jnp.bfloat16
    )
    d_queries = (
        jnp.einsum("shqk,skhd->sqhd", d_scores, key_split, preferred_element_type=jnp.float32)
        * 0.125
    ).astype(jnp.bfloat16)
    d_keys = (
        jnp.einsum("shqk,sqhd->skhd", d_scores, query_heads, preferred_element_type=jnp.float32)
        * 0.125
    ).astype(jnp.bfloat16)
    d_values = jnp.einsum(
        "shqk,sqhd->skhd",
        attn_probs.astype(jnp.bfloat16),
        d_context,
        preferred_element_type=jnp.float32,
    ).astype(jnp.bfloat16)
    flat_shape = (queries.shape[0], queries.shape[1], feature_width)
    d_queries = d_queries.reshape(flat_shape)
    d_keys = d_keys.reshape(flat_shape)
    d_values = d_values.reshape(flat_shape)
    d_mixed = jnp.concatenate([d_queries, d_keys, d_values], -1)
    d_w_qkv = jnp.einsum("std,ste->de", first_low, d_mixed, preferred_element_type=jnp.float32)
    d_first = jnp.einsum("ste,de->std", d_mixed, w_qkv, preferred_element_type=jnp.float32)
    d_input_norm, d_gain_first, d_shift_first = norm_backward(
        d_first, normed_first, inverse_first, vectors[0]
    )
    d_hidden = d_middle + d_input_norm
    d_vectors = jnp.stack(
        [
            d_gain_first,
            d_shift_first,
            jnp.sum(d_queries.astype(jnp.float32), (0, 1)),
            jnp.sum(d_values.astype(jnp.float32), (0, 1)),
            d_out_bias,
            d_gain_second,
            d_shift_second,
            d_proj_bias,
        ]
    )
    return (d_hidden, (d_w_qkv, d_w_out, d_w_fc, d_w_proj, d_vectors, d_fc_bias))


def gather_first(img_stack, txt_stack, picture_feature_mapping):
    return (
        lax.all_gather(img_stack[0], "dp", axis=1, tiled=True),
        lax.all_gather(img_stack[1], "dp", axis=1, tiled=True),
        lax.all_gather(img_stack[2], "dp", axis=1, tiled=True),
        lax.all_gather(img_stack[3], "dp", axis=1, tiled=True),
        lax.all_gather(img_stack[4], "dp", axis=2, tiled=True),
        lax.all_gather(img_stack[5], "dp", axis=1, tiled=True),
        lax.all_gather(txt_stack[0], "dp", axis=1, tiled=True),
        lax.all_gather(txt_stack[1], "dp", axis=1, tiled=True),
        lax.all_gather(txt_stack[2], "dp", axis=1, tiled=True),
        lax.all_gather(txt_stack[3], "dp", axis=1, tiled=True),
        lax.all_gather(txt_stack[4], "dp", axis=2, tiled=True),
        lax.all_gather(txt_stack[5], "dp", axis=1, tiled=True),
        lax.all_gather(picture_feature_mapping, "dp", axis=0, tiled=True),
    )


def layer_of(stacks, layer_index):
    return tuple((stacked[layer_index] for stacked in stacks))


def local_plain(
    picture_patch_inputs,
    caption_packed_inputs,
    picture_attend_entry_weight,
    picture_attend_exit_weight,
    picture_widening_weight,
    picture_narrowing_weight,
    picture_affine_entries,
    picture_widening_offset,
    caption_attend_entry_weight,
    caption_attend_exit_weight,
    caption_widening_weight,
    caption_narrowing_weight,
    caption_affine_entries,
    caption_widening_offset,
    picture_feature_mapping,
    sharpness_exponent,
    caption_token_counts,
    matching_picture_index,
):
    img_stack = (
        picture_attend_entry_weight,
        picture_attend_exit_weight,
        picture_widening_weight,
        picture_narrowing_weight,
        picture_affine_entries,
        picture_widening_offset,
    )
    txt_stack = (
        caption_attend_entry_weight,
        caption_attend_exit_weight,
        caption_widening_weight,
        caption_narrowing_weight,
        caption_affine_entries,
        caption_widening_offset,
    )
    images = picture_patch_inputs.shape[0] // TOK_I
    row_count = caption_packed_inputs.shape[0] // TOK_T
    img_hidden = picture_patch_inputs.astype(jnp.float32).reshape(images, TOK_I, -1)
    txt_hidden = caption_packed_inputs.astype(jnp.float32).reshape(row_count, TOK_T, -1)
    img_allowed = jnp.ones((images, TOK_I, TOK_I), dtype=jnp.bool_)
    seg_ends = jnp.cumsum(caption_token_counts, axis=1)
    position = jnp.arange(TOK_T, dtype=jnp.int32)
    segment = jnp.sum((position[None, :, None] >= seg_ends[:, None, :]).astype(jnp.int32), -1)
    txt_allowed = (segment[:, :, None] == segment[:, None, :]) & (
        position[None, None, :] <= position[None, :, None]
    )
    pooling = (position[None, None, :] == seg_ends[:, :, None] - 1).astype(jnp.float32)
    gathered = gather_first(img_stack, txt_stack, picture_feature_mapping)
    img_full = gathered[0:6]
    txt_full = gathered[6:12]
    projection = gathered[12]
    img_stored, txt_stored = ([], [])
    layer_index = 0
    img_hidden, stored = block_forward(img_hidden, layer_of(img_full, layer_index), img_allowed)
    img_stored.append(stored)
    layer_index = 0
    txt_hidden, stored = block_forward(txt_hidden, layer_of(txt_full, layer_index), txt_allowed)
    txt_stored.append(stored)
    pooled_img = img_hidden[:, 0, :].astype(jnp.bfloat16)
    raw_img = jnp.dot(pooled_img, projection, preferred_element_type=jnp.float32)
    scale_img = lax.rsqrt(jnp.sum(raw_img * raw_img, -1, keepdims=True) + 1e-06)
    unit_img = raw_img * scale_img
    raw_txt = jnp.einsum("sct,std->scd", pooling, txt_hidden, precision=lax.Precision.HIGHEST)
    raw_txt = raw_txt.reshape(-1, raw_txt.shape[-1])
    scale_txt = lax.rsqrt(jnp.sum(raw_txt * raw_txt, -1, keepdims=True) + 1e-06)
    unit_txt = raw_txt * scale_txt
    image_embedding_rows = unit_img.astype(jnp.bfloat16)
    text_embedding_rows = unit_txt.astype(jnp.bfloat16)
    all_img, all_txt = (
        lax.all_gather(image_embedding_rows, "dp", axis=0, tiled=True),
        lax.all_gather(text_embedding_rows, "dp", axis=0, tiled=True),
    )
    batch_total = all_img.shape[0]
    affinity_sharpness = jnp.exp(sharpness_exponent)
    picture_wise_affinity_table = affinity_sharpness * jnp.einsum(
        "ce,ie->ci", text_embedding_rows, all_img, preferred_element_type=jnp.float32
    )
    caption_wise_affinity_table = affinity_sharpness * jnp.einsum(
        "ce,ie->ci", all_txt, image_embedding_rows, preferred_element_type=jnp.float32
    )
    lse_rows = jax.nn.logsumexp(picture_wise_affinity_table, 1)
    lse_cols = jax.nn.logsumexp(caption_wise_affinity_table, 0)
    columns = jnp.arange(batch_total, dtype=jnp.int32)
    target_rows = (matching_picture_index[:, None] == columns[None, :]).astype(jnp.float32)
    loss_part = (jnp.sum(lse_rows) + jnp.sum(lse_cols)) / (2 * batch_total) - jnp.sum(
        target_rows * picture_wise_affinity_table
    ) / batch_total
    probs_rows = jnp.exp(picture_wise_affinity_table - lse_rows[:, None])
    probs_cols = jnp.exp(caption_wise_affinity_table - lse_cols[None, :])
    gathered_image_matrix = all_img.astype(jnp.float32)
    gathered_text_matrix = all_txt.astype(jnp.float32)
    highest_precision = lax.Precision.HIGHEST
    row_gradient = probs_rows / (2 * batch_total) - target_rows / batch_total
    column_gradient = probs_cols / (2 * batch_total)
    caption_normalized_adjoint = affinity_sharpness * jnp.dot(
        row_gradient, gathered_image_matrix, precision=highest_precision
    )
    picture_normalized_adjoint = affinity_sharpness * jnp.dot(
        column_gradient.T, gathered_text_matrix, precision=highest_precision
    )
    picture_distributed_adjoint = affinity_sharpness * jnp.dot(
        row_gradient.T, text_embedding_rows.astype(jnp.float32), precision=highest_precision
    )
    caption_distributed_adjoint = affinity_sharpness * jnp.dot(
        column_gradient, image_embedding_rows.astype(jnp.float32), precision=highest_precision
    )
    back_img, back_txt = (
        lax.psum_scatter(picture_distributed_adjoint, "dp", scatter_dimension=0, tiled=True),
        lax.psum_scatter(caption_distributed_adjoint, "dp", scatter_dimension=0, tiled=True),
    )
    picture_normalized_adjoint = picture_normalized_adjoint + back_img
    caption_normalized_adjoint = caption_normalized_adjoint + back_txt
    scale_part = jnp.sum(row_gradient * picture_wise_affinity_table) + jnp.sum(
        column_gradient * caption_wise_affinity_table
    )
    loss, d_scale = lax.psum((loss_part, scale_part), "dp")
    img_back = gathered[0:6]
    txt_back = gathered[6:12]
    back_projection = gathered[12]
    d_raw_img = scale_img * (
        picture_normalized_adjoint
        - unit_img * jnp.sum(picture_normalized_adjoint * unit_img, -1, keepdims=True)
    )
    d_raw_low = d_raw_img.astype(jnp.bfloat16)
    d_projection = jnp.dot(pooled_img.T, d_raw_low, preferred_element_type=jnp.float32)
    d_pooled = jnp.dot(d_raw_low, back_projection.T, preferred_element_type=jnp.float32)
    d_img_hidden = jnp.concatenate(
        [d_pooled[:, None, :], jnp.zeros((images, TOK_I - 1, d_pooled.shape[-1]), jnp.float32)], 1
    )
    d_raw_txt = scale_txt * (
        caption_normalized_adjoint
        - unit_txt * jnp.sum(caption_normalized_adjoint * unit_txt, -1, keepdims=True)
    )
    d_txt_hidden = jnp.einsum(
        "sct,scd->std",
        pooling,
        d_raw_txt.reshape(row_count, CAP_ROW, -1),
        precision=highest_precision,
    )
    img_layer_grads, txt_layer_grads = ([], [])
    layer_index = 0
    d_img_hidden, layer_grads = block_backward(
        d_img_hidden, layer_of(img_back, layer_index), img_stored[layer_index], img_allowed
    )
    img_layer_grads.append(layer_grads)
    img_layer_grads = img_layer_grads[::-1]
    img_local = tuple(
        (jnp.stack([grads[member] for grads in img_layer_grads]) for member in range(6))
    )
    layer_index = 0
    d_txt_hidden, layer_grads = block_backward(
        d_txt_hidden, layer_of(txt_back, layer_index), txt_stored[layer_index], txt_allowed
    )
    txt_layer_grads.append(layer_grads)
    txt_layer_grads = txt_layer_grads[::-1]
    txt_local = tuple(
        (jnp.stack([grads[member] for grads in txt_layer_grads]) for member in range(6))
    )
    summed = (
        lax.psum_scatter(img_local[0], "dp", scatter_dimension=1, tiled=True),
        lax.psum_scatter(img_local[1], "dp", scatter_dimension=1, tiled=True),
        lax.psum_scatter(img_local[2], "dp", scatter_dimension=1, tiled=True),
        lax.psum_scatter(img_local[3], "dp", scatter_dimension=1, tiled=True),
        lax.psum_scatter(img_local[4], "dp", scatter_dimension=2, tiled=True),
        lax.psum_scatter(img_local[5], "dp", scatter_dimension=1, tiled=True),
        lax.psum_scatter(txt_local[0], "dp", scatter_dimension=1, tiled=True),
        lax.psum_scatter(txt_local[1], "dp", scatter_dimension=1, tiled=True),
        lax.psum_scatter(txt_local[2], "dp", scatter_dimension=1, tiled=True),
        lax.psum_scatter(txt_local[3], "dp", scatter_dimension=1, tiled=True),
        lax.psum_scatter(txt_local[4], "dp", scatter_dimension=2, tiled=True),
        lax.psum_scatter(txt_local[5], "dp", scatter_dimension=1, tiled=True),
        lax.psum_scatter(d_projection, "dp", scatter_dimension=0, tiled=True),
    )
    return (
        loss,
        d_scale,
        d_img_hidden.reshape(images * TOK_I, -1),
        d_txt_hidden.reshape(row_count * TOK_T, -1),
        summed[0],
        summed[1],
        summed[2],
        summed[3],
        summed[4],
        summed[5],
        summed[6],
        summed[7],
        summed[8],
        summed[9],
        summed[10],
        summed[11],
        summed[12],
    )


F32 = jnp.float32
BF16 = jnp.bfloat16
Z_PEERS = (8, 16, 24)
PLANE_PEERS = (2, 4, 6)
CHIP_PEERS = tuple(range(2, 32, 2))
ALL_PEERS = (1, 3, 5, 7, 9, 17, 25) + CHIP_PEERS
PAD = 16
N_SEMS = 84
STEP_ROWS = 32


def fits(mesh):
    return mesh.size == 32


def dot(left, right):
    return lax.dot_general(left, right, (((1,), (0,)), ((), ())), preferred_element_type=F32)


def dot_nt(left, right):
    return lax.dot_general(left, right, (((1,), (1,)), ((), ())), preferred_element_type=F32)


def dot_tn(left, right):
    return lax.dot_general(left, right, (((0,), (0,)), ((), ())), preferred_element_type=F32)


def split_two(values):
    high = values.astype(BF16)
    return high, (values - high.astype(F32)).astype(BF16)


def iota(shape, dim):
    return lax.broadcasted_iota(jnp.int32, shape, dim)


def expand_heads(rows):
    lanes = iota(rows.shape, 1) // HD
    heads = rows.shape[1] // HD
    zero = jnp.zeros_like(rows)
    return jnp.concatenate([jnp.where(lanes == head, rows, zero) for head in range(heads)], 0)


def join_heads(stacked):
    heads = stacked.shape[1] // HD
    lanes = iota((PAD, stacked.shape[1]), 1) // HD
    total = jnp.zeros((PAD, stacked.shape[1]), F32)
    for head in range(heads):
        total = jnp.where(lanes == head, stacked[PAD * head : PAD * (head + 1)], total)
    return total


def small_norm(hidden, gain, shift):
    centred = hidden - jnp.mean(hidden, -1, keepdims=True)
    inverse = lax.rsqrt(jnp.mean(centred * centred, -1, keepdims=True) + 1e-05)
    normed = centred * inverse
    return normed, inverse, normed * gain + shift


def small_norm_back(upstream, normed, inverse, gain):
    scaled = upstream * gain
    return inverse * (
        scaled
        - jnp.mean(scaled, -1, keepdims=True)
        - normed * jnp.mean(scaled * normed, -1, keepdims=True)
    )


def col_sum(values):
    return jnp.sum(values, 0, keepdims=True)


class Split:
    def __init__(self, along_z):
        self.along_z = along_z
        self.group_peers = Z_PEERS if along_z else PLANE_PEERS
        self.copy_peers = PLANE_PEERS if along_z else Z_PEERS
        self.line_peers = (1,) + tuple(mask + core for mask in self.group_peers for core in range(2))

    def stand(self, step):
        self.g, self.r = (step.zed, step.plane) if self.along_z else (step.plane, step.zed)
        self.spot = step.core * 4 + self.g

    def chip_of(self, group, copy):
        return 4 * group + copy if self.along_z else 4 * copy + group

    def device_of(self, group, copy, core):
        return 2 * self.chip_of(group, copy) + core

    def group_of(self, device):
        return device // 8 if self.along_z else lax.rem(device // 2, 4)

    def copy_of(self, device):
        return lax.rem(device // 2, 4) if self.along_z else device // 8

    def chips_of_group(self, ref, group):
        return ref.at[group] if self.along_z else ref.at[:, group]

    def chips_of_copy(self, ref, copy):
        return ref.at[:, copy] if self.along_z else ref.at[copy]


class Tower:
    def __init__(self, along_z, width, real_tokens, rows, block, extra):
        self.ff, self.at = Split(along_z), Split(along_z)
        self.width = width
        self.real_tokens = real_tokens
        self.tokens = -(-real_tokens // 128) * 128
        self.rows = rows
        self.chip_rows = 2 * rows
        self.block = block
        self.group = 4 * block
        self.heads = width // HD
        self.queries = PAD * self.heads
        self.extra = extra
        self.packed = 2 * width + extra + 4 * self.group
        self.row_pad = -(-rows // 16) * 16
        self.fold = 1 if rows % 16 == 0 else 2
        self.tiles = 4 * (self.queries // 128) + 2 * (self.queries % 128 // 64)
        self.near = 2 if along_z else 3
        self.sums = {}
        self.c_r1 = self.c_r2 = None

    def scratch(self):
        d, n, r, g, b, cr = self.width, self.tokens, self.queries, self.group, self.block, self.chip_rows
        c1, c2 = 2 * d + 2 * self.extra, 2 * d
        v = pltpu.VMEM
        return dict(
            pk=v((2, self.row_pad, self.packed), BF16),
            pr=v((self.row_pad, self.packed), BF16),
            w1=v((2, 16 * cr, d), BF16),
            w2=v((2, 16 * cr, d), BF16),
            mf=v((4, cr, g), BF16),
            fa=v((4, 4, cr, g), BF16),
            wp=v((4, b, d), BF16),
            vecs=v((8, d), F32),
            bias=v((8, g), F32),
            xp=v((n, d), BF16),
            xh=v((n, d), F32),
            inv=v((n, 128), F32),
            a=v((n, d), BF16),
            p32=v((r, n), F32),
            lh=v((2 * r + 2 * PAD, n), BF16),
            rh=v((2 * r + 2 * PAD, d), BF16),
            ci=v((8, PAD, d), BF16),
            hpf=v((8, PAD, d), F32),
            hps=v((8, PAD, d), BF16),
            hr=v((7, PAD, d), BF16),
            dcf=v((8, PAD, d), F32),
            dcs=v((8, PAD, d), BF16),
            dcr=v((7, PAD, d), BF16),
            u=v((8 * PAD, g), F32),
            mt=v((4, b, 8 * PAD), BF16),
            mtr=v((4, b, 8 * PAD), BF16),
            gff=v((4, 4, cr, g), F32),
            gfb=v((4, 4, cr, g), BF16),
            gfr=v((3, 4, cr, g), BF16),
            gf2=v((4, cr, g), BF16),
            gf3=v((4, cr, g), F32),
            gf3r=v((4, cr, g), BF16),
            gf4=v((4, self.rows, g), F32),
            in1t=v((self.tiles, 4, cr, 128), BF16),
            in1r=v((4, self.tiles, cr, 128), BF16),
            in2t=v((self.tiles, 4, cr, 128), BF16),
            in2r=v((4, self.tiles, cr, 128), BF16),
            ag=v((4, PAD, d), BF16),
            wg=v((4, PAD, d), BF16),
            dqg=v((4, PAD, d), BF16),
            pg=v((4, PAD, d), BF16),
            og=v((4, PAD, d), BF16),
            in3t=v((4, 4, cr, 8 * PAD), BF16),
            in4t=v((4, 4, cr, 8 * PAD), BF16),
            r1f=v((4, cr, c1), F32),
            r1p=v((4, self.rows, c1), F32),
            r1s=v((4, self.rows, c1), F32),
            r1b=v((4, self.fold * self.rows, c1 // self.fold), BF16),
            r1r=v((3, self.fold * self.rows, c1 // self.fold), BF16),
            r2f=v((4, cr, c2), F32),
            r2p=v((4, self.rows, c2), F32),
            r2s=v((4, self.rows, c2), F32),
            r2b=v((4, self.fold * self.rows, c2 // self.fold), BF16),
            r2r=v((3, self.fold * self.rows, c2 // self.fold), BF16),
            da=v((n, d), F32),
            gp=v((n, d), F32),
            dxs=v((self.real_tokens, d), F32),
            g2=v((8, PAD, d), F32),
            dbs=v((8, g), F32),
            dbr=v((3, 8, g), F32),
        )


def shared_scratch(ti, tt):
    v = pltpu.VMEM
    e = tt.width
    rows = 32 * PAD
    return dict(
        vb=v((2, 16, PAD, 128), BF16),
        w3=v((2, ti.width, ti.extra), BF16),
        eb=v((2, 2, 16, PAD, e), BF16),
        gtxt=v((rows, rows), F32),
        gimg=v((rows, rows), F32),
        drb=v((8, PAD, e), BF16),
        va=v((8, ti.width + tt.width), F32),
        var=v((8, ti.width + tt.width), F32),
        vs=v((16, 8, 128), F32),
        vl=v((16, 8, 128), F32),
    )


class Group:
    def __init__(self, step):
        self.step = step
        self.index = step.used
        step.used += 1
        step.groups.append(self)

    def copy(self, src, dst, mask):
        return pltpu.make_async_remote_copy(
            src_ref=src,
            dst_ref=dst,
            send_sem=self.step.ssem.at[self.index],
            recv_sem=self.step.rsem.at[self.index],
            device_id=(self.step.at_peer(mask),),
            device_id_type=pl.DeviceIdType.MESH,
        )

    def send(self, src, dst, mask):
        self.copy(src, dst, mask).start()

    def wait(self, view):
        self.view = view
        self.copy(view, view, 1).wait_recv()

    def finish(self):
        self.copy(self.view, self.view, 1).wait_send()


class Gather:
    def __init__(self, step, slot, span, whole, relay):
        self.step, self.slot, self.span, self.whole, self.relayed = step, slot, span, whole, relay
        self.own = self.step.chip

    def chip(self, mask):
        return self.step.at_peer(mask) // 2

    def spread(self, group, chip):
        here = self.slot(chip)
        for mask in PLANE_PEERS[:2] if self.relayed else PLANE_PEERS:
            group.send(here, here, mask)

    def begin_z(self):
        self.g_z = Group(self.step)
        here = self.slot(self.own)
        for mask in Z_PEERS:
            self.g_z.send(here, here, mask)

    def begin_plane(self):
        self.g_own = Group(self.step)
        self.spread(self.g_own, self.own)

    def middle(self):
        self.g_z.wait(self.span(3))
        self.g_mid = Group(self.step)
        for mask in Z_PEERS:
            self.spread(self.g_mid, self.chip(mask))

    def hand_on(self, mask):
        for half, near, to in ((0, 2, 4), (1, 4, 2)):
            there = self.slot(self.chip(near | mask), half)
            self.g_relay.send(there, there, to)

    def relay_own(self):
        self.g_own.wait(self.span(2))
        self.g_relay = Group(self.step)
        self.hand_on(0)

    def relay(self):
        self.g_mid.wait(self.span(6))
        for mask in Z_PEERS:
            self.hand_on(mask)

    def end(self):
        if self.relayed:
            self.g_relay.wait(self.span(4))
        else:
            self.g_own.wait(self.span(3))
            self.g_mid.wait(self.span(9))
        self.g_core = Group(self.step)
        self.g_core.send(self.whole, self.whole, 1)

    def done(self):
        self.g_core.wait(self.whole)


class Step:
    def __init__(self, ti, tt, images):
        self.ti, self.tt, self.images = ti, tt, images
        me = lax.axis_index("dp")
        self.bits = [lax.rem(me // (1 << bit), 2) for bit in range(5)]
        self.me = me
        self.core = lax.rem(me, 2)
        self.chip = me // 2
        self.plane = lax.rem(me // 2, 4)
        self.zed = me // 8
        for t in (ti, tt):
            t.ff.stand(self)
            t.at.stand(self)
        self.used = 0
        self.groups = []

    def at_peer(self, mask):
        total = 0
        for bit in range(5):
            value = 1 - self.bits[bit] if mask >> bit & 1 else self.bits[bit]
            total = total + value * (1 << bit)
        return total

    def barrier(self):
        semaphore = pltpu.get_barrier_semaphore()
        for mask in ALL_PEERS:
            pl.semaphore_signal(
                semaphore, inc=1, device_id=(self.at_peer(mask),), device_id_type=pl.DeviceIdType.MESH
            )
        pl.semaphore_wait(semaphore, len(ALL_PEERS))

    def row_gather(self, buffer, rows):
        cols = buffer.shape[2] // 2

        def slot(chip, half=None):
            at = pl.ds(pl.multiple_of(chip * rows, 16), rows)
            if half is None:
                return buffer.at[self.core, at]
            return buffer.at[self.core, at, half * cols : (half + 1) * cols]

        return Gather(
            self, slot, lambda count: buffer.at[self.core, 0 : count * rows], buffer.at[self.core], True
        )

    def line_gather(self, split, buffer):
        group = Group(self)
        here = buffer.at[split.spot]
        for mask in split.line_peers:
            group.send(here, here, mask)
        return group

    def line_scatter(self, split, parts, landing):
        group = Group(self)
        for slot, mask in enumerate(split.line_peers):
            peer = self.at_peer(mask)
            group.send(parts.at[lax.rem(peer, 2) * 4 + split.group_of(peer)], landing.at[slot], mask)
        return group

    def to_group(self, split, block, landing):
        group = Group(self)
        for mask in split.group_peers:
            group.send(block.at[:, split.group_of(self.at_peer(mask))], landing.at[split.g], mask)
        landing[split.g] = block[:, split.g]
        return group

    def share_group(self, split, buffer, values):
        group = Group(self)
        buffer[split.g] = values
        here = buffer.at[split.g]
        for mask in split.group_peers:
            group.send(here, here, mask)
        return group

    def to_copies(self, split, block, landing):
        group = Group(self)
        for slot, mask in enumerate(split.copy_peers):
            group.send(block.at[split.copy_of(self.at_peer(mask))], landing.at[slot], mask)
        return group

    def run(self):
        ti, tt = self.ti, self.tt
        both = (ti, tt)
        self.pack(ti)
        self.pack(tt)
        self.pack_vectors()
        self.barrier()
        for t in both:
            t.pair = Group(self)
            t.pair.send(t.pk.at[1 - self.core], t.pr, 1)
        vb, eb = self.vb, self.eb
        vectors = Gather(
            self,
            lambda chip: vb.at[self.core, chip],
            lambda count: vb.at[self.core, 0:count],
            vb.at[self.core],
            False,
        )
        vectors.begin_z()
        vectors.begin_plane()
        for t in both:
            t.first = self.row_gather(t.w1, t.chip_rows)
            t.second = self.row_gather(t.w2, t.chip_rows)
        third = self.row_gather(self.w3, ti.chip_rows)
        for t in both:
            self.merge(t)
            t.first.begin_z()
            t.first.begin_plane()
        for t in both:
            t.second.begin_z()
        for t in both:
            self.widen_begin(t)
        third.begin_z()
        for t in both:
            self.narrow_begin(t)
        self.standardize(tt)
        vectors.middle()
        self.standardize(ti)
        for t in both:
            t.first.relay_own()
        for t in both:
            t.second.begin_plane()
        for t in both:
            t.first.middle()
        for t in both:
            t.first.relay()
        vectors.end()
        for t in both:
            t.second.relay_own()
        vectors.done()
        self.unpack_vectors()
        self.queries(ti)
        self.queries(tt)
        for t in both:
            t.second.middle()
        for t in both:
            t.first.end()
        third.begin_plane()
        for t in both:
            self.widen_middle(t)
        for t in both:
            t.second.relay()
        for t in both:
            t.first.done()
            self.attend(t)
            self.early_operands(t)
        third.middle()
        third.relay_own()
        for t in both:
            t.second.end()
        third.relay()
        for t in both:
            t.second.done()
            self.mix(t)
        for t in both:
            self.narrow_middle(t)
        for t in both:
            self.widen_relay(t)
        third.end()
        for t in both:
            t.c_o = self.share_group(t.at, t.og, t.o)
        for t in both:
            self.feed(t)
        third.done()
        for t in both:
            self.embed(t)
        rows = Gather(
            self,
            lambda chip: eb.at[:, self.core, chip],
            lambda count: eb.at[:, self.core, 0:count],
            eb.at[:, self.core],
            False,
        )
        rows.begin_z()
        rows.begin_plane()
        ti.c_p = self.share_group(ti.at, ti.pg, self.pooled)
        rows.middle()
        rows.end()
        rows.done()
        self.contrast()
        for t in both:
            self.feed_back(t)
        for t in both:
            self.feed_weights(t)
        for t in both:
            self.feed_proj(t)
        for t in both:
            self.attend_back(t)
        for t in both:
            self.attend_back_end(t)
        for t in both:
            self.input_gradient(t)
        self.vector_sum_begin()
        for t in both:
            self.round_one(t)
        self.vector_sum_spread()
        for t in both:
            self.feed_weights_middle(t)
        for t in both:
            self.round_spread(t, 0)
        for t in both:
            self.round_two(t)
        for t in both:
            self.round_spread(t, 1)
        for t in both:
            self.feed_weights_end(t)
        self.vector_sum_done()
        for t in both:
            self.round_end(t, 0)
        for t in both:
            self.feed_weights_done(t)
        for t in both:
            self.round_end(t, 1)
        for t in both:
            self.copy_out(t).wait()
        for group in self.groups:
            group.finish()

    def pack(self, t):
        pk, qkv, out, fc = t.pk, t.qkv, t.out, t.fc
        d, b = t.width, t.block
        pad = t.row_pad - t.rows

        def padded(values):
            values = values.astype(F32)
            if pad:
                values = jnp.concatenate([values, jnp.zeros((pad, values.shape[1]), F32)], 0)
            return values.astype(BF16)

        pk[0, :, 0:d] = padded(qkv[:, 0:d])
        pk[1, :, 0:d] = padded(qkv[:, d : 2 * d])
        pk[0, :, d : 2 * d] = padded(qkv[:, 2 * d : 3 * d])
        pk[1, :, d : 2 * d] = padded(out[...])
        if t.extra:
            for half in range(2):
                cols = slice(half * t.extra, (half + 1) * t.extra)
                pk[half, :, 2 * d : 2 * d + t.extra] = padded(self.map[:, cols])
        base = 2 * d + t.extra
        values = padded(fc[...]).astype(F32)
        for half in range(2):
            for group in range(4):
                pieces = []
                for copy in range(4):
                    device = t.ff.device_of(group, copy, half)
                    pieces.append(values[:, b * device : b * (device + 1)])
                start = base + group * t.group
                pk[half, :, start : start + t.group] = jnp.concatenate(pieces, 1).astype(BF16)

    def pack_vectors(self):
        def widen(values, at):
            values = values.astype(F32)
            parts = [values, jnp.zeros((values.shape[0], 128 - at - values.shape[1]), F32)]
            if at:
                parts = [jnp.zeros((values.shape[0], at), F32)] + parts
            return jnp.concatenate(parts, 1)

        top = widen(self.ti.vec[...], 0) + widen(self.tt.vec[...], 32)
        row = iota((8, 128), 0)
        bottom = jnp.where(row == 0, widen(self.ti.fcb[...], 0), 0.0)
        bottom = bottom + jnp.where(row == 1, widen(self.tt.fcb[...], 0), 0.0)
        block = jnp.concatenate([top, bottom], 0)
        row, lane = iota((PAD, 128), 0), iota((PAD, 128), 1)
        for caption in range(self.images):
            image = self.match[caption]
            device = image // self.images
            high = lax.rem(device, 2) * 16 + device // 2
            low = image - device * self.images
            block = jnp.where((row == caption) & (lane == 120), high.astype(F32), block)
            block = jnp.where((row == caption) & (lane == 121), low.astype(F32), block)
        self.vb[self.core, self.chip] = block.astype(BF16)

    def unpack_vectors(self):
        vb = self.vb
        for core in range(2):
            for chip in range(16):
                block = vb[core, chip].astype(F32)
                device = 2 * chip + core
                for t, at in ((self.ti, 0), (self.tt, 32)):
                    rows = t.rows
                    t.vecs[:, rows * device : rows * (device + 1)] = block[0:8, at : at + rows]
        for t, row in ((self.ti, 8), (self.tt, 9)):
            for copy in range(4):
                block = vb[self.core, t.ff.chip_of(t.ff.g, copy)].astype(F32)
                b = t.block
                t.bias[0:1, b * copy : b * (copy + 1)] = block[row : row + 1, 0:b]

    def standardize(self, t):
        x, xp, xh, inv = t.x, t.xp, t.xh, t.inv
        step = STEP_ROWS
        full = t.real_tokens // step

        def norm(hidden, rows):
            xp[rows, :] = hidden.astype(BF16)
            centred = hidden - jnp.mean(hidden, -1, keepdims=True)
            inverse = lax.rsqrt(jnp.mean(centred * centred, -1, keepdims=True) + 1e-05)
            xh[rows, :] = centred * inverse
            inv[rows, :] = jnp.broadcast_to(inverse, (step, 128))

        def body(index, carry):
            rows = pl.ds(pl.multiple_of(index * step, step), step)
            norm(x[rows, :].astype(F32), rows)
            return carry

        lax.fori_loop(0, full, body, 0)
        start, rest = full * step, t.real_tokens - full * step
        if rest:
            last = x[start : t.real_tokens, :].astype(F32)
            last = jnp.concatenate([last, jnp.zeros((step - rest, t.width), F32)], 0)
            norm(last, slice(start, start + step))
            start += step
        while start < t.tokens:
            norm(jnp.zeros((step, t.width), F32), slice(start, start + step))
            start += step

    def merge(self, t):
        t.pair.wait(t.pr)
        pk, pr = t.pk, t.pr
        d, g = t.width, t.group
        rows = pl.ds(pl.multiple_of(self.chip * t.chip_rows, 16), t.chip_rows)
        first = self.core == 0

        def merged(cols):
            own = pk[self.core, :, cols].astype(F32)
            got = pr[:, cols].astype(F32)
            upper = jnp.where(first, own, got)[: t.rows]
            lower = jnp.where(first, got, own)[: t.rows]
            return jnp.concatenate([upper, lower], 0).astype(BF16)

        t.w1[self.core, rows, :] = merged(slice(0, d))
        t.w2[self.core, rows, :] = merged(slice(d, 2 * d))
        base = 2 * d
        if t.extra:
            self.w3[self.core, rows, :] = merged(slice(base, base + t.extra))
            base += t.extra
        for group in range(4):
            t.mf[group] = merged(slice(base + group * g, base + (group + 1) * g))

    def widen_begin(self, t):
        t.widen = Group(self)
        for mask in t.ff.group_peers:
            t.widen.send(t.mf.at[t.ff.group_of(self.at_peer(mask))], t.fa.at[self.zed, self.plane], mask)
        t.fa[self.zed, self.plane] = t.mf[t.ff.g]

    def widen_middle(self, t):
        t.widen.wait(t.mf.at[0:3])
        t.widen = Group(self)
        part = t.ff.chips_of_copy(t.fa, t.ff.r)
        for mask in t.ff.copy_peers[: t.near]:
            t.widen.send(part, part, mask)

    def narrow_begin(self, t):
        t.narrow = Group(self)
        for mask in t.ff.copy_peers[: t.near]:
            t.narrow.send(t.proj, t.wp.at[t.ff.r], mask)
        t.wp[t.ff.r] = t.proj[...]

    def narrow_middle(self, t):
        t.narrow.wait(t.wp.at[0 : t.near])
        if t.ff.along_z:
            t.narrow_far, half = Group(self), t.block // 2
            for part, near, to in ((0, 2, 4), (1, 4, 2)):
                rows = pl.ds(part * half, half)
                there = t.wp.at[t.ff.copy_of(self.at_peer(near)), rows]
                t.narrow_far.send(there, there, to)

    def widen_relay(self, t):
        t.widen.wait(t.fa.at[0 : t.near])
        if t.ff.along_z:
            t.widen_far = Group(self)
            for part, near, to in ((0, 2, 4), (1, 4, 2)):
                there = t.fa.at[2 * part : 2 * part + 2, t.ff.copy_of(self.at_peer(near))]
                t.widen_far.send(there, there, to)

    def queries(self, t):
        a, xh, vec = t.a, t.xh, t.vecs
        step = STEP_ROWS

        def body(index, carry):
            rows = pl.ds(pl.multiple_of(index * step, step), step)
            a[rows, :] = (xh[rows, :] * vec[0:1, :] + vec[1:2, :]).astype(BF16)
            return carry

        lax.fori_loop(0, t.tokens // step, body, 0)
        n = t.tokens
        row, token = iota((PAD, n), 0), iota((PAD, n), 1)
        if t is self.ti:
            real = row < self.images
            at = jnp.where(real, row * TOK_I, -1)
            low, high = jnp.where(real, row * TOK_I, -1), jnp.where(real, (row + 1) * TOK_I, -1)
        else:
            counts = self.counts
            column = iota((PAD, 1), 0)
            low, high = jnp.full((PAD, 1), -1, jnp.int32), jnp.full((PAD, 1), -1, jnp.int32)
            for line in range(counts.shape[0]):
                end = line * TOK_T
                for member in range(CAP_ROW):
                    begin, end = end, end + counts[line, member]
                    chosen = column == line * CAP_ROW + member
                    low, high = jnp.where(chosen, begin, low), jnp.where(chosen, end, high)
            at = jnp.where(high > 0, high - 1, -1)
        chosen = (token == at).astype(F32).astype(BF16)
        lh, r = t.lh, t.queries
        lh[2 * r : 2 * r + PAD, :] = chosen
        lh[2 * r + PAD : 2 * r + 2 * PAD, :] = chosen
        t.seen = ((token >= low) & (token < high)).astype(F32)
        t.x0 = dot(chosen, t.xp[...])
        t.a0 = dot(chosen, a[...]).astype(BF16)

    def attend(self, t):
        w1, vec, a, r = t.w1, t.vecs, t.a, t.queries
        t.q = (dot(t.a0, w1[0]) + vec[2:3, :]).astype(BF16)
        qt = dot_nt(expand_heads(t.q), w1[1]).astype(BF16)
        t.rh[0:r, :] = qt
        scores = dot_nt(qt, a[...]) * 0.125
        seen = jnp.concatenate([t.seen] * t.heads, 0) > 0.5
        scores = jnp.where(seen, scores, -1000000000.0)
        top = jnp.max(scores, -1, keepdims=True)
        raw = jnp.where(seen, jnp.exp(scores - top), 0.0)
        total = jnp.sum(raw, -1, keepdims=True)
        probs = raw / jnp.where(total > 0.0, total, 1.0)
        t.p32[...] = probs
        low = probs.astype(BF16)
        t.lh[r : 2 * r, :] = low
        t.pa = dot(low, a[...])

    def mix(self, t):
        w2, vec = t.w2, t.vecs
        context = (join_heads(dot(t.pa.astype(BF16), w2[0])) + vec[3:4, :]).astype(BF16)
        t.o = context
        t.h1 = t.x0 + (dot(context, w2[1]) + vec[4:5, :])
        t.xh2, t.inv2, second = small_norm(t.h1, vec[5:6, :], vec[6:7, :])
        t.ci[t.ff.spot] = second.astype(BF16)
        t.line = self.line_gather(t.ff, t.ci)

    def feed(self, t):
        d, g = t.width, t.group
        if t.ff.along_z:
            t.widen_far.wait(t.fa.at[0])
            t.narrow_far.wait(t.wp.at[0])
        t.line.wait(t.ci.at[0:7])
        c = t.ci[...].reshape(8 * PAD, d)
        up = dot(c, t.fa[...].reshape(d, g)) + t.bias[0:1, :]
        active = up * jax.nn.sigmoid(1.702 * up)
        t.u[...] = up
        t.mt[...] = active.T.astype(BF16).reshape(t.mt.shape)
        active = active.astype(BF16)
        part = dot(active, t.wp[...].reshape(g, d)).reshape(8, PAD, d)
        t.hpf[...] = part
        t.hps[...] = part.astype(BF16)
        t.line = self.line_scatter(t.ff, t.hps, t.hr)
        t.mtr[t.ff.r] = t.mt[t.ff.r]
        t.c_m = Group(self)
        for mask in t.ff.copy_peers:
            t.c_m.send(t.mt.at[t.ff.copy_of(self.at_peer(mask))], t.mtr.at[t.ff.r], mask)

    def line_total(self, t, own, landing):
        t.line.wait(landing)
        total = own[t.ff.spot]
        for slot in range(7):
            total = total + landing[slot].astype(F32)
        return total

    def embed(self, t):
        hidden = t.h1 + (self.line_total(t, t.hpf, t.hr) + t.vecs[7:8, :])
        which = 1
        raw = hidden
        if t is self.ti:
            which = 0
            self.pooled = hidden.astype(BF16)
            raw = jnp.concatenate([dot(self.pooled, self.w3[0]), dot(self.pooled, self.w3[1])], 1)
        scale = lax.rsqrt(jnp.sum(raw * raw, -1, keepdims=True) + 1e-06)
        row, lane = iota(raw.shape, 0), iota(raw.shape, 1)
        across = col_sum(jnp.where(row == lane, scale, 0.0))
        high = across.astype(BF16).astype(F32)
        block = jnp.where(row == self.images, high, raw * scale)
        block = jnp.where(row == self.images + 1, across - high, block)
        self.eb[which, self.core, self.chip] = block.astype(BF16)

    def by_rows(self, t, values, buffer):
        turned = values.T.reshape(4, 4, t.chip_rows, t.queries)
        whole = t.queries // 128
        for tile in range(whole):
            part = turned[:, :, :, 128 * tile : 128 * (tile + 1)].astype(BF16)
            for copy in range(4):
                buffer[4 * tile + copy] = part[:, copy] if t.at.along_z else part[copy]
        if t.queries % 128:
            rest = turned[:, :, :, 128 * whole :]
            for pair in range(2):
                if t.at.along_z:
                    parts = [rest[:, 2 * pair], rest[:, 2 * pair + 1]]
                else:
                    parts = [rest[2 * pair], rest[2 * pair + 1]]
                buffer[4 * whole + pair] = jnp.concatenate(parts, 2).astype(BF16)

    def times_heads(self, t, landing, rows, out, start):
        cr, d = t.chip_rows, t.width
        whole = t.queries // 128
        total, paired = 0.0, 0.0
        for group in range(4):
            wide = expand_heads(rows[PAD * group : PAD * (group + 1)])
            for tile in range(whole):
                operand = landing[group, 4 * tile : 4 * (tile + 1)].reshape(4 * cr, 128)
                total = total + dot(operand, wide[128 * tile : 128 * (tile + 1)])
            if t.queries % 128:
                rest = wide[128 * whole :]
                blank = jnp.zeros_like(rest)
                rest = jnp.concatenate(
                    [jnp.concatenate([rest, blank], 0), jnp.concatenate([blank, rest], 0)], 1
                )
                paired = paired + dot(landing[group, 4 * whole : 4 * whole + 2].reshape(2 * cr, 128), rest)
        for z in range(4):
            values = total[cr * z : cr * (z + 1)]
            if t.queries % 128:
                pair = paired[cr * (z // 2) : cr * (z // 2 + 1)]
                values = values + pair[:, d * (z % 2) : d * (z % 2 + 1)]
            out[z, :, start : start + d] = values

    def early_operands(self, t):
        self.by_rows(t, t.pa, t.in1t)
        t.c_in1 = self.to_group(t.at, t.in1t, t.in1r)
        t.c_a = self.share_group(t.at, t.ag, t.a0)

    def contrast(self):
        eb, gtxt, gimg = self.eb, self.gtxt, self.gimg
        size = 32 * PAD
        total = self.images * 32
        e_img, e_txt = eb[0].reshape(size, eb.shape[-1]), eb[1].reshape(size, eb.shape[-1])
        sharp = jnp.exp(jnp.full((8, 128), self.sharp[0], F32))[0:1, 0:1]
        logits = sharp * dot_nt(e_txt, e_img)
        marks = self.vb[...].reshape(size, 128).astype(F32)
        target = marks[:, 120:121] * float(PAD) + marks[:, 121:122]
        row, col = iota((size, size), 0), iota((size, size), 1)
        real = (lax.rem(row, PAD) < self.images) & (lax.rem(col, PAD) < self.images)
        hit = real & (col.astype(F32) == target)
        powers = jnp.where(real, jnp.exp(logits), 0.0)
        row_sum, col_sums = jnp.sum(powers, 1, keepdims=True), col_sum(powers)
        real_line = lax.rem(iota((size, 1), 0), PAD) < self.images
        real_lane = lax.rem(iota((1, size), 1), PAD) < self.images
        row_sum, col_sums = jnp.where(real_line, row_sum, 1.0), jnp.where(real_lane, col_sums, 1.0)
        grad = powers * ((1.0 / row_sum + 1.0 / col_sums) * (0.5 / total))
        grad = grad - jnp.where(hit, 1.0 / total, 0.0)
        safe = jnp.where(real, logits, 0.0)
        logs = jnp.sum(jnp.log(row_sum), 0, keepdims=True) + jnp.sum(jnp.log(col_sums), 1, keepdims=True)

        def whole(values):
            return jnp.sum(jnp.sum(values, 1, keepdims=True), 0, keepdims=True)

        self.loss[...] = logs * (0.5 / total) - whole(jnp.where(hit, safe, 0.0)) * (1.0 / total)
        self.dls[...] = whole(grad * safe)
        gtxt[...] = grad
        gimg[...] = grad.T
        for t in (self.ti, self.tt):
            d_raw = self.raw_gradient(t, t.ff.r)
            if t is self.ti:
                d_raw, rounded = self.through_map(d_raw)
                self.drb[...] = rounded.reshape(self.drb.shape)
            t.g2[...] = d_raw.reshape(t.g2.shape)

    def raw_gradient(self, t, copy):
        eb = self.eb
        which, rows, others = (0, self.gimg, eb[1]) if t is self.ti else (1, self.gtxt, eb[0])
        others = others.reshape(32 * PAD, eb.shape[-1])
        sharp = jnp.exp(jnp.full((8, 128), self.sharp[0], F32))[0:1, 0:1]
        parts, units, scales = [], [], []
        for core in range(2):
            for group in range(4):
                chip = t.ff.chip_of(group, copy)
                start = (core * 16 + chip) * PAD
                if not isinstance(start, int):
                    start = pl.multiple_of(start, PAD)
                parts.append(rows[pl.ds(start, PAD), :])
                block = eb[which, core, chip].astype(F32)
                units.append(block)
                row, lane = iota((PAD, 128), 0), iota((PAD, 128), 1)
                spare = (row >= self.images) & (row < self.images + 2)
                across = col_sum(jnp.where(spare, block[:, 0:128], 0.0))
                scales.append(jnp.sum(jnp.where(row == lane, across, 0.0), 1, keepdims=True))
        part, unit, scale = (jnp.concatenate(pieces, 0) for pieces in (parts, units, scales))
        high, low = split_two(part)
        d_unit = sharp * (dot(high, others) + dot(low, others))
        return scale * (d_unit - unit * jnp.sum(d_unit * unit, -1, keepdims=True))

    def through_map(self, d_raw):
        w3, half = self.w3, self.ti.extra
        rounded = d_raw.astype(BF16)
        return dot_nt(rounded[:, 0:half], w3[0]) + dot_nt(rounded[:, half : 2 * half], w3[1]), rounded

    def feed_back(self, t):
        d, g = t.width, t.group
        t.y = t.g2[...].reshape(8 * PAD, d).astype(BF16)
        up = t.u[...]
        gate = jax.nn.sigmoid(1.702 * up)
        d_active = dot_nt(t.y, t.wp[...].reshape(g, d))
        t.du = (d_active * (gate + 1.702 * up * gate * (1.0 - gate))).astype(BF16)
        part = dot_nt(t.du, t.fa[...].reshape(d, g)).reshape(8, PAD, d)
        t.dcf[...] = part
        t.dcs[...] = part.astype(BF16)
        t.line = self.line_scatter(t.ff, t.dcs, t.dcr)

    def feed_weights(self, t):
        d, g, cr = t.width, t.group, t.chip_rows
        grad = dot_tn(t.ci[...].reshape(8 * PAD, d), t.du).reshape(4, 4, cr, g)
        t.gff[...] = grad
        t.gfb[...] = grad.astype(BF16)
        t.c_wide, t.c_bias = Group(self), Group(self)
        t.dbs[...] = jnp.broadcast_to(col_sum(t.du.astype(F32)), (8, g))
        for slot, mask in enumerate(t.ff.copy_peers):
            copy = t.ff.copy_of(self.at_peer(mask))
            t.c_wide.send(t.ff.chips_of_copy(t.gfb, copy), t.gfr.at[slot], mask)
            t.c_bias.send(t.dbs, t.dbr.at[slot], mask)

    def feed_proj(self, t):
        t.c_m.wait(t.mtr.at[0:3])
        total = 0.0
        for copy in range(4):
            d_raw = self.raw_gradient(t, copy)
            if t is self.ti:
                d_raw = self.through_map(d_raw)[0]
            total = total + dot(t.mtr[copy], d_raw.astype(BF16))
        t.d_proj[...] = total

    def feed_weights_middle(self, t):
        b = t.block
        t.c_wide.wait(t.gfr)
        total = t.ff.chips_of_copy(t.gff, t.ff.r)[...]
        for slot in range(3):
            total = total + t.gfr[slot].astype(F32)
        t.gf2[...] = total.astype(BF16)
        t.gf3[...] = total
        t.c_line = Group(self)
        for mask in t.ff.group_peers:
            t.c_line.send(t.gf2.at[t.ff.group_of(self.at_peer(mask))], t.gf3r.at[t.ff.g], mask)
        t.c_bias.wait(t.dbr)
        bias = t.dbs[0:1, :]
        for slot in range(3):
            bias = bias + t.dbr[slot, 0:1, :]
        mine = jnp.zeros((1, b), F32)
        for copy in range(4):
            mine = jnp.where(t.ff.r == copy, bias[:, b * copy : b * (copy + 1)], mine)
        t.d_fcb[...] = mine

    def feed_weights_end(self, t):
        t.c_line.wait(t.gf2.at[0:3])
        own = t.gf3[t.ff.g]
        for group in range(4):
            t.gf3[group] = jnp.where(t.ff.g == group, own, t.gf3r[group].astype(F32))
        start = pl.multiple_of((1 - self.core) * t.rows, 8)
        t.c_fc = Group(self)
        t.c_fc.send(t.gf3.at[:, pl.ds(start, t.rows)], t.gf4, 1)

    def attend_back(self, t):
        vec = t.vecs
        total = self.line_total(t, t.dcf, t.dcr)
        g2 = t.g2[t.ff.spot]
        t.g1 = g2 + small_norm_back(total, t.xh2, t.inv2, vec[5:6, :])
        branch = t.g1.astype(BF16)
        t.do = dot_nt(branch, t.w2[1]).astype(BF16)
        t.sums.update(
            dbv=col_sum(t.do.astype(F32)),
            dbo=col_sum(branch.astype(F32)),
            dg2=col_sum(total * t.xh2),
            db2=col_sum(total),
            dbp=col_sum(g2.astype(BF16).astype(F32)),
        )
        t.c_w = self.share_group(t.at, t.wg, branch)

    def attend_back_end(self, t):
        r, w1, a, lh, rh = t.queries, t.w1, t.a, t.lh, t.rh
        dvt = dot_nt(expand_heads(t.do), t.w2[0]).astype(BF16)
        rh[r : 2 * r, :] = dvt
        d_probs = dot_nt(dvt, a[...])
        probs = t.p32[...]
        weighted = probs * d_probs
        d_scores = (weighted - probs * jnp.sum(weighted, -1, keepdims=True)).astype(BF16)
        d_scores = (d_scores.astype(F32) * 0.125).astype(BF16)
        lh[0:r, :] = d_scores
        moved = dot(d_scores, a[...])
        self.by_rows(t, moved, t.in2t)
        t.c_in2 = self.to_group(t.at, t.in2t, t.in2r)
        d_query = join_heads(dot(moved.astype(BF16), w1[1])).astype(BF16)
        t.c_dq = self.share_group(t.at, t.dqg, d_query)
        t.sums.update(dbq=col_sum(d_query.astype(F32)))
        high, low = split_two(dot_nt(d_query, w1[0]))
        rh[2 * r : 2 * r + PAD, :] = high
        rh[2 * r + PAD : 2 * r + 2 * PAD, :] = low

    def copy_out(self, t):
        return pltpu.make_async_copy(t.dxs, t.d_x, self.osem.at[0 if t is self.ti else 1])

    def input_gradient(self, t):
        r, d = t.queries, t.width
        lh, da, gp, xh, inv, vec, out = t.lh, t.da, t.gp, t.xh, t.inv, t.vecs, t.dxs
        da[...] = dot_tn(lh[...], t.rh[...])
        high, low = split_two(t.g1)
        gp[...] = dot_tn(lh[2 * r : 2 * r + 2 * PAD, :], jnp.concatenate([high, low], 0))
        step = STEP_ROWS
        full = t.real_tokens // step

        def one(rows, carry):
            z, normed = da[rows, :], xh[rows, :]
            inner = small_norm_back(z, normed, inv[rows, 0:1], vec[0:1, :])
            return inner + gp[rows, :], (
                carry[0] + jnp.sum((z * normed).reshape(step // 8, 8, d), 0),
                carry[1] + jnp.sum(z.reshape(step // 8, 8, d), 0),
            )

        def body(index, carry):
            rows = pl.ds(pl.multiple_of(index * step, step), step)
            out[rows, :], carry = one(rows, carry)
            return carry

        zero = jnp.zeros((8, d), F32)
        carry = lax.fori_loop(0, full, body, (zero, zero))
        start, rest = full * step, t.real_tokens - full * step
        if rest:
            last, carry = one(slice(start, start + step), carry)
            out[start : start + rest, :] = last[:rest]
        self.copy_out(t).start()
        s = t.sums
        rows = [col_sum(carry[0]), col_sum(carry[1])]
        rows += [s.pop(name) for name in list(dict(dbq=0, dbv=0, dbo=0, dg2=0, db2=0, dbp=0))]
        start = 0 if t is self.ti else self.ti.width
        self.va[:, start : start + d] = jnp.concatenate(rows, 0)

    def vector_sum_begin(self):
        self.c_vec = Group(self)
        self.c_vec.send(self.va, self.var, 1)

    def vector_sum_spread(self):
        self.c_vec.wait(self.var)
        total = self.va[...] + self.var[...]
        for chip in range(16):
            pieces, at = [], 0
            for t in (self.ti, self.tt):
                cols = t.chip_rows
                start = at + chip * cols
                pieces += [total[:, start : start + cols], jnp.zeros((8, 64 - cols), F32)]
                at += t.width
            self.vs[chip] = jnp.concatenate(pieces, 1)
        self.c_vec = Group(self)
        for mask in CHIP_PEERS:
            self.c_vec.send(self.vs.at[self.at_peer(mask) // 2], self.vl.at[self.chip], mask)
        self.vl[self.chip] = self.vs[self.chip]

    def vector_sum_done(self):
        self.c_vec.wait(self.vl.at[0:15])
        total = jnp.sum(self.vl[...], 0)
        for t, lane in ((self.ti, 0), (self.tt, 64)):
            rows = t.rows
            halves = [total[:, lane + rows * core : lane + rows * (core + 1)] for core in range(2)]
            t.d_vec[...] = jnp.where(self.core == 0, halves[0], halves[1])

    def turn_members(self, t, first, second, buffer):
        d = t.width
        rows = [part[...].reshape(4 * PAD, d) for part in (first, second)]
        buffer[...] = jnp.concatenate(rows, 0).astype(F32).T.astype(BF16).reshape(buffer.shape)
        return t.at.chips_of_group(buffer, t.at.g)[...].reshape(4 * t.chip_rows, 8 * PAD)

    def round_one(self, t):
        t.c_in1.wait(t.in1r.at[0:3])
        t.c_w.wait(t.wg.at[0:3])
        t.c_o.wait(t.og.at[0:3])
        t.c_a.wait(t.ag.at[0:3])
        d, cr = t.width, t.chip_rows
        members = 4 * PAD
        branch = t.wg[...].reshape(members, d)
        self.times_heads(t, t.in1r, dot_nt(branch, t.w2[1]).astype(BF16), t.r1f, 0)
        t.in3 = self.turn_members(t, t.og, t.ag, t.in3t)
        out = dot(t.in3, jnp.concatenate([branch, jnp.zeros_like(branch)], 0))
        t.r1f[:, :, d : 2 * d] = out.reshape(4, cr, d)
        if t.extra:
            t.c_p.wait(t.pg.at[0:3])
            operand = self.turn_members(t, t.pg, t.pg, t.in4t)
            units = self.drb[pl.ds(self.core * 4, 4)].reshape(members, 2 * t.extra)
            proj = dot(operand, jnp.concatenate([units, jnp.zeros_like(units)], 0))
            t.r1f[:, :, 2 * d :] = proj.reshape(4, cr, 2 * t.extra)
        t.c_r1 = self.round_pair(t, t.r1f, t.r1p)

    def round_two(self, t):
        t.c_in2.wait(t.in2r.at[0:3])
        d, cr = t.width, t.chip_rows
        members = 4 * PAD
        query = dot(t.ag[...].reshape(members, d), t.w1[0]) + t.vecs[2:3, :]
        self.times_heads(t, t.in2r, query.astype(BF16), t.r2f, d)
        t.c_dq.wait(t.dqg.at[0:3])
        d_query = t.dqg[...].reshape(members, d)
        d_query = jnp.concatenate([jnp.zeros_like(d_query), d_query], 0)
        t.r2f[:, :, 0:d] = dot(t.in3, d_query).reshape(4, cr, d)
        t.c_r2 = self.round_pair(t, t.r2f, t.r2p)

    def round_pair(self, t, grad, landing):
        start = pl.multiple_of((1 - self.core) * t.rows, 8)
        group = Group(self)
        group.send(grad.at[:, pl.ds(start, t.rows)], landing, 1)
        return group

    def round_spread(self, t, which):
        group, grad, came, total, packed, landing = (
            (t.c_r1, t.r1f, t.r1p, t.r1s, t.r1b, t.r1r),
            (t.c_r2, t.r2f, t.r2p, t.r2s, t.r2b, t.r2r),
        )[which]
        group.wait(came)
        start = pl.multiple_of(self.core * t.rows, 8)
        values = grad[:, pl.ds(start, t.rows), :] + came[...]
        total[...] = values
        cols = values.shape[2] // t.fold
        pieces = [values[:, :, cols * part : cols * (part + 1)] for part in range(t.fold)]
        packed[...] = jnp.concatenate(pieces, 1).astype(BF16)
        group = self.to_copies(t.at, packed, landing)
        if which:
            t.c_r2 = group
        else:
            t.c_r1 = group

    def round_end(self, t, which):
        group, total, landing = ((t.c_r1, t.r1s, t.r1r), (t.c_r2, t.r2s, t.r2r))[which]
        group.wait(landing)
        arrived = landing[0].astype(F32) + landing[1].astype(F32) + landing[2].astype(F32)
        pieces = [arrived[t.rows * part : t.rows * (part + 1)] for part in range(t.fold)]
        values = total[t.at.r] + jnp.concatenate(pieces, 1)
        d = t.width
        if which:
            t.d_qkv[:, 0 : 2 * d] = values
        else:
            t.d_qkv[:, 2 * d : 3 * d] = values[:, 0:d]
            t.d_out[...] = values[:, d : 2 * d]
            if t.extra:
                self.dmap[...] = values[:, 2 * d :]

    def feed_weights_done(self, t):
        rows, b = t.rows, t.block
        start = pl.multiple_of(self.core * rows, 8)
        t.c_fc.wait(t.gf4)
        for group in range(4):
            own, got = t.gf3[group, pl.ds(start, rows), :], t.gf4[group]
            for half in range(2):
                values = jnp.where(self.core == half, own, got)
                for copy in range(4):
                    device = t.ff.device_of(group, copy, half)
                    t.d_fc[:, b * device : b * (device + 1)] = values[:, b * copy : b * (copy + 1)]


def set_all(target, names, refs):
    for name, ref in zip(names, refs, strict=True):
        setattr(target, name, ref)


def hand_over(results):
    count = len(results)
    cuts = []
    for index, value in enumerate(results):
        rows = value.shape[0]
        step = 120 if rows > 120 and rows % 120 == 0 else rows
        cuts += [(index, start, step) for start in range(0, rows, step)]

    def kernel(*refs):
        came, went = refs[3 * count], refs[3 * count + 1]
        reads, writes = [], []
        for at, (index, start, rows) in enumerate(cuts):
            src, dst, mid = (refs[index + part * count] for part in range(3))
            if rows != src.shape[0]:
                src, dst, mid = (ref.at[start : start + rows] for ref in (src, dst, mid))
            reads.append(pltpu.make_async_copy(src, mid, came.at[at]))
            writes.append(pltpu.make_async_copy(mid, dst, went.at[at]))
        for read in reads:
            read.start()
        for read, write in zip(reads, writes, strict=True):
            read.wait()
            write.start()
        for write in writes:
            write.wait()

    sems = pltpu.SemaphoreType.DMA((len(cuts),))
    return pl.pallas_call(
        kernel,
        out_shape=tuple(jax.ShapeDtypeStruct(value.shape, value.dtype) for value in results),
        in_specs=[pl.BlockSpec(memory_space=pl.ANY)] * count,
        out_specs=tuple([pl.BlockSpec(memory_space=pl.ANY)] * count),
        scratch_shapes=[pltpu.VMEM(value.shape, value.dtype) for value in results] + [sems, sems],
        compiler_params=pltpu.CompilerParams(vmem_limit_bytes=60 * 2**20),
        name="hand_over",
    )(*results)


def local_fused(
    picture_patch_inputs,
    caption_packed_inputs,
    picture_attend_entry_weight,
    picture_attend_exit_weight,
    picture_widening_weight,
    picture_narrowing_weight,
    picture_affine_entries,
    picture_widening_offset,
    caption_attend_entry_weight,
    caption_attend_exit_weight,
    caption_widening_weight,
    caption_narrowing_weight,
    caption_affine_entries,
    caption_widening_offset,
    picture_feature_mapping,
    sharpness_exponent,
    caption_token_counts,
    matching_picture_index,
):
    n_img, d_img = picture_patch_inputs.shape
    n_txt, d_txt = caption_packed_inputs.shape
    images = n_img // TOK_I
    ti = Tower(
        True,
        d_img,
        n_img,
        picture_attend_entry_weight.shape[1],
        picture_widening_offset.shape[1],
        picture_feature_mapping.shape[1] // 2,
    )
    tt = Tower(
        False, d_txt, n_txt, caption_attend_entry_weight.shape[1], caption_widening_offset.shape[1], 0
    )
    img_args = dict(
        x=picture_patch_inputs,
        qkv=picture_attend_entry_weight[0],
        out=picture_attend_exit_weight[0],
        fc=picture_widening_weight[0],
        proj=picture_narrowing_weight[0],
        vec=picture_affine_entries[0],
        fcb=picture_widening_offset,
    )
    txt_args = dict(
        x=caption_packed_inputs,
        qkv=caption_attend_entry_weight[0],
        out=caption_attend_exit_weight[0],
        fc=caption_widening_weight[0],
        proj=caption_narrowing_weight[0],
        vec=caption_affine_entries[0],
        fcb=caption_widening_offset,
    )
    more_args = dict(
        map=picture_feature_mapping,
        sharp=sharpness_exponent.reshape(1),
        counts=caption_token_counts,
        match=matching_picture_index,
    )

    def out(*shape):
        return jax.ShapeDtypeStruct(shape, F32)

    def tower_outs(t):
        return dict(
            d_x=out(t.real_tokens, t.width),
            d_qkv=out(t.rows, 3 * t.width),
            d_out=out(t.rows, t.width),
            d_fc=out(t.rows, 32 * t.block),
            d_proj=out(t.block, t.width),
            d_vec=out(8, t.rows),
            d_fcb=out(1, t.block),
        )

    more_outs = dict(loss=out(1, 1), dls=out(1, 1), dmap=out(ti.rows, 2 * ti.extra))
    in_vmem, in_smem = pl.BlockSpec(memory_space=pltpu.VMEM), pl.BlockSpec(memory_space=pltpu.SMEM)
    anywhere = pl.BlockSpec(memory_space=pl.ANY)
    parts = [
        (ti, img_args, [in_vmem] * 7),
        (tt, txt_args, [in_vmem] * 7),
        (None, more_args, [in_vmem, in_smem, in_smem, in_smem]),
        (ti, tower_outs(ti), [anywhere] + [in_vmem] * 6),
        (tt, tower_outs(tt), [anywhere] + [in_vmem] * 6),
        (None, more_outs, [in_vmem] * 3),
        (ti, ti.scratch(), None),
        (tt, tt.scratch(), None),
        (None, shared_scratch(ti, tt), None),
        (
            None,
            dict(
                ssem=pltpu.SemaphoreType.DMA((N_SEMS,)),
                rsem=pltpu.SemaphoreType.DMA((N_SEMS,)),
                osem=pltpu.SemaphoreType.DMA((2,)),
            ),
            None,
        ),
    ]

    def kernel(*refs):
        step = Step(ti, tt, images)
        at = 0
        for owner, values, _ in parts:
            set_all(step if owner is None else owner, values, refs[at : at + len(values)])
            at += len(values)
        step.run()

    def joined(chosen, field):
        return [item for part in chosen for item in (part[field] if field == 2 else part[field].values())]

    results = pl.pallas_call(
        kernel,
        out_shape=tuple(joined(parts[3:6], 1)),
        in_specs=joined(parts[0:3], 2),
        out_specs=tuple(joined(parts[3:6], 2)),
        scratch_shapes=joined(parts[6:], 1),
        compiler_params=pltpu.CompilerParams(
            collective_id=0, has_side_effects=True, vmem_limit_bytes=60 * 2**20
        ),
        name="contrastive_step",
    )(*joined(parts[0:3], 1))
    results = hand_over(results)
    img, txt, (loss, d_scale, d_map) = results[0:7], results[7:14], results[14:17]
    return (
        loss.reshape(()),
        d_scale.reshape(()),
        img[0],
        txt[0],
        img[1][None],
        img[2][None],
        img[3][None],
        img[4][None],
        img[5][None],
        img[6],
        txt[1][None],
        txt[2][None],
        txt[3][None],
        txt[4][None],
        txt[5][None],
        txt[6],
        d_map,
    )


def solution(mesh):
    placed = (
        P("dp", None),
        P("dp", None),
        P(None, "dp", None),
        P(None, "dp", None),
        P(None, "dp", None),
        P(None, "dp", None),
        P(None, None, "dp"),
        P(None, "dp"),
        P(None, "dp", None),
        P(None, "dp", None),
        P(None, "dp", None),
        P(None, "dp", None),
        P(None, None, "dp"),
        P(None, "dp"),
        P("dp", None),
        P(),
        P("dp", None),
        P("dp"),
    )
    return jax.shard_map(
        local_fused if fits(mesh) else local_plain,
        mesh=mesh,
        in_specs=placed,
        out_specs=(
            P(),
            P(),
            P("dp", None),
            P("dp", None),
            P(None, "dp", None),
            P(None, "dp", None),
            P(None, "dp", None),
            P(None, "dp", None),
            P(None, None, "dp"),
            P(None, "dp"),
            P(None, "dp", None),
            P(None, "dp", None),
            P(None, "dp", None),
            P(None, "dp", None),
            P(None, None, "dp"),
            P(None, "dp"),
            P("dp", None),
        ),
        check_vma=False,
    )
```

```python
import jax
import jax.numpy as jnp
from jax import lax
from jax.experimental import pallas as pl
from jax.experimental.pallas import tpu as pltpu
from jax.sharding import PartitionSpec as P

HD = 64
TOK_I = 50
TOK_T = 77
CAP_ROW = 4


def norm_forward(hidden, norm_gain, norm_shift):
    row_mean = jnp.mean(hidden, -1, keepdims=True)
    centred = hidden - row_mean
    inverse = lax.rsqrt(jnp.mean(centred * centred, -1, keepdims=True) + 1e-05)
    normed = centred * inverse
    return (normed, inverse, normed * norm_gain + norm_shift)


def norm_backward(upstream, normed, inverse, norm_gain):
    scaled = upstream * norm_gain
    inner_sum = (
        scaled
        - jnp.mean(scaled, -1, keepdims=True)
        - normed * jnp.mean(scaled * normed, -1, keepdims=True)
    )
    return (inverse * inner_sum, jnp.sum(upstream * normed, (0, 1)), jnp.sum(upstream, (0, 1)))


def split_heads(values):
    return values.reshape(values.shape[0], values.shape[1], values.shape[2] // HD, HD)


def attention_scores(queries, key_heads, allowed):
    scores = (
        jnp.einsum("sqhd,skhd->shqk", queries, key_heads, preferred_element_type=jnp.float32)
        * 0.125
    )
    return jnp.where(allowed[:, None], scores, -1000000000.0)


def block_forward(hidden, weights, allowed):
    w_qkv, w_out, w_fc, w_proj, vectors, fc_bias = weights
    vectors = vectors.astype(jnp.float32)
    fc_bias = fc_bias.astype(jnp.float32)
    feature_width = hidden.shape[-1]
    normed_first, inverse_first, first = norm_forward(hidden, vectors[0], vectors[1])
    first_low = first.astype(jnp.bfloat16)
    projected = jnp.einsum("std,de->ste", first_low, w_qkv, preferred_element_type=jnp.float32)
    queries = (projected[..., :feature_width] + vectors[2]).astype(jnp.bfloat16)
    key_heads = projected[..., feature_width : 2 * feature_width].astype(jnp.bfloat16)
    values = (projected[..., 2 * feature_width :] + vectors[3]).astype(jnp.bfloat16)
    scores = attention_scores(split_heads(queries), split_heads(key_heads), allowed)
    totals = jax.nn.logsumexp(scores, -1, keepdims=True)
    attn_probs = jnp.exp(scores - totals).astype(jnp.bfloat16)
    context = jnp.einsum(
        "shqk,skhd->sqhd", attn_probs, split_heads(values), preferred_element_type=jnp.float32
    )
    context = context.reshape(hidden.shape).astype(jnp.bfloat16)
    middle = hidden + (
        jnp.einsum("std,de->ste", context, w_out, preferred_element_type=jnp.float32) + vectors[4]
    )
    normed_second, inverse_second, second = norm_forward(middle, vectors[5], vectors[6])
    second_low = second.astype(jnp.bfloat16)
    upward = (
        jnp.einsum("std,df->stf", second_low, w_fc, preferred_element_type=jnp.float32) + fc_bias
    )
    activated = (upward * jax.nn.sigmoid(1.702 * upward)).astype(jnp.bfloat16)
    output = middle + (
        jnp.einsum("stf,fd->std", activated, w_proj, preferred_element_type=jnp.float32)
        + vectors[7]
    )
    stored = (
        normed_first,
        inverse_first,
        first_low,
        queries,
        key_heads,
        values,
        totals,
        context,
        normed_second,
        inverse_second,
        second_low,
        upward,
        activated,
    )
    return (output, stored)


def block_backward(upstream, weights, stored, allowed):
    w_qkv, w_out, w_fc, w_proj, vectors, fc_bias = weights
    vectors = vectors.astype(jnp.float32)
    (
        normed_first,
        inverse_first,
        first_low,
        queries,
        key_heads,
        values,
        totals,
        context,
        normed_second,
        inverse_second,
        second_low,
        upward,
        activated,
    ) = stored
    feature_width = queries.shape[-1]
    branch = upstream.astype(jnp.bfloat16)
    d_proj_bias = jnp.sum(branch.astype(jnp.float32), (0, 1))
    d_w_proj = jnp.einsum("stf,std->fd", activated, branch, preferred_element_type=jnp.float32)
    d_activated = jnp.einsum("std,fd->stf", branch, w_proj, preferred_element_type=jnp.float32)
    sigmoid_up = jax.nn.sigmoid(1.702 * upward)
    d_upward = (
        d_activated * (sigmoid_up + 1.702 * upward * sigmoid_up * (1.0 - sigmoid_up))
    ).astype(jnp.bfloat16)
    d_fc_bias = jnp.sum(d_upward.astype(jnp.float32), (0, 1))
    d_w_fc = jnp.einsum("std,stf->df", second_low, d_upward, preferred_element_type=jnp.float32)
    d_second = jnp.einsum("stf,df->std", d_upward, w_fc, preferred_element_type=jnp.float32)
    d_middle_norm, d_gain_second, d_shift_second = norm_backward(
        d_second, normed_second, inverse_second, vectors[5]
    )
    d_middle = upstream + d_middle_norm
    attn_branch = d_middle.astype(jnp.bfloat16)
    d_out_bias = jnp.sum(attn_branch.astype(jnp.float32), (0, 1))
    d_w_out = jnp.einsum("std,ste->de", context, attn_branch, preferred_element_type=jnp.float32)
    d_context = jnp.einsum("ste,de->std", attn_branch, w_out, preferred_element_type=jnp.float32)
    d_context = split_heads(d_context.astype(jnp.bfloat16))
    query_heads = split_heads(queries)
    key_split = split_heads(key_heads)
    scores = attention_scores(query_heads, key_split, allowed)
    attn_probs = jnp.exp(scores - totals)
    d_probs = jnp.einsum(
        "sqhd,skhd->shqk", d_context, split_heads(values), preferred_element_type=jnp.float32
    )
    d_scores = (attn_probs * (d_probs - jnp.sum(attn_probs * d_probs, -1, keepdims=True))).astype(
        jnp.bfloat16
    )
    d_queries = (
        jnp.einsum("shqk,skhd->sqhd", d_scores, key_split, preferred_element_type=jnp.float32)
        * 0.125
    ).astype(jnp.bfloat16)
    d_keys = (
        jnp.einsum("shqk,sqhd->skhd", d_scores, query_heads, preferred_element_type=jnp.float32)
        * 0.125
    ).astype(jnp.bfloat16)
    d_values = jnp.einsum(
        "shqk,sqhd->skhd",
        attn_probs.astype(jnp.bfloat16),
        d_context,
        preferred_element_type=jnp.float32,
    ).astype(jnp.bfloat16)
    flat_shape = (queries.shape[0], queries.shape[1], feature_width)
    d_queries = d_queries.reshape(flat_shape)
    d_keys = d_keys.reshape(flat_shape)
    d_values = d_values.reshape(flat_shape)
    d_mixed = jnp.concatenate([d_queries, d_keys, d_values], -1)
    d_w_qkv = jnp.einsum("std,ste->de", first_low, d_mixed, preferred_element_type=jnp.float32)
    d_first = jnp.einsum("ste,de->std", d_mixed, w_qkv, preferred_element_type=jnp.float32)
    d_input_norm, d_gain_first, d_shift_first = norm_backward(
        d_first, normed_first, inverse_first, vectors[0]
    )
    d_hidden = d_middle + d_input_norm
    d_vectors = jnp.stack(
        [
            d_gain_first,
            d_shift_first,
            jnp.sum(d_queries.astype(jnp.float32), (0, 1)),
            jnp.sum(d_values.astype(jnp.float32), (0, 1)),
            d_out_bias,
            d_gain_second,
            d_shift_second,
            d_proj_bias,
        ]
    )
    return (d_hidden, (d_w_qkv, d_w_out, d_w_fc, d_w_proj, d_vectors, d_fc_bias))


def gather_first(img_stack, txt_stack, picture_feature_mapping):
    return (
        lax.all_gather(img_stack[0], "dp", axis=1, tiled=True),
        lax.all_gather(img_stack[1], "dp", axis=1, tiled=True),
        lax.all_gather(img_stack[2], "dp", axis=1, tiled=True),
        lax.all_gather(img_stack[3], "dp", axis=1, tiled=True),
        lax.all_gather(img_stack[4], "dp", axis=2, tiled=True),
        lax.all_gather(img_stack[5], "dp", axis=1, tiled=True),
        lax.all_gather(txt_stack[0], "dp", axis=1, tiled=True),
        lax.all_gather(txt_stack[1], "dp", axis=1, tiled=True),
        lax.all_gather(txt_stack[2], "dp", axis=1, tiled=True),
        lax.all_gather(txt_stack[3], "dp", axis=1, tiled=True),
        lax.all_gather(txt_stack[4], "dp", axis=2, tiled=True),
        lax.all_gather(txt_stack[5], "dp", axis=1, tiled=True),
        lax.all_gather(picture_feature_mapping, "dp", axis=0, tiled=True),
    )


def layer_of(stacks, layer_index):
    return tuple((stacked[layer_index] for stacked in stacks))


def local_plain(
    picture_patch_inputs,
    caption_packed_inputs,
    picture_attend_entry_weight,
    picture_attend_exit_weight,
    picture_widening_weight,
    picture_narrowing_weight,
    picture_affine_entries,
    picture_widening_offset,
    caption_attend_entry_weight,
    caption_attend_exit_weight,
    caption_widening_weight,
    caption_narrowing_weight,
    caption_affine_entries,
    caption_widening_offset,
    picture_feature_mapping,
    sharpness_exponent,
    caption_token_counts,
    matching_picture_index,
):
    img_stack = (
        picture_attend_entry_weight,
        picture_attend_exit_weight,
        picture_widening_weight,
        picture_narrowing_weight,
        picture_affine_entries,
        picture_widening_offset,
    )
    txt_stack = (
        caption_attend_entry_weight,
        caption_attend_exit_weight,
        caption_widening_weight,
        caption_narrowing_weight,
        caption_affine_entries,
        caption_widening_offset,
    )
    images = picture_patch_inputs.shape[0] // TOK_I
    row_count = caption_packed_inputs.shape[0] // TOK_T
    img_hidden = picture_patch_inputs.astype(jnp.float32).reshape(images, TOK_I, -1)
    txt_hidden = caption_packed_inputs.astype(jnp.float32).reshape(row_count, TOK_T, -1)
    img_allowed = jnp.ones((images, TOK_I, TOK_I), dtype=jnp.bool_)
    seg_ends = jnp.cumsum(caption_token_counts, axis=1)
    position = jnp.arange(TOK_T, dtype=jnp.int32)
    segment = jnp.sum((position[None, :, None] >= seg_ends[:, None, :]).astype(jnp.int32), -1)
    txt_allowed = (segment[:, :, None] == segment[:, None, :]) & (
        position[None, None, :] <= position[None, :, None]
    )
    pooling = (position[None, None, :] == seg_ends[:, :, None] - 1).astype(jnp.float32)
    gathered = gather_first(img_stack, txt_stack, picture_feature_mapping)
    img_full = gathered[0:6]
    txt_full = gathered[6:12]
    projection = gathered[12]
    img_stored, txt_stored = ([], [])
    layer_index = 0
    img_hidden, stored = block_forward(img_hidden, layer_of(img_full, layer_index), img_allowed)
    img_stored.append(stored)
    layer_index = 0
    txt_hidden, stored = block_forward(txt_hidden, layer_of(txt_full, layer_index), txt_allowed)
    txt_stored.append(stored)
    pooled_img = img_hidden[:, 0, :].astype(jnp.bfloat16)
    raw_img = jnp.dot(pooled_img, projection, preferred_element_type=jnp.float32)
    scale_img = lax.rsqrt(jnp.sum(raw_img * raw_img, -1, keepdims=True) + 1e-06)
    unit_img = raw_img * scale_img
    raw_txt = jnp.einsum("sct,std->scd", pooling, txt_hidden, precision=lax.Precision.HIGHEST)
    raw_txt = raw_txt.reshape(-1, raw_txt.shape[-1])
    scale_txt = lax.rsqrt(jnp.sum(raw_txt * raw_txt, -1, keepdims=True) + 1e-06)
    unit_txt = raw_txt * scale_txt
    image_embedding_rows = unit_img.astype(jnp.bfloat16)
    text_embedding_rows = unit_txt.astype(jnp.bfloat16)
    all_img, all_txt = (
        lax.all_gather(image_embedding_rows, "dp", axis=0, tiled=True),
        lax.all_gather(text_embedding_rows, "dp", axis=0, tiled=True),
    )
    batch_total = all_img.shape[0]
    affinity_sharpness = jnp.exp(sharpness_exponent)
    picture_wise_affinity_table = affinity_sharpness * jnp.einsum(
        "ce,ie->ci", text_embedding_rows, all_img, preferred_element_type=jnp.float32
    )
    caption_wise_affinity_table = affinity_sharpness * jnp.einsum(
        "ce,ie->ci", all_txt, image_embedding_rows, preferred_element_type=jnp.float32
    )
    lse_rows = jax.nn.logsumexp(picture_wise_affinity_table, 1)
    lse_cols = jax.nn.logsumexp(caption_wise_affinity_table, 0)
    columns = jnp.arange(batch_total, dtype=jnp.int32)
    target_rows = (matching_picture_index[:, None] == columns[None, :]).astype(jnp.float32)
    loss_part = (jnp.sum(lse_rows) + jnp.sum(lse_cols)) / (2 * batch_total) - jnp.sum(
        target_rows * picture_wise_affinity_table
    ) / batch_total
    probs_rows = jnp.exp(picture_wise_affinity_table - lse_rows[:, None])
    probs_cols = jnp.exp(caption_wise_affinity_table - lse_cols[None, :])
    gathered_image_matrix = all_img.astype(jnp.float32)
    gathered_text_matrix = all_txt.astype(jnp.float32)
    highest_precision = lax.Precision.HIGHEST
    row_gradient = probs_rows / (2 * batch_total) - target_rows / batch_total
    column_gradient = probs_cols / (2 * batch_total)
    caption_normalized_adjoint = affinity_sharpness * jnp.dot(
        row_gradient, gathered_image_matrix, precision=highest_precision
    )
    picture_normalized_adjoint = affinity_sharpness * jnp.dot(
        column_gradient.T, gathered_text_matrix, precision=highest_precision
    )
    picture_distributed_adjoint = affinity_sharpness * jnp.dot(
        row_gradient.T, text_embedding_rows.astype(jnp.float32), precision=highest_precision
    )
    caption_distributed_adjoint = affinity_sharpness * jnp.dot(
        column_gradient, image_embedding_rows.astype(jnp.float32), precision=highest_precision
    )
    back_img, back_txt = (
        lax.psum_scatter(picture_distributed_adjoint, "dp", scatter_dimension=0, tiled=True),
        lax.psum_scatter(caption_distributed_adjoint, "dp", scatter_dimension=0, tiled=True),
    )
    picture_normalized_adjoint = picture_normalized_adjoint + back_img
    caption_normalized_adjoint = caption_normalized_adjoint + back_txt
    scale_part = jnp.sum(row_gradient * picture_wise_affinity_table) + jnp.sum(
        column_gradient * caption_wise_affinity_table
    )
    loss, d_scale = lax.psum((loss_part, scale_part), "dp")
    img_back = gathered[0:6]
    txt_back = gathered[6:12]
    back_projection = gathered[12]
    d_raw_img = scale_img * (
        picture_normalized_adjoint
        - unit_img * jnp.sum(picture_normalized_adjoint * unit_img, -1, keepdims=True)
    )
    d_raw_low = d_raw_img.astype(jnp.bfloat16)
    d_projection = jnp.dot(pooled_img.T, d_raw_low, preferred_element_type=jnp.float32)
    d_pooled = jnp.dot(d_raw_low, back_projection.T, preferred_element_type=jnp.float32)
    d_img_hidden = jnp.concatenate(
        [d_pooled[:, None, :], jnp.zeros((images, TOK_I - 1, d_pooled.shape[-1]), jnp.float32)], 1
    )
    d_raw_txt = scale_txt * (
        caption_normalized_adjoint
        - unit_txt * jnp.sum(caption_normalized_adjoint * unit_txt, -1, keepdims=True)
    )
    d_txt_hidden = jnp.einsum(
        "sct,scd->std",
        pooling,
        d_raw_txt.reshape(row_count, CAP_ROW, -1),
        precision=highest_precision,
    )
    img_layer_grads, txt_layer_grads = ([], [])
    layer_index = 0
    d_img_hidden, layer_grads = block_backward(
        d_img_hidden, layer_of(img_back, layer_index), img_stored[layer_index], img_allowed
    )
    img_layer_grads.append(layer_grads)
    img_layer_grads = img_layer_grads[::-1]
    img_local = tuple(
        (jnp.stack([grads[member] for grads in img_layer_grads]) for member in range(6))
    )
    layer_index = 0
    d_txt_hidden, layer_grads = block_backward(
        d_txt_hidden, layer_of(txt_back, layer_index), txt_stored[layer_index], txt_allowed
    )
    txt_layer_grads.append(layer_grads)
    txt_layer_grads = txt_layer_grads[::-1]
    txt_local = tuple(
        (jnp.stack([grads[member] for grads in txt_layer_grads]) for member in range(6))
    )
    summed = (
        lax.psum_scatter(img_local[0], "dp", scatter_dimension=1, tiled=True),
        lax.psum_scatter(img_local[1], "dp", scatter_dimension=1, tiled=True),
        lax.psum_scatter(img_local[2], "dp", scatter_dimension=1, tiled=True),
        lax.psum_scatter(img_local[3], "dp", scatter_dimension=1, tiled=True),
        lax.psum_scatter(img_local[4], "dp", scatter_dimension=2, tiled=True),
        lax.psum_scatter(img_local[5], "dp", scatter_dimension=1, tiled=True),
        lax.psum_scatter(txt_local[0], "dp", scatter_dimension=1, tiled=True),
        lax.psum_scatter(txt_local[1], "dp", scatter_dimension=1, tiled=True),
        lax.psum_scatter(txt_local[2], "dp", scatter_dimension=1, tiled=True),
        lax.psum_scatter(txt_local[3], "dp", scatter_dimension=1, tiled=True),
        lax.psum_scatter(txt_local[4], "dp", scatter_dimension=2, tiled=True),
        lax.psum_scatter(txt_local[5], "dp", scatter_dimension=1, tiled=True),
        lax.psum_scatter(d_projection, "dp", scatter_dimension=0, tiled=True),
    )
    return (
        loss,
        d_scale,
        d_img_hidden.reshape(images * TOK_I, -1),
        d_txt_hidden.reshape(row_count * TOK_T, -1),
        summed[0],
        summed[1],
        summed[2],
        summed[3],
        summed[4],
        summed[5],
        summed[6],
        summed[7],
        summed[8],
        summed[9],
        summed[10],
        summed[11],
        summed[12],
    )


F32 = jnp.float32
BF16 = jnp.bfloat16
Z_PEERS = (8, 16, 24)
PLANE_PEERS = (2, 4, 6)
CHIP_PEERS = tuple(range(2, 32, 2))
ALL_PEERS = (1, 3, 5, 7, 9, 17, 25) + CHIP_PEERS
PAD = 16
N_SEMS = 84
STEP_ROWS = 32


def fits(mesh):
    return mesh.size == 32


def dot(left, right):
    return lax.dot_general(left, right, (((1,), (0,)), ((), ())), preferred_element_type=F32)


def dot_nt(left, right):
    return lax.dot_general(left, right, (((1,), (1,)), ((), ())), preferred_element_type=F32)


def dot_tn(left, right):
    return lax.dot_general(left, right, (((0,), (0,)), ((), ())), preferred_element_type=F32)


def split_two(values):
    high = values.astype(BF16)
    return high, (values - high.astype(F32)).astype(BF16)


def iota(shape, dim):
    return lax.broadcasted_iota(jnp.int32, shape, dim)


def expand_heads(rows):
    lanes = iota(rows.shape, 1) // HD
    heads = rows.shape[1] // HD
    zero = jnp.zeros_like(rows)
    return jnp.concatenate([jnp.where(lanes == head, rows, zero) for head in range(heads)], 0)


def join_heads(stacked):
    heads = stacked.shape[1] // HD
    lanes = iota((PAD, stacked.shape[1]), 1) // HD
    total = jnp.zeros((PAD, stacked.shape[1]), F32)
    for head in range(heads):
        total = jnp.where(lanes == head, stacked[PAD * head : PAD * (head + 1)], total)
    return total


def small_norm(hidden, gain, shift):
    centred = hidden - jnp.mean(hidden, -1, keepdims=True)
    inverse = lax.rsqrt(jnp.mean(centred * centred, -1, keepdims=True) + 1e-05)
    normed = centred * inverse
    return normed, inverse, normed * gain + shift


def small_norm_back(upstream, normed, inverse, gain):
    scaled = upstream * gain
    return inverse * (
        scaled
        - jnp.mean(scaled, -1, keepdims=True)
        - normed * jnp.mean(scaled * normed, -1, keepdims=True)
    )


def col_sum(values):
    return jnp.sum(values, 0, keepdims=True)


class Split:
    def __init__(self, along_z):
        self.along_z = along_z
        self.group_peers = Z_PEERS if along_z else PLANE_PEERS
        self.copy_peers = PLANE_PEERS if along_z else Z_PEERS
        self.line_peers = (1,) + tuple(mask + core for mask in self.group_peers for core in range(2))

    def stand(self, step):
        self.g, self.r = (step.zed, step.plane) if self.along_z else (step.plane, step.zed)
        self.spot = step.core * 4 + self.g

    def chip_of(self, group, copy):
        return 4 * group + copy if self.along_z else 4 * copy + group

    def device_of(self, group, copy, core):
        return 2 * self.chip_of(group, copy) + core

    def group_of(self, device):
        return device // 8 if self.along_z else lax.rem(device // 2, 4)

    def copy_of(self, device):
        return lax.rem(device // 2, 4) if self.along_z else device // 8

    def chips_of_group(self, ref, group):
        return ref.at[group] if self.along_z else ref.at[:, group]

    def chips_of_copy(self, ref, copy):
        return ref.at[:, copy] if self.along_z else ref.at[copy]


class Tower:
    def __init__(self, along_z, width, real_tokens, rows, block, extra):
        self.ff, self.at = Split(along_z), Split(along_z)
        self.width = width
        self.real_tokens = real_tokens
        self.tokens = -(-real_tokens // 128) * 128
        self.rows = rows
        self.chip_rows = 2 * rows
        self.block = block
        self.group = 4 * block
        self.heads = width // HD
        self.queries = PAD * self.heads
        self.extra = extra
        self.packed = 2 * width + extra + 4 * self.group
        self.row_pad = -(-rows // 16) * 16
        self.fold = 1 if rows % 16 == 0 else 2
        self.tiles = 4 * (self.queries // 128) + 2 * (self.queries % 128 // 64)
        self.near = 2 if along_z else 3
        self.sums = {}
        self.c_r1 = self.c_r2 = None

    def scratch(self):
        d, n, r, g, b, cr = self.width, self.tokens, self.queries, self.group, self.block, self.chip_rows
        c1, c2 = 2 * d + 2 * self.extra, 2 * d
        v = pltpu.VMEM
        return dict(
            pk=v((2, self.row_pad, self.packed), BF16),
            pr=v((self.row_pad, self.packed), BF16),
            w1=v((2, 16 * cr, d), BF16),
            w2=v((2, 16 * cr, d), BF16),
            mf=v((4, cr, g), BF16),
            fa=v((4, 4, cr, g), BF16),
            wp=v((4, b, d), BF16),
            vecs=v((8, d), F32),
            bias=v((8, g), F32),
            xp=v((n, d), BF16),
            xh=v((n, d), F32),
            inv=v((n, 128), F32),
            a=v((n, d), BF16),
            p32=v((r, n), F32),
            lh=v((2 * r + 2 * PAD, n), BF16),
            rh=v((2 * r + 2 * PAD, d), BF16),
            ci=v((8, PAD, d), BF16),
            hpf=v((8, PAD, d), F32),
            hps=v((8, PAD, d), BF16),
            hr=v((7, PAD, d), BF16),
            dcf=v((8, PAD, d), F32),
            dcs=v((8, PAD, d), BF16),
            dcr=v((7, PAD, d), BF16),
            u=v((8 * PAD, g), F32),
            prj=v((b, d), F32),
            mt=v((4, b, 8 * PAD), BF16),
            mtr=v((4, b, 8 * PAD), BF16),
            gff=v((4, 4, cr, g), F32),
            gfb=v((4, 4, cr, g), BF16),
            gfr=v((3, 4, cr, g), BF16),
            gf2=v((4, cr, g), BF16),
            gf3=v((4, cr, g), F32),
            gf3r=v((4, cr, g), BF16),
            gf4=v((4, self.rows, g), F32),
            in1t=v((self.tiles, 4, cr, 128), BF16),
            in1r=v((4, self.tiles, cr, 128), BF16),
            in2t=v((self.tiles, 4, cr, 128), BF16),
            in2r=v((4, self.tiles, cr, 128), BF16),
            ag=v((4, PAD, d), BF16),
            wg=v((4, PAD, d), BF16),
            dqg=v((4, PAD, d), BF16),
            pg=v((4, PAD, d), BF16),
            og=v((4, PAD, d), BF16),
            in3t=v((4, 4, cr, 8 * PAD), BF16),
            in4t=v((4, 4, cr, 8 * PAD), BF16),
            r1f=v((4, cr, c1), F32),
            r1p=v((4, self.rows, c1), F32),
            r1s=v((4, self.rows, c1), F32),
            r1b=v((4, self.fold * self.rows, c1 // self.fold), BF16),
            r1r=v((3, self.fold * self.rows, c1 // self.fold), BF16),
            r2f=v((4, cr, c2), F32),
            r2p=v((4, self.rows, c2), F32),
            r2s=v((4, self.rows, c2), F32),
            r2b=v((4, self.fold * self.rows, c2 // self.fold), BF16),
            r2r=v((3, self.fold * self.rows, c2 // self.fold), BF16),
            da=v((n, d), F32),
            gp=v((n, d), F32),
            dxs=v((self.real_tokens, d), F32),
            g2=v((8, PAD, d), F32),
            dbs=v((8, g), F32),
            dbr=v((3, 8, g), F32),
        )


def shared_scratch(ti, tt):
    v = pltpu.VMEM
    e = tt.width
    rows = 32 * PAD
    return dict(
        vb=v((2, 16, PAD, 128), BF16),
        w3=v((2, ti.width, ti.extra), BF16),
        eb=v((2, 2, 16, PAD, e), BF16),
        gtxt=v((rows, rows), F32),
        gimg=v((rows, rows), F32),
        drb=v((8, PAD, e), BF16),
        va=v((8, ti.width + tt.width), F32),
        var=v((8, ti.width + tt.width), F32),
        vs=v((16, 8, 128), F32),
        vl=v((16, 8, 128), F32),
    )


class Group:
    def __init__(self, step):
        self.step = step
        self.index = step.used
        step.used += 1
        step.groups.append(self)

    def copy(self, src, dst, mask):
        return pltpu.make_async_remote_copy(
            src_ref=src,
            dst_ref=dst,
            send_sem=self.step.ssem.at[self.index],
            recv_sem=self.step.rsem.at[self.index],
            device_id=(self.step.at_peer(mask),),
            device_id_type=pl.DeviceIdType.MESH,
        )

    def send(self, src, dst, mask):
        self.copy(src, dst, mask).start()

    def wait(self, view):
        self.view = view
        self.copy(view, view, 1).wait_recv()

    def finish(self):
        self.copy(self.view, self.view, 1).wait_send()


class Gather:
    def __init__(self, step, slot, span, whole, relay):
        self.step, self.slot, self.span, self.whole, self.relayed = step, slot, span, whole, relay
        self.own = self.step.chip

    def chip(self, mask):
        return self.step.at_peer(mask) // 2

    def spread(self, group, chip):
        here = self.slot(chip)
        for mask in PLANE_PEERS[:2] if self.relayed else PLANE_PEERS:
            group.send(here, here, mask)

    def begin_z(self):
        self.g_z = Group(self.step)
        here = self.slot(self.own)
        for mask in Z_PEERS:
            self.g_z.send(here, here, mask)

    def begin_plane(self):
        self.g_own = Group(self.step)
        self.spread(self.g_own, self.own)

    def middle(self):
        self.g_z.wait(self.span(3))
        self.g_mid = Group(self.step)
        for mask in Z_PEERS:
            self.spread(self.g_mid, self.chip(mask))

    def hand_on(self, mask):
        for half, near, to in ((0, 2, 4), (1, 4, 2)):
            there = self.slot(self.chip(near | mask), half)
            self.g_relay.send(there, there, to)

    def relay_own(self):
        self.g_own.wait(self.span(2))
        self.g_relay = Group(self.step)
        self.hand_on(0)

    def relay(self):
        self.g_mid.wait(self.span(6))
        for mask in Z_PEERS:
            self.hand_on(mask)

    def end(self):
        if self.relayed:
            self.g_relay.wait(self.span(4))
        else:
            self.g_own.wait(self.span(3))
            self.g_mid.wait(self.span(9))
        self.g_core = Group(self.step)
        self.g_core.send(self.whole, self.whole, 1)

    def done(self):
        self.g_core.wait(self.whole)


class Step:
    def __init__(self, ti, tt, images):
        self.ti, self.tt, self.images = ti, tt, images
        me = lax.axis_index("dp")
        self.bits = [lax.rem(me // (1 << bit), 2) for bit in range(5)]
        self.me = me
        self.core = lax.rem(me, 2)
        self.chip = me // 2
        self.plane = lax.rem(me // 2, 4)
        self.zed = me // 8
        for t in (ti, tt):
            t.ff.stand(self)
            t.at.stand(self)
        self.used = 0
        self.groups = []

    def at_peer(self, mask):
        total = 0
        for bit in range(5):
            value = 1 - self.bits[bit] if mask >> bit & 1 else self.bits[bit]
            total = total + value * (1 << bit)
        return total

    def barrier(self):
        semaphore = pltpu.get_barrier_semaphore()
        for mask in ALL_PEERS:
            pl.semaphore_signal(
                semaphore, inc=1, device_id=(self.at_peer(mask),), device_id_type=pl.DeviceIdType.MESH
            )
        pl.semaphore_wait(semaphore, len(ALL_PEERS))

    def row_gather(self, buffer, rows):
        cols = buffer.shape[2] // 2

        def slot(chip, half=None):
            at = pl.ds(pl.multiple_of(chip * rows, 16), rows)
            if half is None:
                return buffer.at[self.core, at]
            return buffer.at[self.core, at, half * cols : (half + 1) * cols]

        return Gather(
            self, slot, lambda count: buffer.at[self.core, 0 : count * rows], buffer.at[self.core], True
        )

    def line_gather(self, split, buffer):
        group = Group(self)
        here = buffer.at[split.spot]
        for mask in split.line_peers:
            group.send(here, here, mask)
        return group

    def line_scatter(self, split, parts, landing):
        group = Group(self)
        for slot, mask in enumerate(split.line_peers):
            peer = self.at_peer(mask)
            group.send(parts.at[lax.rem(peer, 2) * 4 + split.group_of(peer)], landing.at[slot], mask)
        return group

    def to_group(self, split, block, landing):
        group = Group(self)
        for mask in split.group_peers:
            group.send(block.at[:, split.group_of(self.at_peer(mask))], landing.at[split.g], mask)
        landing[split.g] = block[:, split.g]
        return group

    def share_group(self, split, buffer, values):
        group = Group(self)
        buffer[split.g] = values
        here = buffer.at[split.g]
        for mask in split.group_peers:
            group.send(here, here, mask)
        return group

    def to_copies(self, split, block, landing):
        group = Group(self)
        for slot, mask in enumerate(split.copy_peers):
            group.send(block.at[split.copy_of(self.at_peer(mask))], landing.at[slot], mask)
        return group

    def run(self):
        ti, tt = self.ti, self.tt
        both = (ti, tt)
        self.pack(ti)
        self.pack(tt)
        self.pack_vectors()
        self.barrier()
        for t in both:
            t.pair = Group(self)
            t.pair.send(t.pk.at[1 - self.core], t.pr, 1)
        vb, eb = self.vb, self.eb
        vectors = Gather(
            self,
            lambda chip: vb.at[self.core, chip],
            lambda count: vb.at[self.core, 0:count],
            vb.at[self.core],
            False,
        )
        vectors.begin_z()
        vectors.begin_plane()
        for t in both:
            t.first = self.row_gather(t.w1, t.chip_rows)
            t.second = self.row_gather(t.w2, t.chip_rows)
        third = self.row_gather(self.w3, ti.chip_rows)
        for t in both:
            self.merge(t)
            t.first.begin_z()
            t.first.begin_plane()
        for t in both:
            t.second.begin_z()
        for t in both:
            self.widen_begin(t)
        third.begin_z()
        for t in both:
            self.narrow_begin(t)
        self.standardize(tt)
        vectors.middle()
        self.standardize(ti)
        for t in both:
            t.first.relay_own()
        for t in both:
            t.second.begin_plane()
        for t in both:
            t.first.middle()
        for t in both:
            t.first.relay()
        vectors.end()
        for t in both:
            t.second.relay_own()
        vectors.done()
        self.unpack_vectors()
        self.queries(ti)
        self.queries(tt)
        for t in both:
            t.second.middle()
        for t in both:
            t.first.end()
        third.begin_plane()
        for t in both:
            self.widen_middle(t)
        for t in both:
            t.second.relay()
        for t in both:
            t.first.done()
            self.attend(t)
            self.early_operands(t)
        third.middle()
        third.relay_own()
        for t in both:
            t.second.end()
        third.relay()
        for t in both:
            t.second.done()
            self.mix(t)
        for t in both:
            self.narrow_middle(t)
        for t in both:
            self.widen_relay(t)
        third.end()
        for t in both:
            t.c_o = self.share_group(t.at, t.og, t.o)
        for t in both:
            self.feed(t)
        third.done()
        for t in both:
            self.embed(t)
        rows = Gather(
            self,
            lambda chip: eb.at[:, self.core, chip],
            lambda count: eb.at[:, self.core, 0:count],
            eb.at[:, self.core],
            False,
        )
        rows.begin_z()
        rows.begin_plane()
        ti.c_p = self.share_group(ti.at, ti.pg, self.pooled)
        rows.middle()
        rows.end()
        rows.done()
        self.contrast()
        for t in both:
            self.feed_back(t)
        for t in both:
            self.feed_weights(t)
        for t in both:
            self.feed_proj(t)
        for t in both:
            self.attend_back(t)
            self.attend_back_end(t)
        for t in both:
            self.input_gradient(t)
        self.vector_sum_begin()
        for t in both:
            self.round_one(t)
        self.vector_sum_spread()
        for t in both:
            self.feed_weights_middle(t)
        for t in both:
            self.round_spread(t, 0)
        for t in both:
            self.round_two(t)
        for t in both:
            self.round_spread(t, 1)
        for t in both:
            self.feed_weights_end(t)
        self.vector_sum_done()
        for t in both:
            self.round_end(t, 0)
        for t in both:
            self.feed_weights_done(t)
        for t in both:
            self.round_end(t, 1)
        for t in both:
            self.copy_out(t).wait()
            self.proj_out(t).wait()
        for group in self.groups:
            group.finish()

    def pack(self, t):
        pk, qkv, out, fc = t.pk, t.qkv, t.out, t.fc
        d, b = t.width, t.block
        pad = t.row_pad - t.rows

        def padded(values):
            values = values.astype(F32)
            if pad:
                values = jnp.concatenate([values, jnp.zeros((pad, values.shape[1]), F32)], 0)
            return values.astype(BF16)

        pk[0, :, 0:d] = padded(qkv[:, 0:d])
        pk[1, :, 0:d] = padded(qkv[:, d : 2 * d])
        pk[0, :, d : 2 * d] = padded(qkv[:, 2 * d : 3 * d])
        pk[1, :, d : 2 * d] = padded(out[...])
        if t.extra:
            for half in range(2):
                cols = slice(half * t.extra, (half + 1) * t.extra)
                pk[half, :, 2 * d : 2 * d + t.extra] = padded(self.map[:, cols])
        base = 2 * d + t.extra
        values = padded(fc[...]).astype(F32)
        for half in range(2):
            for group in range(4):
                pieces = []
                for copy in range(4):
                    device = t.ff.device_of(group, copy, half)
                    pieces.append(values[:, b * device : b * (device + 1)])
                start = base + group * t.group
                pk[half, :, start : start + t.group] = jnp.concatenate(pieces, 1).astype(BF16)

    def pack_vectors(self):
        def widen(values, at):
            values = values.astype(F32)
            parts = [values, jnp.zeros((values.shape[0], 128 - at - values.shape[1]), F32)]
            if at:
                parts = [jnp.zeros((values.shape[0], at), F32)] + parts
            return jnp.concatenate(parts, 1)

        top = widen(self.ti.vec[...], 0) + widen(self.tt.vec[...], 32)
        row = iota((8, 128), 0)
        bottom = jnp.where(row == 0, widen(self.ti.fcb[...], 0), 0.0)
        bottom = bottom + jnp.where(row == 1, widen(self.tt.fcb[...], 0), 0.0)
        block = jnp.concatenate([top, bottom], 0)
        row, lane = iota((PAD, 128), 0), iota((PAD, 128), 1)
        for caption in range(self.images):
            image = self.match[caption]
            device = image // self.images
            high = lax.rem(device, 2) * 16 + device // 2
            low = image - device * self.images
            block = jnp.where((row == caption) & (lane == 120), high.astype(F32), block)
            block = jnp.where((row == caption) & (lane == 121), low.astype(F32), block)
        self.vb[self.core, self.chip] = block.astype(BF16)

    def unpack_vectors(self):
        vb = self.vb
        for core in range(2):
            for chip in range(16):
                block = vb[core, chip].astype(F32)
                device = 2 * chip + core
                for t, at in ((self.ti, 0), (self.tt, 32)):
                    rows = t.rows
                    t.vecs[:, rows * device : rows * (device + 1)] = block[0:8, at : at + rows]
        for t, row in ((self.ti, 8), (self.tt, 9)):
            for copy in range(4):
                block = vb[self.core, t.ff.chip_of(t.ff.g, copy)].astype(F32)
                b = t.block
                t.bias[0:1, b * copy : b * (copy + 1)] = block[row : row + 1, 0:b]

    def standardize(self, t):
        x, xp, xh, inv = t.x, t.xp, t.xh, t.inv
        step = STEP_ROWS
        full = t.real_tokens // step

        def norm(hidden, rows):
            xp[rows, :] = hidden.astype(BF16)
            centred = hidden - jnp.mean(hidden, -1, keepdims=True)
            inverse = lax.rsqrt(jnp.mean(centred * centred, -1, keepdims=True) + 1e-05)
            xh[rows, :] = centred * inverse
            inv[rows, :] = jnp.broadcast_to(inverse, (step, 128))

        def body(index, carry):
            rows = pl.ds(pl.multiple_of(index * step, step), step)
            norm(x[rows, :].astype(F32), rows)
            return carry

        lax.fori_loop(0, full, body, 0)
        start, rest = full * step, t.real_tokens - full * step
        if rest:
            last = x[start : t.real_tokens, :].astype(F32)
            last = jnp.concatenate([last, jnp.zeros((step - rest, t.width), F32)], 0)
            norm(last, slice(start, start + step))
            start += step
        while start < t.tokens:
            norm(jnp.zeros((step, t.width), F32), slice(start, start + step))
            start += step

    def merge(self, t):
        t.pair.wait(t.pr)
        pk, pr = t.pk, t.pr
        d, g = t.width, t.group
        rows = pl.ds(pl.multiple_of(self.chip * t.chip_rows, 16), t.chip_rows)
        first = self.core == 0

        def merged(cols):
            own = pk[self.core, :, cols].astype(F32)
            got = pr[:, cols].astype(F32)
            upper = jnp.where(first, own, got)[: t.rows]
            lower = jnp.where(first, got, own)[: t.rows]
            return jnp.concatenate([upper, lower], 0).astype(BF16)

        t.w1[self.core, rows, :] = merged(slice(0, d))
        t.w2[self.core, rows, :] = merged(slice(d, 2 * d))
        base = 2 * d
        if t.extra:
            self.w3[self.core, rows, :] = merged(slice(base, base + t.extra))
            base += t.extra
        for group in range(4):
            t.mf[group] = merged(slice(base + group * g, base + (group + 1) * g))

    def widen_begin(self, t):
        t.widen = Group(self)
        for mask in t.ff.group_peers:
            t.widen.send(t.mf.at[t.ff.group_of(self.at_peer(mask))], t.fa.at[self.zed, self.plane], mask)
        t.fa[self.zed, self.plane] = t.mf[t.ff.g]

    def widen_middle(self, t):
        t.widen.wait(t.mf.at[0:3])
        t.widen = Group(self)
        part = t.ff.chips_of_copy(t.fa, t.ff.r)
        for mask in t.ff.copy_peers[: t.near]:
            t.widen.send(part, part, mask)

    def narrow_begin(self, t):
        t.narrow = Group(self)
        for mask in t.ff.copy_peers[: t.near]:
            t.narrow.send(t.proj, t.wp.at[t.ff.r], mask)
        t.wp[t.ff.r] = t.proj[...]

    def narrow_middle(self, t):
        t.narrow.wait(t.wp.at[0 : t.near])
        if t.ff.along_z:
            t.narrow_far, half = Group(self), t.block // 2
            for part, near, to in ((0, 2, 4), (1, 4, 2)):
                rows = pl.ds(part * half, half)
                there = t.wp.at[t.ff.copy_of(self.at_peer(near)), rows]
                t.narrow_far.send(there, there, to)

    def widen_relay(self, t):
        t.widen.wait(t.fa.at[0 : t.near])
        if t.ff.along_z:
            t.widen_far = Group(self)
            for part, near, to in ((0, 2, 4), (1, 4, 2)):
                there = t.fa.at[2 * part : 2 * part + 2, t.ff.copy_of(self.at_peer(near))]
                t.widen_far.send(there, there, to)

    def queries(self, t):
        a, xh, vec = t.a, t.xh, t.vecs
        step = STEP_ROWS

        def body(index, carry):
            rows = pl.ds(pl.multiple_of(index * step, step), step)
            a[rows, :] = (xh[rows, :] * vec[0:1, :] + vec[1:2, :]).astype(BF16)
            return carry

        lax.fori_loop(0, t.tokens // step, body, 0)
        n = t.tokens
        row, token = iota((PAD, n), 0), iota((PAD, n), 1)
        if t is self.ti:
            real = row < self.images
            at = jnp.where(real, row * TOK_I, -1)
            low, high = jnp.where(real, row * TOK_I, -1), jnp.where(real, (row + 1) * TOK_I, -1)
        else:
            counts = self.counts
            column = iota((PAD, 1), 0)
            low, high = jnp.full((PAD, 1), -1, jnp.int32), jnp.full((PAD, 1), -1, jnp.int32)
            for line in range(counts.shape[0]):
                end = line * TOK_T
                for member in range(CAP_ROW):
                    begin, end = end, end + counts[line, member]
                    chosen = column == line * CAP_ROW + member
                    low, high = jnp.where(chosen, begin, low), jnp.where(chosen, end, high)
            at = jnp.where(high > 0, high - 1, -1)
        chosen = (token == at).astype(F32).astype(BF16)
        lh, r = t.lh, t.queries
        lh[2 * r : 2 * r + PAD, :] = chosen
        lh[2 * r + PAD : 2 * r + 2 * PAD, :] = chosen
        t.seen = ((token >= low) & (token < high)).astype(F32)
        t.x0 = dot(chosen, t.xp[...])
        t.a0 = dot(chosen, a[...]).astype(BF16)

    def attend(self, t):
        w1, vec, a, r = t.w1, t.vecs, t.a, t.queries
        t.q = (dot(t.a0, w1[0]) + vec[2:3, :]).astype(BF16)
        qt = dot_nt(expand_heads(t.q), w1[1]).astype(BF16)
        t.rh[0:r, :] = qt
        scores = dot_nt(qt, a[...]) * 0.125
        seen = jnp.concatenate([t.seen] * t.heads, 0) > 0.5
        scores = jnp.where(seen, scores, -1000000000.0)
        top = jnp.max(scores, -1, keepdims=True)
        raw = jnp.where(seen, jnp.exp(scores - top), 0.0)
        total = jnp.sum(raw, -1, keepdims=True)
        probs = raw / jnp.where(total > 0.0, total, 1.0)
        t.p32[...] = probs
        low = probs.astype(BF16)
        t.lh[r : 2 * r, :] = low
        t.pa = dot(low, a[...])

    def mix(self, t):
        w2, vec = t.w2, t.vecs
        context = (join_heads(dot(t.pa.astype(BF16), w2[0])) + vec[3:4, :]).astype(BF16)
        t.o = context
        t.h1 = t.x0 + (dot(context, w2[1]) + vec[4:5, :])
        t.xh2, t.inv2, second = small_norm(t.h1, vec[5:6, :], vec[6:7, :])
        t.ci[t.ff.spot] = second.astype(BF16)
        t.line = self.line_gather(t.ff, t.ci)

    def feed(self, t):
        d, g = t.width, t.group
        if t.ff.along_z:
            t.widen_far.wait(t.fa.at[0])
            t.narrow_far.wait(t.wp.at[0])
        t.line.wait(t.ci.at[0:7])
        c = t.ci[...].reshape(8 * PAD, d)
        up = dot(c, t.fa[...].reshape(d, g)) + t.bias[0:1, :]
        active = up * jax.nn.sigmoid(1.702 * up)
        t.u[...] = up
        t.mt[...] = active.T.astype(BF16).reshape(t.mt.shape)
        active = active.astype(BF16)
        part = dot(active, t.wp[...].reshape(g, d)).reshape(8, PAD, d)
        t.hpf[...] = part
        t.hps[...] = part.astype(BF16)
        t.line = self.line_scatter(t.ff, t.hps, t.hr)
        t.mtr[t.ff.r] = t.mt[t.ff.r]
        t.c_m = Group(self)
        for mask in t.ff.copy_peers:
            t.c_m.send(t.mt.at[t.ff.copy_of(self.at_peer(mask))], t.mtr.at[t.ff.r], mask)

    def line_total(self, t, own, landing):
        t.line.wait(landing)
        total = own[t.ff.spot]
        for slot in range(7):
            total = total + landing[slot].astype(F32)
        return total

    def embed(self, t):
        hidden = t.h1 + (self.line_total(t, t.hpf, t.hr) + t.vecs[7:8, :])
        which = 1
        raw = hidden
        if t is self.ti:
            which = 0
            self.pooled = hidden.astype(BF16)
            raw = jnp.concatenate([dot(self.pooled, self.w3[0]), dot(self.pooled, self.w3[1])], 1)
        scale = lax.rsqrt(jnp.sum(raw * raw, -1, keepdims=True) + 1e-06)
        row, lane = iota(raw.shape, 0), iota(raw.shape, 1)
        across = col_sum(jnp.where(row == lane, scale, 0.0))
        high = across.astype(BF16).astype(F32)
        block = jnp.where(row == self.images, high, raw * scale)
        block = jnp.where(row == self.images + 1, across - high, block)
        self.eb[which, self.core, self.chip] = block.astype(BF16)

    def by_rows(self, t, values, buffer):
        turned = values.T.reshape(4, 4, t.chip_rows, t.queries)
        whole = t.queries // 128
        for tile in range(whole):
            part = turned[:, :, :, 128 * tile : 128 * (tile + 1)].astype(BF16)
            for copy in range(4):
                buffer[4 * tile + copy] = part[:, copy] if t.at.along_z else part[copy]
        if t.queries % 128:
            rest = turned[:, :, :, 128 * whole :]
            for pair in range(2):
                if t.at.along_z:
                    parts = [rest[:, 2 * pair], rest[:, 2 * pair + 1]]
                else:
                    parts = [rest[2 * pair], rest[2 * pair + 1]]
                buffer[4 * whole + pair] = jnp.concatenate(parts, 2).astype(BF16)

    def times_heads(self, t, landing, rows, out, start):
        cr, d = t.chip_rows, t.width
        whole = t.queries // 128
        total, paired = 0.0, 0.0
        for group in range(4):
            wide = expand_heads(rows[PAD * group : PAD * (group + 1)])
            for tile in range(whole):
                operand = landing[group, 4 * tile : 4 * (tile + 1)].reshape(4 * cr, 128)
                total = total + dot(operand, wide[128 * tile : 128 * (tile + 1)])
            if t.queries % 128:
                rest = wide[128 * whole :]
                blank = jnp.zeros_like(rest)
                rest = jnp.concatenate(
                    [jnp.concatenate([rest, blank], 0), jnp.concatenate([blank, rest], 0)], 1
                )
                paired = paired + dot(landing[group, 4 * whole : 4 * whole + 2].reshape(2 * cr, 128), rest)
        for z in range(4):
            values = total[cr * z : cr * (z + 1)]
            if t.queries % 128:
                pair = paired[cr * (z // 2) : cr * (z // 2 + 1)]
                values = values + pair[:, d * (z % 2) : d * (z % 2 + 1)]
            out[z, :, start : start + d] = values

    def early_operands(self, t):
        self.by_rows(t, t.pa, t.in1t)
        t.c_in1 = self.to_group(t.at, t.in1t, t.in1r)
        t.c_a = self.share_group(t.at, t.ag, t.a0)

    def contrast(self):
        eb, gtxt, gimg = self.eb, self.gtxt, self.gimg
        size = 32 * PAD
        total = self.images * 32
        e_img, e_txt = eb[0].reshape(size, eb.shape[-1]), eb[1].reshape(size, eb.shape[-1])
        sharp = jnp.exp(jnp.full((8, 128), self.sharp[0], F32))[0:1, 0:1]
        logits = sharp * dot_nt(e_txt, e_img)
        marks = self.vb[...].reshape(size, 128).astype(F32)
        target = marks[:, 120:121] * float(PAD) + marks[:, 121:122]
        row, col = iota((size, size), 0), iota((size, size), 1)
        real = (lax.rem(row, PAD) < self.images) & (lax.rem(col, PAD) < self.images)
        hit = real & (col.astype(F32) == target)
        powers = jnp.where(real, jnp.exp(logits), 0.0)
        row_sum, col_sums = jnp.sum(powers, 1, keepdims=True), col_sum(powers)
        real_line = lax.rem(iota((size, 1), 0), PAD) < self.images
        real_lane = lax.rem(iota((1, size), 1), PAD) < self.images
        row_sum, col_sums = jnp.where(real_line, row_sum, 1.0), jnp.where(real_lane, col_sums, 1.0)
        grad = powers * ((1.0 / row_sum + 1.0 / col_sums) * (0.5 / total))
        grad = grad - jnp.where(hit, 1.0 / total, 0.0)
        safe = jnp.where(real, logits, 0.0)
        logs = jnp.sum(jnp.log(row_sum), 0, keepdims=True) + jnp.sum(jnp.log(col_sums), 1, keepdims=True)

        def whole(values):
            return jnp.sum(jnp.sum(values, 1, keepdims=True), 0, keepdims=True)

        self.loss[...] = logs * (0.5 / total) - whole(jnp.where(hit, safe, 0.0)) * (1.0 / total)
        self.dls[...] = whole(grad * safe)
        gtxt[...] = grad
        gimg[...] = grad.T
        for t in (self.ti, self.tt):
            d_raw = self.raw_gradient(t, t.ff.r)
            if t is self.ti:
                d_raw, rounded = self.through_map(d_raw)
                self.drb[...] = rounded.reshape(self.drb.shape)
            t.g2[...] = d_raw.reshape(t.g2.shape)

    def raw_gradient(self, t, copy):
        eb = self.eb
        which, rows, others = (0, self.gimg, eb[1]) if t is self.ti else (1, self.gtxt, eb[0])
        others = others.reshape(32 * PAD, eb.shape[-1])
        sharp = jnp.exp(jnp.full((8, 128), self.sharp[0], F32))[0:1, 0:1]
        parts, units, scales = [], [], []
        for core in range(2):
            for group in range(4):
                chip = t.ff.chip_of(group, copy)
                start = (core * 16 + chip) * PAD
                if not isinstance(start, int):
                    start = pl.multiple_of(start, PAD)
                parts.append(rows[pl.ds(start, PAD), :])
                block = eb[which, core, chip].astype(F32)
                units.append(block)
                row, lane = iota((PAD, 128), 0), iota((PAD, 128), 1)
                spare = (row >= self.images) & (row < self.images + 2)
                across = col_sum(jnp.where(spare, block[:, 0:128], 0.0))
                scales.append(jnp.sum(jnp.where(row == lane, across, 0.0), 1, keepdims=True))
        part, unit, scale = (jnp.concatenate(pieces, 0) for pieces in (parts, units, scales))
        high, low = split_two(part)
        d_unit = sharp * (dot(high, others) + dot(low, others))
        return scale * (d_unit - unit * jnp.sum(d_unit * unit, -1, keepdims=True))

    def through_map(self, d_raw):
        w3, half = self.w3, self.ti.extra
        rounded = d_raw.astype(BF16)
        return dot_nt(rounded[:, 0:half], w3[0]) + dot_nt(rounded[:, half : 2 * half], w3[1]), rounded

    def feed_back(self, t):
        d, g = t.width, t.group
        t.y = t.g2[...].reshape(8 * PAD, d).astype(BF16)
        up = t.u[...]
        gate = jax.nn.sigmoid(1.702 * up)
        d_active = dot_nt(t.y, t.wp[...].reshape(g, d))
        t.du = (d_active * (gate + 1.702 * up * gate * (1.0 - gate))).astype(BF16)
        part = dot_nt(t.du, t.fa[...].reshape(d, g)).reshape(8, PAD, d)
        t.dcf[...] = part
        t.dcs[...] = part.astype(BF16)
        t.line = self.line_scatter(t.ff, t.dcs, t.dcr)

    def feed_weights(self, t):
        d, g, cr = t.width, t.group, t.chip_rows
        grad = dot_tn(t.ci[...].reshape(8 * PAD, d), t.du).reshape(4, 4, cr, g)
        t.gff[...] = grad
        t.gfb[...] = grad.astype(BF16)
        t.c_wide, t.c_bias = Group(self), Group(self)
        t.dbs[...] = jnp.broadcast_to(col_sum(t.du.astype(F32)), (8, g))
        for slot, mask in enumerate(t.ff.copy_peers):
            copy = t.ff.copy_of(self.at_peer(mask))
            t.c_wide.send(t.ff.chips_of_copy(t.gfb, copy), t.gfr.at[slot], mask)
            t.c_bias.send(t.dbs, t.dbr.at[slot], mask)

    def feed_proj(self, t):
        t.c_m.wait(t.mtr.at[0:3])
        total = 0.0
        for copy in range(4):
            d_raw = self.raw_gradient(t, copy)
            if t is self.ti:
                d_raw = self.through_map(d_raw)[0]
            total = total + dot(t.mtr[copy], d_raw.astype(BF16))
        t.prj[...] = total
        self.proj_out(t).start()

    def feed_weights_middle(self, t):
        b = t.block
        t.c_wide.wait(t.gfr)
        total = t.ff.chips_of_copy(t.gff, t.ff.r)[...]
        for slot in range(3):
            total = total + t.gfr[slot].astype(F32)
        t.gf2[...] = total.astype(BF16)
        t.gf3[...] = total
        t.c_line = Group(self)
        for mask in t.ff.group_peers:
            t.c_line.send(t.gf2.at[t.ff.group_of(self.at_peer(mask))], t.gf3r.at[t.ff.g], mask)
        t.c_bias.wait(t.dbr)
        bias = t.dbs[0:1, :]
        for slot in range(3):
            bias = bias + t.dbr[slot, 0:1, :]
        mine = jnp.zeros((1, b), F32)
        for copy in range(4):
            mine = jnp.where(t.ff.r == copy, bias[:, b * copy : b * (copy + 1)], mine)
        t.d_fcb[...] = mine

    def feed_weights_end(self, t):
        t.c_line.wait(t.gf2.at[0:3])
        own = t.gf3[t.ff.g]
        for group in range(4):
            t.gf3[group] = jnp.where(t.ff.g == group, own, t.gf3r[group].astype(F32))
        start = pl.multiple_of((1 - self.core) * t.rows, 8)
        t.c_fc = Group(self)
        t.c_fc.send(t.gf3.at[:, pl.ds(start, t.rows)], t.gf4, 1)

    def attend_back(self, t):
        vec = t.vecs
        total = self.line_total(t, t.dcf, t.dcr)
        g2 = t.g2[t.ff.spot]
        t.g1 = g2 + small_norm_back(total, t.xh2, t.inv2, vec[5:6, :])
        branch = t.g1.astype(BF16)
        t.do = dot_nt(branch, t.w2[1]).astype(BF16)
        t.sums.update(
            dbv=col_sum(t.do.astype(F32)),
            dbo=col_sum(branch.astype(F32)),
            dg2=col_sum(total * t.xh2),
            db2=col_sum(total),
            dbp=col_sum(g2.astype(BF16).astype(F32)),
        )
        t.c_w = self.share_group(t.at, t.wg, branch)

    def attend_back_end(self, t):
        r, w1, a, lh, rh = t.queries, t.w1, t.a, t.lh, t.rh
        dvt = dot_nt(expand_heads(t.do), t.w2[0]).astype(BF16)
        rh[r : 2 * r, :] = dvt
        d_probs = dot_nt(dvt, a[...])
        probs = t.p32[...]
        weighted = probs * d_probs
        d_scores = (weighted - probs * jnp.sum(weighted, -1, keepdims=True)).astype(BF16)
        d_scores = (d_scores.astype(F32) * 0.125).astype(BF16)
        lh[0:r, :] = d_scores
        moved = dot(d_scores, a[...])
        self.by_rows(t, moved, t.in2t)
        t.c_in2 = self.to_group(t.at, t.in2t, t.in2r)
        d_query = join_heads(dot(moved.astype(BF16), w1[1])).astype(BF16)
        t.c_dq = self.share_group(t.at, t.dqg, d_query)
        t.sums.update(dbq=col_sum(d_query.astype(F32)))
        high, low = split_two(dot_nt(d_query, w1[0]))
        rh[2 * r : 2 * r + PAD, :] = high
        rh[2 * r + PAD : 2 * r + 2 * PAD, :] = low

    def proj_out(self, t):
        return pltpu.make_async_copy(t.prj, t.d_proj, self.osem.at[2 if t is self.ti else 3])

    def copy_out(self, t):
        return pltpu.make_async_copy(t.dxs, t.d_x, self.osem.at[0 if t is self.ti else 1])

    def input_gradient(self, t):
        r, d = t.queries, t.width
        lh, da, gp, xh, inv, vec, out = t.lh, t.da, t.gp, t.xh, t.inv, t.vecs, t.dxs
        da[...] = dot_tn(lh[...], t.rh[...])
        image = t is self.ti
        if not image:
            high, low = split_two(t.g1)
            gp[...] = dot_tn(lh[2 * r : 2 * r + 2 * PAD, :], jnp.concatenate([high, low], 0))
        step = STEP_ROWS
        full = t.real_tokens // step

        def one(rows, carry):
            z, normed = da[rows, :], xh[rows, :]
            inner = small_norm_back(z, normed, inv[rows, 0:1], vec[0:1, :])
            return inner if image else inner + gp[rows, :], (
                carry[0] + jnp.sum((z * normed).reshape(step // 8, 8, d), 0),
                carry[1] + jnp.sum(z.reshape(step // 8, 8, d), 0),
            )

        def body(index, carry):
            rows = pl.ds(pl.multiple_of(index * step, step), step)
            out[rows, :], carry = one(rows, carry)
            return carry

        zero = jnp.zeros((8, d), F32)
        carry = lax.fori_loop(0, full, body, (zero, zero))
        start, rest = full * step, t.real_tokens - full * step
        if rest:
            last, carry = one(slice(start, start + step), carry)
            out[start : start + rest, :] = last[:rest]
        if image:
            for at in range(self.images):
                place = slice(at * TOK_I, at * TOK_I + 1)
                out[place, :] = out[place, :] + t.g1[at : at + 1]
        self.copy_out(t).start()
        s = t.sums
        rows = [col_sum(carry[0]), col_sum(carry[1])]
        rows += [s.pop(name) for name in list(dict(dbq=0, dbv=0, dbo=0, dg2=0, db2=0, dbp=0))]
        start = 0 if t is self.ti else self.ti.width
        self.va[:, start : start + d] = jnp.concatenate(rows, 0)

    def vector_sum_begin(self):
        self.c_vec = Group(self)
        self.c_vec.send(self.va, self.var, 1)

    def vector_sum_spread(self):
        self.c_vec.wait(self.var)
        total = self.va[...] + self.var[...]
        for chip in range(16):
            pieces, at = [], 0
            for t in (self.ti, self.tt):
                cols = t.chip_rows
                start = at + chip * cols
                pieces += [total[:, start : start + cols], jnp.zeros((8, 64 - cols), F32)]
                at += t.width
            self.vs[chip] = jnp.concatenate(pieces, 1)
        self.c_vec = Group(self)
        for mask in CHIP_PEERS:
            self.c_vec.send(self.vs.at[self.at_peer(mask) // 2], self.vl.at[self.chip], mask)
        self.vl[self.chip] = self.vs[self.chip]

    def vector_sum_done(self):
        self.c_vec.wait(self.vl.at[0:15])
        total = jnp.sum(self.vl[...], 0)
        for t, lane in ((self.ti, 0), (self.tt, 64)):
            rows = t.rows
            halves = [total[:, lane + rows * core : lane + rows * (core + 1)] for core in range(2)]
            t.d_vec[...] = jnp.where(self.core == 0, halves[0], halves[1])

    def turn_members(self, t, first, second, buffer):
        d = t.width
        rows = [part[...].reshape(4 * PAD, d) for part in (first, second)]
        buffer[...] = jnp.concatenate(rows, 0).astype(F32).T.astype(BF16).reshape(buffer.shape)
        return t.at.chips_of_group(buffer, t.at.g)[...].reshape(4 * t.chip_rows, 8 * PAD)

    def round_one(self, t):
        t.c_in1.wait(t.in1r.at[0:3])
        t.c_w.wait(t.wg.at[0:3])
        t.c_o.wait(t.og.at[0:3])
        t.c_a.wait(t.ag.at[0:3])
        d, cr = t.width, t.chip_rows
        members = 4 * PAD
        branch = t.wg[...].reshape(members, d)
        self.times_heads(t, t.in1r, dot_nt(branch, t.w2[1]).astype(BF16), t.r1f, 0)
        t.in3 = self.turn_members(t, t.og, t.ag, t.in3t)
        out = dot(t.in3, jnp.concatenate([branch, jnp.zeros_like(branch)], 0))
        t.r1f[:, :, d : 2 * d] = out.reshape(4, cr, d)
        if t.extra:
            t.c_p.wait(t.pg.at[0:3])
            operand = self.turn_members(t, t.pg, t.pg, t.in4t)
            units = self.drb[pl.ds(self.core * 4, 4)].reshape(members, 2 * t.extra)
            proj = dot(operand, jnp.concatenate([units, jnp.zeros_like(units)], 0))
            t.r1f[:, :, 2 * d :] = proj.reshape(4, cr, 2 * t.extra)
        t.c_r1 = self.round_pair(t, t.r1f, t.r1p)

    def round_two(self, t):
        t.c_in2.wait(t.in2r.at[0:3])
        d, cr = t.width, t.chip_rows
        members = 4 * PAD
        query = dot(t.ag[...].reshape(members, d), t.w1[0]) + t.vecs[2:3, :]
        self.times_heads(t, t.in2r, query.astype(BF16), t.r2f, d)
        t.c_dq.wait(t.dqg.at[0:3])
        d_query = t.dqg[...].reshape(members, d)
        d_query = jnp.concatenate([jnp.zeros_like(d_query), d_query], 0)
        t.r2f[:, :, 0:d] = dot(t.in3, d_query).reshape(4, cr, d)
        t.c_r2 = self.round_pair(t, t.r2f, t.r2p)

    def round_pair(self, t, grad, landing):
        start = pl.multiple_of((1 - self.core) * t.rows, 8)
        group = Group(self)
        group.send(grad.at[:, pl.ds(start, t.rows)], landing, 1)
        return group

    def round_spread(self, t, which):
        group, grad, came, total, packed, landing = (
            (t.c_r1, t.r1f, t.r1p, t.r1s, t.r1b, t.r1r),
            (t.c_r2, t.r2f, t.r2p, t.r2s, t.r2b, t.r2r),
        )[which]
        group.wait(came)
        start = pl.multiple_of(self.core * t.rows, 8)
        values = grad[:, pl.ds(start, t.rows), :] + came[...]
        total[...] = values
        cols = values.shape[2] // t.fold
        pieces = [values[:, :, cols * part : cols * (part + 1)] for part in range(t.fold)]
        packed[...] = jnp.concatenate(pieces, 1).astype(BF16)
        group = self.to_copies(t.at, packed, landing)
        if which:
            t.c_r2 = group
        else:
            t.c_r1 = group

    def round_end(self, t, which):
        group, total, landing = ((t.c_r1, t.r1s, t.r1r), (t.c_r2, t.r2s, t.r2r))[which]
        group.wait(landing)
        arrived = landing[0].astype(F32) + landing[1].astype(F32) + landing[2].astype(F32)
        pieces = [arrived[t.rows * part : t.rows * (part + 1)] for part in range(t.fold)]
        values = total[t.at.r] + jnp.concatenate(pieces, 1)
        d = t.width
        if which:
            t.d_qkv[:, 0 : 2 * d] = values
        else:
            t.d_qkv[:, 2 * d : 3 * d] = values[:, 0:d]
            t.d_out[...] = values[:, d : 2 * d]
            if t.extra:
                self.dmap[...] = values[:, 2 * d :]

    def feed_weights_done(self, t):
        rows, b = t.rows, t.block
        start = pl.multiple_of(self.core * rows, 8)
        t.c_fc.wait(t.gf4)
        for group in range(4):
            own, got = t.gf3[group, pl.ds(start, rows), :], t.gf4[group]
            for half in range(2):
                values = jnp.where(self.core == half, own, got)
                for copy in range(4):
                    device = t.ff.device_of(group, copy, half)
                    t.d_fc[:, b * device : b * (device + 1)] = values[:, b * copy : b * (copy + 1)]


def set_all(target, names, refs):
    for name, ref in zip(names, refs, strict=True):
        setattr(target, name, ref)


def hand_over(results):
    count = len(results)
    cuts = []
    for index, value in enumerate(results):
        rows = value.shape[0]
        step = 120 if rows > 120 and rows % 120 == 0 else rows
        cuts += [(index, start, step) for start in range(0, rows, step)]

    def kernel(*refs):
        came, went = refs[3 * count], refs[3 * count + 1]
        reads, writes = [], []
        for at, (index, start, rows) in enumerate(cuts):
            src, dst, mid = (refs[index + part * count] for part in range(3))
            if rows != src.shape[0]:
                src, dst, mid = (ref.at[start : start + rows] for ref in (src, dst, mid))
            reads.append(pltpu.make_async_copy(src, mid, came.at[at]))
            writes.append(pltpu.make_async_copy(mid, dst, went.at[at]))
        for read in reads:
            read.start()
        for read, write in zip(reads, writes, strict=True):
            read.wait()
            write.start()
        for write in writes:
            write.wait()

    sems = pltpu.SemaphoreType.DMA((len(cuts),))
    return pl.pallas_call(
        kernel,
        out_shape=tuple(jax.ShapeDtypeStruct(value.shape, value.dtype) for value in results),
        in_specs=[pl.BlockSpec(memory_space=pl.ANY)] * count,
        out_specs=tuple([pl.BlockSpec(memory_space=pl.ANY)] * count),
        scratch_shapes=[pltpu.VMEM(value.shape, value.dtype) for value in results] + [sems, sems],
        compiler_params=pltpu.CompilerParams(vmem_limit_bytes=60 * 2**20),
        name="hand_over",
    )(*results)


def local_fused(
    picture_patch_inputs,
    caption_packed_inputs,
    picture_attend_entry_weight,
    picture_attend_exit_weight,
    picture_widening_weight,
    picture_narrowing_weight,
    picture_affine_entries,
    picture_widening_offset,
    caption_attend_entry_weight,
    caption_attend_exit_weight,
    caption_widening_weight,
    caption_narrowing_weight,
    caption_affine_entries,
    caption_widening_offset,
    picture_feature_mapping,
    sharpness_exponent,
    caption_token_counts,
    matching_picture_index,
):
    n_img, d_img = picture_patch_inputs.shape
    n_txt, d_txt = caption_packed_inputs.shape
    images = n_img // TOK_I
    ti = Tower(
        True,
        d_img,
        n_img,
        picture_attend_entry_weight.shape[1],
        picture_widening_offset.shape[1],
        picture_feature_mapping.shape[1] // 2,
    )
    tt = Tower(
        False, d_txt, n_txt, caption_attend_entry_weight.shape[1], caption_widening_offset.shape[1], 0
    )
    img_args = dict(
        x=picture_patch_inputs,
        qkv=picture_attend_entry_weight[0],
        out=picture_attend_exit_weight[0],
        fc=picture_widening_weight[0],
        proj=picture_narrowing_weight[0],
        vec=picture_affine_entries[0],
        fcb=picture_widening_offset,
    )
    txt_args = dict(
        x=caption_packed_inputs,
        qkv=caption_attend_entry_weight[0],
        out=caption_attend_exit_weight[0],
        fc=caption_widening_weight[0],
        proj=caption_narrowing_weight[0],
        vec=caption_affine_entries[0],
        fcb=caption_widening_offset,
    )
    more_args = dict(
        map=picture_feature_mapping,
        sharp=sharpness_exponent.reshape(1),
        counts=caption_token_counts,
        match=matching_picture_index,
    )

    def out(*shape):
        return jax.ShapeDtypeStruct(shape, F32)

    def tower_outs(t):
        return dict(
            d_x=out(t.real_tokens, t.width),
            d_qkv=out(t.rows, 3 * t.width),
            d_out=out(t.rows, t.width),
            d_fc=out(t.rows, 32 * t.block),
            d_proj=out(t.block, t.width),
            d_vec=out(8, t.rows),
            d_fcb=out(1, t.block),
        )

    more_outs = dict(loss=out(1, 1), dls=out(1, 1), dmap=out(ti.rows, 2 * ti.extra))
    in_vmem, in_smem = pl.BlockSpec(memory_space=pltpu.VMEM), pl.BlockSpec(memory_space=pltpu.SMEM)
    anywhere = pl.BlockSpec(memory_space=pl.ANY)
    parts = [
        (ti, img_args, [in_vmem] * 7),
        (tt, txt_args, [in_vmem] * 7),
        (None, more_args, [in_vmem, in_smem, in_smem, in_smem]),
        (ti, tower_outs(ti), [anywhere] + [in_vmem] * 3 + [anywhere] + [in_vmem] * 2),
        (tt, tower_outs(tt), [anywhere] + [in_vmem] * 3 + [anywhere] + [in_vmem] * 2),
        (None, more_outs, [in_vmem] * 3),
        (ti, ti.scratch(), None),
        (tt, tt.scratch(), None),
        (None, shared_scratch(ti, tt), None),
        (
            None,
            dict(
                ssem=pltpu.SemaphoreType.DMA((N_SEMS,)),
                rsem=pltpu.SemaphoreType.DMA((N_SEMS,)),
                osem=pltpu.SemaphoreType.DMA((4,)),
            ),
            None,
        ),
    ]

    def kernel(*refs):
        step = Step(ti, tt, images)
        at = 0
        for owner, values, _ in parts:
            set_all(step if owner is None else owner, values, refs[at : at + len(values)])
            at += len(values)
        step.run()

    def joined(chosen, field):
        return [item for part in chosen for item in (part[field] if field == 2 else part[field].values())]

    results = pl.pallas_call(
        kernel,
        out_shape=tuple(joined(parts[3:6], 1)),
        in_specs=joined(parts[0:3], 2),
        out_specs=tuple(joined(parts[3:6], 2)),
        scratch_shapes=joined(parts[6:], 1),
        compiler_params=pltpu.CompilerParams(
            collective_id=0, has_side_effects=True, vmem_limit_bytes=60 * 2**20
        ),
        name="contrastive_step",
    )(*joined(parts[0:3], 1))
    results = hand_over(results)
    img, txt, (loss, d_scale, d_map) = results[0:7], results[7:14], results[14:17]
    return (
        loss.reshape(()),
        d_scale.reshape(()),
        img[0],
        txt[0],
        img[1][None],
        img[2][None],
        img[3][None],
        img[4][None],
        img[5][None],
        img[6],
        txt[1][None],
        txt[2][None],
        txt[3][None],
        txt[4][None],
        txt[5][None],
        txt[6],
        d_map,
    )


def solution(mesh):
    placed = (
        P("dp", None),
        P("dp", None),
        P(None, "dp", None),
        P(None, "dp", None),
        P(None, "dp", None),
        P(None, "dp", None),
        P(None, None, "dp"),
        P(None, "dp"),
        P(None, "dp", None),
        P(None, "dp", None),
        P(None, "dp", None),
        P(None, "dp", None),
        P(None, None, "dp"),
        P(None, "dp"),
        P("dp", None),
        P(),
        P("dp", None),
        P("dp"),
    )
    return jax.shard_map(
        local_fused if fits(mesh) else local_plain,
        mesh=mesh,
        in_specs=placed,
        out_specs=(
            P(),
            P(),
            P("dp", None),
            P("dp", None),
            P(None, "dp", None),
            P(None, "dp", None),
            P(None, "dp", None),
            P(None, "dp", None),
            P(None, None, "dp"),
            P(None, "dp"),
            P(None, "dp", None),
            P(None, "dp", None),
            P(None, "dp", None),
            P(None, "dp", None),
            P(None, None, "dp"),
            P(None, "dp"),
            P("dp", None),
        ),
        check_vma=False,
    )
```
